512 devices in a mesh: img: 32 (over x, z_hi, core), ref: 16 (over y, z_lo).
Axes of the slice: x: 4, y: 4, z: 16 (z_hi: 4, z_lo: 4; z = z_hi * 4 + z_lo), core: 2. Of those that a mesh axis runs over, the one named last changes fastest.
Arguments:
- images: bfloat16 [2048, 2, 4224], P('img', None, 'ref'), may hold values from -40 to 40
- projections: bfloat16 [768, 2, 4224], P('ref'), may hold values from -3 to 3
- contrast_curve: float32 [16, 4224], replicated, may hold values from 0.2 to 1
- noise_weight: float32 [4224], replicated, may hold values from 0.5 to 2
- defocus_group: int32 [2048], P('img'), may hold values from 0 to 15
- shifts: int32 [9, 2], replicated, may hold values from -3 to 3, as said below
- orient_index: int32 [768], P('ref'), may hold values from 0 to 255
- orient_prior: float32 [256], replicated, may hold values from -1.4 to 1.4
Outputs:
- class_sums: float32 [768, 2, 4224], P('ref', None, 'img')
- contrast_weight: float32 [768, 4224], P('ref', 'img')
- evidence: float32 [2048], P('img')
The draws below stay inside these ranges and needn't reach their ends.
Inputs may be any that keep to these rules, and one draw needn't show every extreme that they name: `shifts`: shift 0 is (0, 0); shift 1 moves 3 pixels along x and shift 2 moves -3 pixels along x.
All inputs are finite; a program needn't handle non-finite values.
Results may differ from the reference program's by a relative error of at most 0.0044.
Values may be sent and summed in bfloat16 or wider, within the bound.
A program may use at most 64 MiB of HBM per device.

```python
import math
import jax
import jax.numpy as jnp
from jax import lax

NPIX = 4224
BOX = 128
NSHIFT = 9
NORIENT = 256
GROUPS = 16
IMAGES = 2048
PROJ = 768


def projection_base(key):
    spread = 4.0 / jnp.sqrt(jnp.float32(NPIX))
    return jnp.clip(jax.random.normal(key, (PROJ, 2, NPIX), jnp.float32), -6.0, 6.0) * spread


def draw_projections(key, part):
    shared = projection_base(key)
    return shared.astype(jnp.bfloat16)


def draw_images(key, part):
    key = jax.random.fold_in(key, 12)
    key_noise = jax.random.fold_in(key, 0)
    values = 0.25 * jnp.clip(jax.random.normal(key_noise, (IMAGES, 2, NPIX), jnp.float32), -6.0, 6.0)
    return jnp.clip(values, -40.0, 40.0).astype(jnp.bfloat16)


def draw_shifts(key, part):
    key = jax.random.fold_in(key, 13)
    raw_grid = jax.random.randint(key, (NSHIFT, 2), -3, 4)
    slot = lax.iota(jnp.int32, NSHIFT)[:, None]
    column = lax.iota(jnp.int32, 2)[None, :]
    grid = jnp.where((slot == 1) & (column == 0), 3, raw_grid)
    grid = jnp.where((slot == 2) & (column == 0), -3, grid)
    return jnp.where(slot == 0, 0, grid).astype(jnp.int32)


def place_ends(drawn, own_key, least, top_value):
    longest = drawn.shape.index(max(drawn.shape))
    spots = []
    for shift in (0, 1):
        where = [jax.random.randint(jax.random.fold_in(own_key, axis), (), 0, length) for axis, length in enumerate(drawn.shape)]
        where[longest] = (where[longest] + shift) % drawn.shape[longest]
        spots.append(tuple(where))
    return drawn.at[spots[0]].set(least).at[spots[1]].set(top_value)


def noise(own_key, extent, width, most, kind=jnp.bfloat16):
    return jnp.clip(width * jax.random.normal(own_key, extent, jnp.float32), -most, most).astype(kind)


def setup_inputs(seed: int = 0) -> dict:
    splits = jax.random.split(jax.random.key(seed), 9)
    return {
        "images": draw_images(jax.random.fold_in(splits[8], 71), 0),
        "projections": draw_projections(jax.random.fold_in(splits[8], 71), 0),
        "contrast_curve": jnp.clip(jax.random.uniform(splits[2], (GROUPS, NPIX), jnp.float32, 0.2, 1.0), 0.2, 1.0),
        "noise_weight": jnp.clip(jnp.exp(jax.random.uniform(splits[3], (NPIX,), jnp.float32, math.log(0.5), math.log(2.0))), 0.5, 2.0),
        "defocus_group": place_ends(jax.random.randint(splits[4], (IMAGES,), 0, GROUPS), jax.random.fold_in(splits[4], 1), 0, GROUPS - 1).astype(jnp.int32),
        "shifts": draw_shifts(jax.random.fold_in(splits[8], 71), 0),
        "orient_index": place_ends(jax.random.randint(splits[6], (PROJ,), 0, NORIENT), jax.random.fold_in(splits[6], 1), 0, NORIENT - 1).astype(jnp.int32),
        "orient_prior": noise(splits[7], (NORIENT,), 0.35, 1.4, jnp.float32),
    }


def phase_tables(shifts, start_pixel, pixel_count):
    pixel_index = start_pixel + lax.iota(jnp.int32, pixel_count)
    half_box = BOX // 2
    freq_x = (pixel_index % half_box).astype(jnp.float32)
    freq_y = (pixel_index // half_box - NPIX // BOX).astype(jnp.float32)
    move_x = shifts[:, 0].astype(jnp.float32)[:, None]
    move_y = shifts[:, 1].astype(jnp.float32)[:, None]
    phase_angle = (2.0 * math.pi / BOX) * (move_x * freq_x[None, :] + move_y * freq_y[None, :])
    return jnp.cos(phase_angle), jnp.sin(phase_angle)


def shifted(weighted, cosine_row, sine_row):
    real_part = weighted[:, 0, :].astype(jnp.float32)
    imag_part = weighted[:, 1, :].astype(jnp.float32)
    return jnp.stack([real_part * cosine_row + imag_part * sine_row, imag_part * cosine_row - real_part * sine_row], axis=1).astype(jnp.bfloat16)


def reference(images, projections, contrast_curve, noise_weight, defocus_group, shifts, orient_index, orient_prior):
    gain_rows = contrast_curve[defocus_group] * noise_weight[None, :]
    weighted = (images.astype(jnp.float32) * gain_rows[:, None, :]).astype(jnp.bfloat16)
    cosine_table, sine_table = phase_tables(shifts, 0, NPIX)
    flat_proj = projections.reshape(PROJ, 2 * NPIX)
    proj_wide = projections.astype(jnp.float32)
    proj_power = proj_wide[:, 0, :] * proj_wide[:, 0, :] + proj_wide[:, 1, :] * proj_wide[:, 1, :]
    power_gain = contrast_curve * contrast_curve * noise_weight[None, :]
    group_norm = jnp.einsum("gk,jk->gj", 0.5 * power_gain, proj_power, precision=lax.Precision.HIGHEST)
    orient_term = orient_prior[orient_index]
    score_base = orient_term[None, :] - group_norm[defocus_group]
    score_list = []
    for shift_slot in range(NSHIFT):
        shift_layer = shifted(weighted, cosine_table[shift_slot], sine_table[shift_slot]).reshape(IMAGES, 2 * NPIX)
        score_list.append(jnp.dot(shift_layer, flat_proj.T, preferred_element_type=jnp.float32) + score_base)
    scores = jnp.stack(score_list)
    highest = jnp.max(scores, axis=(0, 2))
    totals = jnp.sum(jnp.exp(scores - highest[None, :, None]), axis=(0, 2))
    evidence = highest + jnp.log(totals)
    weights = jnp.exp(scores - evidence[None, :, None]).astype(jnp.bfloat16)
    class_sums = jnp.zeros((PROJ, 2 * NPIX), jnp.float32)
    for shift_slot in range(NSHIFT):
        shift_layer = shifted(weighted, cosine_table[shift_slot], sine_table[shift_slot]).reshape(IMAGES, 2 * NPIX)
        class_sums = class_sums + jnp.dot(weights[shift_slot].T, shift_layer, preferred_element_type=jnp.float32)
    members = (defocus_group[:, None] == lax.iota(jnp.int32, GROUPS)[None, :]).astype(jnp.float32)
    summed = jnp.sum(weights.astype(jnp.float32), axis=0)
    per_group = jnp.einsum("ij,ig->jg", summed, members, precision=lax.Precision.HIGHEST)
    contrast_weight = jnp.dot(per_group, power_gain, precision=lax.Precision.HIGHEST)
    return class_sums.reshape(PROJ, 2, NPIX), contrast_weight, evidence
```

```python
import math

import jax
import jax.numpy as jnp
from jax import lax
from jax.experimental import pallas as pl
from jax.experimental.pallas import tpu as pltpu
from jax.sharding import PartitionSpec as P

MESH = pl.DeviceIdType.MESH
F32 = jnp.float32
BF16 = jnp.bfloat16
HIGHEST = lax.Precision.HIGHEST
NT = (((1,), (1,)), ((), ()))
TN = (((0,), (0,)), ((), ()))

NPIX = 4224
BOX = 128
NSHIFT = 9
NIMG = 64
NPROJ = 48
GROUPS = 16
ROWS = NSHIFT * NIMG
SHARD = 272
PIECE = 48
MSG = 400
HALF = 208
FIRST = 112


def sincos(steps):
    quadrant = lax.shift_right_arithmetic(steps + 16, 5)
    rest = (steps - quadrant * 32).astype(F32) * (2.0 * math.pi / BOX)
    sq = rest * rest
    sin_part = rest * (
        1.0 + sq * (-1.0 / 6 + sq * (1.0 / 120 + sq * (-1.0 / 5040 + sq * (1.0 / 362880))))
    )
    cos_part = 1.0 + sq * (
        -0.5 + sq * (1.0 / 24 + sq * (-1.0 / 720 + sq * (1.0 / 40320 - sq * (1.0 / 3628800))))
    )
    odd = (quadrant & 1) == 1
    flip_sin = (quadrant & 2) == 2
    flip_cos = ((quadrant + 1) & 2) == 2
    sine = jnp.where(odd, cos_part, sin_part)
    cosine = jnp.where(odd, sin_part, cos_part)
    return jnp.where(flip_cos, -cosine, cosine), jnp.where(flip_sin, -sine, sine)


def body(
    img_ref,
    proj_ref,
    curve_ref,
    noise_ref,
    group_ref,
    shift_ref,
    orient_ref,
    prior_ref,
    cls_ref,
    con_ref,
    ev_ref,
    xbuf,
    pmain,
    prest,
    ctab,
    stab,
    crest,
    srest,
    smain,
    shrest,
    score,
    wts,
    stat,
    core_out,
    core_in,
    rest_out,
    rest_in,
    x_out,
    x_near_a,
    x_near_b,
    x_in,
    held,
    z_out,
    z_relay,
    z_in,
    z_core,
    ag_u_s,
    ag_d_s,
    ag_z_r,
    ag_y_s,
    ag_y_r,
    ag_f_s,
    ag_f_r,
    st_s,
    st_r,
    co_s,
    co_r,
    xs_s,
    xs_r,
    zs_s,
    zs_r,
):
    img = lax.axis_index("img")
    ref = lax.axis_index("ref")
    x = lax.div(img, 8)
    h = lax.rem(lax.div(img, 2), 4)
    d = lax.rem(img, 2)
    o = 1 - d
    y = lax.div(ref, 4)
    l = lax.rem(ref, 4)

    def ring(v):
        return lax.rem(v + 4, 4)

    def dev(img_at=img, ref_at=ref):
        return {"img": img_at, "ref": ref_at}

    def at_img(xx, hh, dd):
        return dev(img_at=(xx * 4 + hh) * 2 + dd)

    def copy(src, dst, send, recv, to):
        return pltpu.make_async_remote_copy(
            src_ref=src, dst_ref=dst, send_sem=send, recv_sem=recv, device_id=to, device_id_type=MESH
        )

    barrier = pltpu.get_barrier_semaphore()
    peers = [dev(ref_at=lax.rem(ref + k, 16)) for k in range(1, 16)]
    peers += [at_img(x, h, o), at_img(ring(x + 1), h, d), at_img(ring(x - 1), h, d)]
    for hh in (ring(h + 1), ring(h - 1)):
        peers += [at_img(x, hh, d), at_img(x, hh, o)]
    for peer in peers:
        pl.semaphore_signal(barrier, inc=1, device_id=peer, device_id_type=MESH)

    lane = lax.broadcasted_iota(jnp.int32, (1, 128), 1)

    def noise_row(tile, count):
        return jnp.concatenate([noise_ref[pl.ds(tile + t, 1), :] for t in range(count)], axis=1)


    group_row = group_ref[...].astype(F32)
    group_row = jnp.concatenate([group_row, group_row], axis=1)
    group_col = jnp.transpose(jnp.broadcast_to(group_row, (128, 128)))[:NIMG, :]
    start = pl.multiple_of(ref * 256, 128)
    turn = lax.rem(384 - 8 * ref, 384)
    curve_here = pltpu.roll(curve_ref[:, pl.ds(start, 384)], turn, 1)
    noise_here = pltpu.roll(jnp.broadcast_to(noise_row(2 * ref, 3), (8, 384)), turn, 1)[:1, :]
    parts = []
    for tile in range(3):
        span = slice(tile * 128, tile * 128 + 128)
        gain = jnp.zeros((NIMG, 128), F32)
        for g in range(GROUPS):
            gain = jnp.where(group_col == float(g), curve_here[g : g + 1, span], gain)
        gain = gain * noise_here[:, span]
        parts.append(img_ref[:, span].astype(F32) * jnp.concatenate([gain, gain], axis=0))
    second = pltpu.roll(jnp.concatenate(parts[1:], axis=1), 252, 1)[:, :128]
    rest = jnp.transpose(jnp.where(lane < 4, parts[1], parts[2]))[:16, :]
    row16 = lax.broadcasted_iota(jnp.int32, (16, 128), 0)
    rest = jnp.where(row16 < 8, rest, 0.0)
    xbuf[ref, 0:128, :] = parts[0].astype(BF16)
    xbuf[ref, 128:256, :] = second.astype(BF16)
    xbuf[ref, 256:272, :] = rest.astype(BF16)

    pl.semaphore_wait(barrier, len(peers))

    col_1 = jnp.where(l == 0, 1, l - 1)
    col_2 = jnp.where(l < 2, 2, jnp.where(l == 2, 3, 1))
    col_3 = jnp.where(l < 2, 3, 0)
    columns = [l, col_1, col_2, col_3]

    def shard(yy, e):
        return yy * 4 + columns[e]

    def z_copy_of(col, up):
        block = xbuf.at[y * 4 + col]
        to = dev(ref_at=y * 4 + lax.rem(l + (1 if up else 3), 4))
        return copy(block, block, (ag_u_s if up else ag_d_s).at[col], ag_z_r.at[col], to)

    def forward(col, start):
        @pl.when((col <= l) & (l < 3))
        def _():
            c = z_copy_of(col, True)
            c.start() if start else c.wait_send()

        @pl.when((col >= l) & (l > 0))
        def _():
            c = z_copy_of(col, False)
            c.start() if start else c.wait_send()

    y_up, y_down, y_far = ring(y + 1), ring(y - 1), ring(y + 2)

    def y_copy(way, e, src_y):
        to = dev(ref_at=(y_up if way == 0 else y_down) * 4 + l)
        block = xbuf.at[shard(src_y, e)]
        return copy(block, block, ag_y_s.at[way, e], ag_y_r.at[way, e], to)

    def f_copy(way, e, src_y):
        to = dev(ref_at=(y_up if way == 0 else y_down) * 4 + l)
        rows = pl.ds(0, 144) if way == 0 else pl.ds(144, 128)
        block = xbuf.at[shard(src_y, e), rows]
        return copy(block, block, ag_f_s.at[way, e], ag_f_r.at[way, e], to)

    y_copy(0, 0, y).start()
    y_copy(1, 0, y).start()
    forward(l, True)

    def take_z(e):
        z_copy_of(columns[e], True).wait_recv()
        forward(columns[e], True)
        y_copy(0, e, y).start()
        y_copy(1, e, y).start()

    def take_y(e):
        y_copy(0, e, y_down).wait_recv()
        f_copy(0, e, y_down).start()
        y_copy(1, e, y_up).wait_recv()
        f_copy(1, e, y_up).start()

    def take_far(e):
        f_copy(0, e, y_far).wait_recv()
        f_copy(1, e, y_far).wait_recv()

    def table(pixel, width):
        srow = lax.broadcasted_iota(jnp.int32, (8, width), 0) + 1
        move_x = jnp.zeros((8, width), jnp.int32)
        move_y = jnp.zeros((8, width), jnp.int32)
        for s in range(1, NSHIFT):
            move_x = jnp.where(srow == s, shift_ref[0, s], move_x)
            move_y = jnp.where(srow == s, shift_ref[1, s], move_y)
        freq_x = pixel & (BOX // 2 - 1)
        freq_y = lax.shift_right_logical(pixel, 6) - NPIX // BOX
        return sincos((move_x * freq_x + move_y * freq_y) & (BOX - 1))

    def table_step(b, carry):
        at = lax.broadcasted_iota(jnp.int32, (8, 256), 1)
        pixel = 264 * b + at + jnp.where(at >= 128, 4, 0)
        cosine, sine = table(pixel, 256)
        ctab[b] = cosine
        stab[b] = sine
        return carry

    lax.fori_loop(0, 16, table_step, 0)
    at = lax.broadcasted_iota(jnp.int32, (8, 128), 1)
    cosine, sine = table(132 * lax.shift_right_logical(at, 2) + 128 + (at & 3), 128)
    crest[...] = cosine
    srest[...] = sine

    def proj_step(b, carry):
        out = []
        for c in range(2):
            kept = carry[c]
            for u in range(2):
                n = 2 * b + u
                window = proj_ref[c, :, pl.ds(pl.multiple_of(n * 128, 128), 256)].astype(F32)
                turned = pltpu.roll(window, lax.rem(256 - 4 * n, 256), 1)
                pmain[b, c, :, u * 128 : u * 128 + 128] = turned[:, :128].astype(BF16)
                kept = jnp.where(lax.shift_right_logical(lane, 2) == n, window[:, 128:], kept)
            out.append(kept)
        return tuple(out)

    zero_rest = jnp.zeros((NPROJ, 128), F32)
    rests = lax.fori_loop(0, 16, proj_step, (zero_rest, zero_rest))
    for c in range(2):
        prest[c] = rests[c].astype(BF16)

    take_z(1)
    take_y(0)

    def norm_step(t, total):
        span = pl.ds(pl.multiple_of(t * 384, 128), 384)
        re = proj_ref[0, :, span].astype(F32)
        im = proj_ref[1, :, span].astype(F32)
        curve = curve_ref[:, span]
        gain = 0.5 * (curve * curve * noise_row(3 * t, 3))
        power = re * re + im * im
        return total + lax.dot_general(
            two_parts(power), two_parts(gain), NT, preferred_element_type=F32
        )

    def two_parts(value):
        high = value.astype(BF16)
        return jnp.concatenate([high, (value - high.astype(F32)).astype(BF16)], axis=0)

    norm = lax.fori_loop(0, 11, norm_step, jnp.zeros((2 * NPROJ, 2 * GROUPS), F32))
    norm = norm[:NPROJ] + norm[NPROJ:]
    norm = norm[:, :GROUPS] + norm[:, GROUPS:]
    grow = lax.broadcasted_iota(jnp.int32, (GROUPS, 128), 0)
    members = (group_row == grow.astype(F32)).astype(F32)
    penalty = jnp.dot(norm, members, precision=HIGHEST, preferred_element_type=F32)
    orient_row = jnp.concatenate([orient_ref[...].astype(F32), jnp.zeros((1, 80), F32)], axis=1)
    orient_col = jnp.transpose(jnp.broadcast_to(orient_row, (128, 128)))[:NPROJ, :]
    prior = jnp.zeros((NPROJ, 1), F32)
    for half in range(2):
        hit = orient_col == (lane + half * 128).astype(F32)
        prior += jnp.sum(
            jnp.where(hit, prior_ref[half : half + 1, :], 0.0), axis=1, keepdims=True
        )
    base = prior - penalty

    score[...] = jnp.zeros_like(score)
    take_z(2)
    take_y(1)

    def process(b):
        for t in range(2):
            span = slice(t * 128, t * 128 + 128)
            re = xbuf[b, t * 128 : t * 128 + 64, :]
            im = xbuf[b, t * 128 + 64 : t * 128 + 128, :]
            smain[b, 0, 0:NIMG, span] = re
            smain[b, 1, 0:NIMG, span] = im
            re = re.astype(F32)
            im = im.astype(F32)
            for s in range(1, NSHIFT):
                rows = slice(s * NIMG, s * NIMG + NIMG)
                cosine = ctab[b, s - 1 : s, span]
                sine = stab[b, s - 1 : s, span]
                smain[b, 0, rows, span] = (re * cosine + im * sine).astype(BF16)
                smain[b, 1, rows, span] = (im * cosine - re * sine).astype(BF16)
        score[...] += lax.dot_general(
            smain[b, 0], pmain[b, 0], NT, preferred_element_type=F32
        ) + lax.dot_general(smain[b, 1], pmain[b, 1], NT, preferred_element_type=F32)

    def process_all(blocks):
        def step(t, carry):
            b = blocks[0]
            for k in range(1, len(blocks)):
                b = jnp.where(t == k, blocks[k], b)
            process(b)
            return carry

        lax.fori_loop(0, len(blocks), step, 0)

    process_all([shard(y, 0), shard(y, 1), shard(y_down, 0), shard(y_up, 0)])
    take_z(3)
    take_y(2)
    take_far(0)
    process_all([shard(y, 2), shard(y_down, 1), shard(y_up, 1), shard(y_far, 0)])
    take_y(3)
    take_far(1)
    process_all([shard(y, 3), shard(y_down, 2), shard(y_up, 2), shard(y_far, 1)])
    process_all([shard(y_down, 3), shard(y_up, 3)])
    take_far(2)
    process(shard(y_far, 2))
    take_far(3)
    process(shard(y_far, 3))

    rest_t = jnp.concatenate([xbuf[b, 256:272, :].astype(F32)[:8] for b in range(16)], axis=0)
    rest_x = jnp.transpose(rest_t)
    re, im = rest_x[:NIMG], rest_x[NIMG:]
    shrest[0, 0:NIMG, :] = re.astype(BF16)
    shrest[1, 0:NIMG, :] = im.astype(BF16)
    for s in range(1, NSHIFT):
        rows = slice(s * NIMG, s * NIMG + NIMG)
        cosine = crest[s - 1 : s, :]
        sine = srest[s - 1 : s, :]
        shrest[0, rows, :] = (re * cosine + im * sine).astype(BF16)
        shrest[1, rows, :] = (im * cosine - re * sine).astype(BF16)
    full = (
        score[...]
        + lax.dot_general(shrest[0], prest[0], NT, preferred_element_type=F32)
        + lax.dot_general(shrest[1], prest[1], NT, preferred_element_type=F32)
    )
    full = jnp.concatenate([full, jnp.zeros((ROWS, 128 - NPROJ), F32)], axis=1)

    tiles = []
    for t in range(5):
        if t < 4:
            tiles.append(jnp.transpose(full[t * 128 : t * 128 + 128])[:NPROJ] + base)
        else:
            last = jnp.concatenate([full[512:576], jnp.zeros((64, 128), F32)], axis=0)
            tiles.append(jnp.where(lane < 64, jnp.transpose(last)[:NPROJ] + base, -3e38))
    high = tiles[0]
    for t in range(1, 5):
        high = jnp.maximum(high, tiles[t])
    high = jnp.max(high, axis=0, keepdims=True)
    high = jnp.maximum(high, pltpu.roll(jnp.broadcast_to(high, (8, 128)), 64, 1)[:1])
    total = jnp.exp(tiles[0] - high)
    for t in range(1, 5):
        total += jnp.exp(tiles[t] - high)
    total = jnp.sum(total, axis=0, keepdims=True)
    total = total + pltpu.roll(jnp.broadcast_to(total, (8, 128)), 64, 1)[:1]
    row8 = lax.broadcasted_iota(jnp.int32, (8, 128), 0)
    stat[ref] = jnp.where(row8 == 0, high, total)
    st_copies = []
    for k in range(1, 16):
        st_copies.append(
            copy(stat.at[ref], stat.at[ref], st_s.at[k], st_r.at[k], dev(ref_at=lax.rem(ref + k, 16)))
        )
    for c in st_copies:
        c.start()
    for k in range(1, 16):
        src = lax.rem(ref + 16 - k, 16)
        copy(stat.at[src], stat.at[src], st_s.at[k], st_r.at[k], dev(ref_at=src)).wait_recv()
    highest = stat[0, 0:1, :]
    for b in range(1, 16):
        highest = jnp.maximum(highest, stat[b, 0:1, :])
    whole = jnp.zeros((1, 128), F32)
    for b in range(16):
        whole += stat[b, 1:2, :] * jnp.exp(stat[b, 0:1, :] - highest)
    evidence = highest + jnp.log(whole)
    ev_ref[...] = evidence
    for t in range(5):
        w = jnp.exp(tiles[t] - evidence).astype(BF16)
        if t < 4:
            wts[:, t * 128 : t * 128 + 128] = w
        else:
            wts[:, 512:576] = w[:, :64]
    members_all = jnp.concatenate([members.astype(BF16)] * 4 + [members[:, :64].astype(BF16)], axis=1)
    group_sum = lax.dot_general(members_all, wts[...], NT, preferred_element_type=F32)
    group_sum = jnp.concatenate([group_sum, jnp.zeros((GROUPS, 80), F32)], axis=1)

    other = at_img(x, h, o)
    rest_out[0:48, :] = jnp.dot(wts[...], shrest[o], preferred_element_type=F32).astype(BF16)
    rest_out[48:64, :] = group_sum.astype(BF16)
    rest_copy = copy(rest_out, rest_in, co_s.at[4], co_r.at[4], other)
    rest_copy.start()

    order = [ring(x + 2), ring(x + 1), ring(x + 3), x]
    runs = [ring(h + 2), ring(h + 1), ring(h + 3), h]

    def core_copy(i):
        return copy(core_out.at[i], core_in.at[i], co_s.at[i], co_r.at[i], other)

    def other_chunk(i):
        for u in range(4):
            got = jnp.dot(wts[...], smain[4 * order[i] + runs[u], o], preferred_element_type=F32)
            for v in range(2):
                r = PIECE * (2 * u + v)
                core_out[i, r : r + PIECE, :] = got[:, v * 128 : v * 128 + 128].astype(BF16)
        core_copy(i).start()

    other_chunk(0)
    other_chunk(1)

    rest_sum = jnp.dot(wts[...], shrest[d], preferred_element_type=F32)
    rest_copy.wait_recv()
    rest_sum = rest_sum + rest_in[0:48, :].astype(F32)
    group_sum = group_sum + rest_in[48:64, :].astype(F32)

    def left(value, by):
        return pltpu.roll(value, lax.rem(256 - by, 128), 1)

    group_half = left(group_sum, 32 + 24 * d)

    def packed(q):
        out = left(rest_sum[0:16], 32 * q)
        out = jnp.where(lane < 32, out, left(rest_sum[16:32], 32 * q - 32))
        out = jnp.where(lane < 64, out, left(rest_sum[32:48], 32 * q - 64))
        return jnp.where(lane < 96, out, group_half)

    def piece_row(k):
        return 16 + PIECE * k

    def own_chunk(i, store):
        q = order[i]
        core_copy(i).wait_recv()
        for u in range(4):
            got = jnp.dot(wts[...], smain[4 * q + runs[u], d], preferred_element_type=F32)
            for v in range(2):
                k = 2 * u + v
                r = PIECE * k
                store(k, got[:, v * 128 : v * 128 + 128] + core_in[i, r : r + PIECE, :].astype(F32))
        store(-1, packed(q))

    x_up, x_down = at_img(ring(x + 1), h, d), at_img(ring(x - 1), h, d)

    def rows_of(k):
        return slice(0, 16) if k < 0 else slice(piece_row(k), piece_row(k) + PIECE)

    def store_far(k, value):
        x_out[0, rows_of(k), :] = value.astype(BF16)

    own_chunk(0, store_far)
    near_a = copy(x_out.at[0, pl.ds(0, HALF)], x_near_a, xs_s.at[0], xs_r.at[0], x_up)
    near_b = copy(x_out.at[0, pl.ds(HALF, MSG - HALF)], x_near_b, xs_s.at[1], xs_r.at[1], x_down)
    near_a.start()
    near_b.start()

    def store_up(k, value):
        held[rows_of(k), :] = value

    def x_copy(way, part):
        rows = pl.ds(0, FIRST) if part == 0 else pl.ds(FIRST, MSG - FIRST)
        k = 2 + 2 * way + part
        to = x_up if way == 0 else x_down
        return copy(x_out.at[1 + way, rows], x_in.at[way, rows], xs_s.at[k], xs_r.at[k], to)

    other_chunk(2)
    own_chunk(1, store_up)
    x_out[1, HALF:MSG, :] = held[HALF:MSG, :].astype(BF16)
    near_a.wait_recv()
    x_out[1, 0:HALF, :] = (held[0:HALF, :] + x_near_a[...].astype(F32)).astype(BF16)
    x_copy(0, 0).start()
    x_copy(0, 1).start()

    other_chunk(3)
    own_chunk(2, store_up)
    x_out[2, 0:HALF, :] = held[0:HALF, :].astype(BF16)
    x_copy(1, 0).start()
    near_b.wait_recv()
    x_out[2, HALF:MSG, :] = (held[HALF:MSG, :] + x_near_b[...].astype(F32)).astype(BF16)
    x_copy(1, 1).start()

    own_chunk(3, store_up)

    def add_x(part):
        rows = slice(0, FIRST) if part == 0 else slice(FIRST, MSG)
        x_copy(0, part).wait_recv()
        x_copy(1, part).wait_recv()
        held[rows, :] += x_in[0, rows, :].astype(F32) + x_in[1, rows, :].astype(F32)

    add_x(0)

    def piece_of(u, dd):
        return held[pl.ds(pl.multiple_of(16 + PIECE * (2 * u + dd), 16), PIECE), :]

    rest_pack = held[0:16, :]
    h_up, h_down = ring(h + 1), ring(h - 1)

    def fill(slot, value, extra):
        z_out[slot, 0:48, :] = value.astype(BF16)
        z_out[slot, 48:64, :] = extra.astype(BF16)

    fill(0, piece_of(0, 0), rest_pack)
    fill(1, piece_of(0, 1), rest_pack)
    relay_up = copy(z_out.at[0], z_relay.at[0], zs_s.at[0], zs_r.at[0], at_img(x, h_up, d))
    relay_down = copy(z_out.at[1], z_relay.at[1], zs_s.at[1], zs_r.at[1], at_img(x, h_down, d))
    relay_up.start()
    relay_down.start()
    add_x(1)

    def z_copy(slot):
        way, dd = (slot - 2) // 2, (slot - 2) % 2
        to = at_img(x, h_up if way == 0 else h_down, dd)
        return copy(z_out.at[slot], z_in.at[way, d], zs_s.at[slot], zs_r.at[2 + 2 * way + d], to)

    fill(3, piece_of(1, 1), rest_pack)
    z_copy(3).start()
    fill(4, piece_of(2, 0), rest_pack)
    z_copy(4).start()
    fill(6, piece_of(3, o), rest_pack)
    core_last = copy(z_out.at[6], z_core, zs_s.at[6], zs_r.at[6], other)
    core_last.start()
    relay_up.wait_recv()
    fill(
        2,
        piece_of(1, 0) + z_relay[0, 0:48, :].astype(F32),
        rest_pack + z_relay[0, 48:64, :].astype(F32),
    )
    z_copy(2).start()
    relay_down.wait_recv()
    fill(
        5,
        piece_of(2, 1) + z_relay[1, 0:48, :].astype(F32),
        rest_pack + z_relay[1, 48:64, :].astype(F32),
    )
    z_copy(5).start()

    mine = jnp.concatenate([piece_of(3, d), rest_pack], axis=0)
    core_last.wait_recv()
    theirs = z_core[...].astype(F32)
    for way in range(2):
        for c in range(2):
            slot = z_in.at[way, c]
            copy(slot, slot, zs_s.at[2], zs_r.at[2 + 2 * way + c], other).wait_recv()
    local = 2 * h + d
    packs = []
    for c in range(2):
        both = jnp.where(d == c, mine, theirs)
        both = both + z_in[0, c].astype(F32) + z_in[1, c].astype(F32)
        cls_ref[c, :, 0:128] = both[0:48]
        pack = both[48:64]
        packs.append(pack)
        for a in range(3):
            cls_ref[c, 16 * a : 16 * a + 16, 128:256] = left(pack, 32 * a + 4 * local)
    group_all = jnp.where(lane < 24, left(packs[0], 96), left(packs[1], 72))
    group_all = jnp.where(lane < 48, group_all, 0.0)
    span = pl.ds(pl.multiple_of(img * 128, 128), 256)
    turn = lax.rem(256 - 4 * img, 256)
    curve = curve_ref[:, span]
    gain = pltpu.roll(curve * curve * noise_row(img, 2), turn, 1)
    contrast = lax.dot_general(
        jnp.transpose(jnp.concatenate([group_all, jnp.zeros((112, 128), F32)], axis=0))[:NPROJ, :GROUPS],
        gain,
        (((1,), (0,)), ((), ())),
        precision=HIGHEST,
        preferred_element_type=F32,
    )
    con_ref[...] = contrast

    for e in range(4):
        forward(columns[e], False)
        for way in range(2):
            y_copy(way, e, y).wait_send()
            f_copy(way, e, y).wait_send()
    for c in st_copies:
        c.wait_send()
    for i in range(4):
        core_copy(i).wait_send()
    for c in (rest_copy, near_a, near_b, relay_up, relay_down, core_last):
        c.wait_send()
    for way in range(2):
        for part in range(2):
            x_copy(way, part).wait_send()
    for slot in range(2, 6):
        z_copy(slot).wait_send()


def on_device(
    images, projections, contrast_curve, noise_weight, defocus_group, shifts, orient_index, orient_prior
):
    rows = jnp.pad(images.transpose(1, 0, 2).reshape(2 * NIMG, 264), ((0, 0), (0, 120)))
    vmem = pl.BlockSpec(memory_space=pltpu.VMEM)
    sem = pltpu.SemaphoreType.DMA
    cls, con, ev = pl.pallas_call(
        body,
        out_shape=(
            jax.ShapeDtypeStruct((2, NPROJ, 256), F32),
            jax.ShapeDtypeStruct((NPROJ, 256), F32),
            jax.ShapeDtypeStruct((1, 128), F32),
        ),
        in_specs=[vmem, vmem, vmem, vmem, vmem, pl.BlockSpec(memory_space=pltpu.SMEM), vmem, vmem],
        out_specs=(vmem, vmem, vmem),
        scratch_shapes=[
            pltpu.VMEM((16, SHARD, 128), BF16),
            pltpu.VMEM((16, 2, NPROJ, 256), BF16),
            pltpu.VMEM((2, NPROJ, 128), BF16),
            pltpu.VMEM((16, 8, 256), F32),
            pltpu.VMEM((16, 8, 256), F32),
            pltpu.VMEM((8, 128), F32),
            pltpu.VMEM((8, 128), F32),
            pltpu.VMEM((16, 2, ROWS, 256), BF16),
            pltpu.VMEM((2, ROWS, 128), BF16),
            pltpu.VMEM((ROWS, NPROJ), F32),
            pltpu.VMEM((NPROJ, ROWS), BF16),
            pltpu.VMEM((16, 8, 128), F32),
            pltpu.VMEM((4, 8 * PIECE, 128), BF16),
            pltpu.VMEM((4, 8 * PIECE, 128), BF16),
            pltpu.VMEM((64, 128), BF16),
            pltpu.VMEM((64, 128), BF16),
            pltpu.VMEM((3, MSG, 128), BF16),
            pltpu.VMEM((HALF, 128), BF16),
            pltpu.VMEM((MSG - HALF, 128), BF16),
            pltpu.VMEM((2, MSG, 128), BF16),
            pltpu.VMEM((MSG, 128), F32),
            pltpu.VMEM((7, 64, 128), BF16),
            pltpu.VMEM((2, 64, 128), BF16),
            pltpu.VMEM((2, 2, 64, 128), BF16),
            pltpu.VMEM((64, 128), BF16),
            sem((4,)),
            sem((4,)),
            sem((4,)),
            sem((2, 4)),
            sem((2, 4)),
            sem((2, 4)),
            sem((2, 4)),
            sem((16,)),
            sem((16,)),
            sem((5,)),
            sem((5,)),
            sem((6,)),
            sem((6,)),
            sem((7,)),
            sem((7,)),
        ],
        compiler_params=pltpu.CompilerParams(
            collective_id=0, has_side_effects=True, vmem_limit_bytes=40 * 1024 * 1024
        ),
        name="expectation",
    )(
        rows,
        projections.transpose(1, 0, 2),
        contrast_curve,
        noise_weight.reshape(NPIX // 128, 128),
        defocus_group.reshape(1, NIMG),
        shifts.T,
        orient_index.reshape(1, NPROJ),
        orient_prior.reshape(2, 128),
    )
    return cls[:, :, :132].transpose(1, 0, 2), con[:, :132], ev[0, :NIMG]


def solution(mesh):
    in_specs = (P("img", None, "ref"), P("ref", None, None), P(), P(), P("img"), P(), P("ref"), P())
    out_specs = (P("ref", None, "img"), P("ref", "img"), P("img"))
    return jax.shard_map(
        on_device, mesh=mesh, in_specs=in_specs, out_specs=out_specs, check_vma=False
    )
```

```python
import math

import jax
import jax.numpy as jnp
from jax import lax
from jax.experimental import pallas as pl
from jax.experimental.pallas import tpu as pltpu
from jax.sharding import PartitionSpec as P

MESH = pl.DeviceIdType.MESH
F32 = jnp.float32
BF16 = jnp.bfloat16
HIGHEST = lax.Precision.HIGHEST
NT = (((1,), (1,)), ((), ()))
TN = (((0,), (0,)), ((), ()))

NPIX = 4224
BOX = 128
NSHIFT = 9
NIMG = 64
NPROJ = 48
GROUPS = 16
ROWS = NSHIFT * NIMG
SHARD = 272
PIECE = 48
MSG = 400
HALF = 208
FIRST = 112


def sincos(steps):
    quadrant = lax.shift_right_arithmetic(steps + 16, 5)
    rest = (steps - quadrant * 32).astype(F32) * (2.0 * math.pi / BOX)
    sq = rest * rest
    sin_part = rest * (
        1.0 + sq * (-1.0 / 6 + sq * (1.0 / 120 + sq * (-1.0 / 5040 + sq * (1.0 / 362880))))
    )
    cos_part = 1.0 + sq * (
        -0.5 + sq * (1.0 / 24 + sq * (-1.0 / 720 + sq * (1.0 / 40320 - sq * (1.0 / 3628800))))
    )
    odd = (quadrant & 1) == 1
    flip_sin = (quadrant & 2) == 2
    flip_cos = ((quadrant + 1) & 2) == 2
    sine = jnp.where(odd, cos_part, sin_part)
    cosine = jnp.where(odd, sin_part, cos_part)
    return jnp.where(flip_cos, -cosine, cosine), jnp.where(flip_sin, -sine, sine)


def gather(img_ref, proj_ref, curve_ref, noise_ref, group_ref, shift_ref, orient_ref, prior_ref,
    smain, shrest, wts, gsum_ref, ev_ref,
    xbuf, pmain, prest, ctab, stab, crest, srest, score, stat, ag_z_s, ag_z_r, ag_y_s, ag_y_r, ag_f_s, ag_f_r, st_s, st_r):
    img = lax.axis_index("img")
    ref = lax.axis_index("ref")
    x = lax.div(img, 8)
    h = lax.rem(lax.div(img, 2), 4)
    d = lax.rem(img, 2)
    o = 1 - d
    y = lax.div(ref, 4)
    l = lax.rem(ref, 4)

    def ring(v):
        return lax.rem(v + 4, 4)

    def dev(img_at=img, ref_at=ref):
        return {"img": img_at, "ref": ref_at}

    def at_img(xx, hh, dd):
        return dev(img_at=(xx * 4 + hh) * 2 + dd)

    def copy(src, dst, send, recv, to):
        return pltpu.make_async_remote_copy(
            src_ref=src, dst_ref=dst, send_sem=send, recv_sem=recv, device_id=to, device_id_type=MESH
        )

    barrier = pltpu.get_barrier_semaphore()
    peers = [dev(ref_at=lax.rem(ref + k, 16)) for k in range(1, 16)]
    for peer in peers:
        pl.semaphore_signal(barrier, inc=1, device_id=peer, device_id_type=MESH)
    lane = lax.broadcasted_iota(jnp.int32, (1, 128), 1)

    def noise_row(tile, count):
        return jnp.concatenate([noise_ref[pl.ds(tile + t, 1), :] for t in range(count)], axis=1)


    group_row = group_ref[...].astype(F32)
    group_row = jnp.concatenate([group_row, group_row], axis=1)
    group_col = jnp.transpose(jnp.broadcast_to(group_row, (128, 128)))[:NIMG, :]
    start = pl.multiple_of(ref * 256, 128)
    turn = lax.rem(384 - 8 * ref, 384)
    curve_here = pltpu.roll(curve_ref[:, pl.ds(start, 384)], turn, 1)
    noise_here = pltpu.roll(jnp.broadcast_to(noise_row(2 * ref, 3), (8, 384)), turn, 1)[:1, :]
    parts = []
    for tile in range(3):
        span = slice(tile * 128, tile * 128 + 128)
        gain = jnp.zeros((NIMG, 128), F32)
        for g in range(GROUPS):
            gain = jnp.where(group_col == float(g), curve_here[g : g + 1, span], gain)
        gain = gain * noise_here[:, span]
        parts.append(img_ref[:, span].astype(F32) * jnp.concatenate([gain, gain], axis=0))
    second = pltpu.roll(jnp.concatenate(parts[1:], axis=1), 252, 1)[:, :128]
    rest = jnp.transpose(jnp.where(lane < 4, parts[1], parts[2]))[:16, :]
    row16 = lax.broadcasted_iota(jnp.int32, (16, 128), 0)
    rest = jnp.where(row16 < 8, rest, 0.0)
    xbuf[ref, 0:128, :] = parts[0].astype(BF16)
    xbuf[ref, 128:256, :] = second.astype(BF16)
    xbuf[ref, 256:272, :] = rest.astype(BF16)

    pl.semaphore_wait(barrier, len(peers))

    columns = [lax.rem(l + 4 - e, 4) for e in range(4)]
    halves = (pl.ds(0, 144), pl.ds(144, 128))

    def shard(yy, e):
        return yy * 4 + columns[e]

    def z_send(e, part):
        block = xbuf.at[ref, halves[part]]
        to = dev(ref_at=y * 4 + lax.rem(l + e, 4))
        return copy(block, block, ag_z_s.at[e, part], ag_z_r.at[e, part], to)

    y_up, y_down, y_far = ring(y + 1), ring(y - 1), ring(y + 2)

    def y_copy(way, e, src_y, part):
        to = dev(ref_at=(y_up if way == 0 else y_down) * 4 + l)
        block = xbuf.at[shard(src_y, e), halves[part]]
        return copy(block, block, ag_y_s.at[way, e, part], ag_y_r.at[way, e, part], to)

    def f_copy(way, e, src_y):
        to = dev(ref_at=(y_up if way == 0 else y_down) * 4 + l)
        block = xbuf.at[shard(src_y, e), halves[way]]
        return copy(block, block, ag_f_s.at[way, e], ag_f_r.at[way, e], to)

    def send_y(e):
        y_copy(0, e, y, 0).start()
        y_copy(1, e, y, 1).start()
        y_copy(0, e, y, 1).start()
        y_copy(1, e, y, 0).start()

    z_send(1, 0).start()
    z_send(3, 0).start()
    send_y(0)
    z_send(1, 1).start()
    z_send(3, 1).start()
    z_send(2, 0).start()
    z_send(2, 1).start()

    def take_z(e):
        for part in range(2):
            block = xbuf.at[shard(y, e), halves[part]]
            copy(block, block, ag_z_s.at[e, part], ag_z_r.at[e, part], dev(ref_at=shard(y, e))).wait_recv()
        send_y(e)

    def take_y(e):
        y_copy(0, e, y_down, 0).wait_recv()
        f_copy(0, e, y_down).start()
        y_copy(1, e, y_up, 1).wait_recv()
        f_copy(1, e, y_up).start()
        y_copy(0, e, y_down, 1).wait_recv()
        y_copy(1, e, y_up, 0).wait_recv()

    def take_far(e):
        f_copy(0, e, y_far).wait_recv()
        f_copy(1, e, y_far).wait_recv()

    def table(pixel, width):
        srow = lax.broadcasted_iota(jnp.int32, (8, width), 0) + 1
        move_x = jnp.zeros((8, width), jnp.int32)
        move_y = jnp.zeros((8, width), jnp.int32)
        for s in range(1, NSHIFT):
            move_x = jnp.where(srow == s, shift_ref[0, s], move_x)
            move_y = jnp.where(srow == s, shift_ref[1, s], move_y)
        freq_x = pixel & (BOX // 2 - 1)
        freq_y = lax.shift_right_logical(pixel, 6) - NPIX // BOX
        return sincos((move_x * freq_x + move_y * freq_y) & (BOX - 1))

    def table_step(b, carry):
        at = lax.broadcasted_iota(jnp.int32, (8, 256), 1)
        pixel = 264 * b + at + jnp.where(at >= 128, 4, 0)
        cosine, sine = table(pixel, 256)
        ctab[b] = cosine
        stab[b] = sine
        return carry

    lax.fori_loop(0, 16, table_step, 0)
    at = lax.broadcasted_iota(jnp.int32, (8, 128), 1)
    cosine, sine = table(132 * lax.shift_right_logical(at, 2) + 128 + (at & 3), 128)
    crest[...] = cosine
    srest[...] = sine

    def proj_step(b, carry):
        out = []
        for c in range(2):
            kept = carry[c]
            for u in range(2):
                n = 2 * b + u
                window = proj_ref[c, :, pl.ds(pl.multiple_of(n * 128, 128), 256)].astype(F32)
                turned = pltpu.roll(window, lax.rem(256 - 4 * n, 256), 1)
                pmain[b, c, :, u * 128 : u * 128 + 128] = turned[:, :128].astype(BF16)
                kept = jnp.where(lax.shift_right_logical(lane, 2) == n, window[:, 128:], kept)
            out.append(kept)
        return tuple(out)

    zero_rest = jnp.zeros((NPROJ, 128), F32)
    rests = lax.fori_loop(0, 16, proj_step, (zero_rest, zero_rest))
    for c in range(2):
        prest[c] = rests[c].astype(BF16)

    take_y(0)
    take_z(1)
    take_z(3)

    def norm_step(t, total):
        span = pl.ds(pl.multiple_of(t * 384, 128), 384)
        re = proj_ref[0, :, span].astype(F32)
        im = proj_ref[1, :, span].astype(F32)
        curve = curve_ref[:, span]
        gain = 0.5 * (curve * curve * noise_row(3 * t, 3))
        power = re * re + im * im
        return total + lax.dot_general(
            two_parts(power), two_parts(gain), NT, preferred_element_type=F32
        )

    def two_parts(value):
        high = value.astype(BF16)
        return jnp.concatenate([high, (value - high.astype(F32)).astype(BF16)], axis=0)

    norm = lax.fori_loop(0, 11, norm_step, jnp.zeros((2 * NPROJ, 2 * GROUPS), F32))
    norm = norm[:NPROJ] + norm[NPROJ:]
    norm = norm[:, :GROUPS] + norm[:, GROUPS:]
    grow = lax.broadcasted_iota(jnp.int32, (GROUPS, 128), 0)
    members = (group_row == grow.astype(F32)).astype(F32)
    penalty = jnp.dot(norm, members, precision=HIGHEST, preferred_element_type=F32)
    orient_row = jnp.concatenate([orient_ref[...].astype(F32), jnp.zeros((1, 80), F32)], axis=1)
    orient_col = jnp.transpose(jnp.broadcast_to(orient_row, (128, 128)))[:NPROJ, :]
    prior = jnp.zeros((NPROJ, 1), F32)
    for half in range(2):
        hit = orient_col == (lane + half * 128).astype(F32)
        prior += jnp.sum(
            jnp.where(hit, prior_ref[half : half + 1, :], 0.0), axis=1, keepdims=True
        )
    base = prior - penalty

    score[...] = jnp.zeros_like(score)
    take_y(1)
    take_z(2)

    def process(b):
        for t in range(2):
            span = slice(t * 128, t * 128 + 128)
            re = xbuf[b, t * 128 : t * 128 + 64, :]
            im = xbuf[b, t * 128 + 64 : t * 128 + 128, :]
            smain[b, 0, 0:NIMG, span] = re
            smain[b, 1, 0:NIMG, span] = im
            re = re.astype(F32)
            im = im.astype(F32)
            for s in range(1, NSHIFT):
                rows = slice(s * NIMG, s * NIMG + NIMG)
                cosine = ctab[b, s - 1 : s, span]
                sine = stab[b, s - 1 : s, span]
                smain[b, 0, rows, span] = (re * cosine + im * sine).astype(BF16)
                smain[b, 1, rows, span] = (im * cosine - re * sine).astype(BF16)
        score[...] += lax.dot_general(
            smain[b, 0], pmain[b, 0], NT, preferred_element_type=F32
        ) + lax.dot_general(smain[b, 1], pmain[b, 1], NT, preferred_element_type=F32)

    def process_all(blocks):
        def step(t, carry):
            b = blocks[0]
            for k in range(1, len(blocks)):
                b = jnp.where(t == k, blocks[k], b)
            process(b)
            return carry

        lax.fori_loop(0, len(blocks), step, 0)

    process_all([shard(y, 0), shard(y, 1), shard(y_down, 0), shard(y_up, 0)])
    take_y(3)
    take_far(0)
    process_all([shard(y, 3), shard(y_down, 1), shard(y_up, 1), shard(y_far, 0)])
    take_y(2)
    take_far(1)
    process_all([shard(y, 2), shard(y_down, 3), shard(y_up, 3), shard(y_far, 1)])
    process_all([shard(y_down, 2), shard(y_up, 2)])
    take_far(3)
    process(shard(y_far, 3))
    take_far(2)
    process(shard(y_far, 2))

    rest_t = jnp.concatenate([xbuf[b, 256:272, :].astype(F32)[:8] for b in range(16)], axis=0)
    rest_x = jnp.transpose(rest_t)
    re, im = rest_x[:NIMG], rest_x[NIMG:]
    shrest[0, 0:NIMG, :] = re.astype(BF16)
    shrest[1, 0:NIMG, :] = im.astype(BF16)
    for s in range(1, NSHIFT):
        rows = slice(s * NIMG, s * NIMG + NIMG)
        cosine = crest[s - 1 : s, :]
        sine = srest[s - 1 : s, :]
        shrest[0, rows, :] = (re * cosine + im * sine).astype(BF16)
        shrest[1, rows, :] = (im * cosine - re * sine).astype(BF16)
    full = (
        score[...]
        + lax.dot_general(shrest[0], prest[0], NT, preferred_element_type=F32)
        + lax.dot_general(shrest[1], prest[1], NT, preferred_element_type=F32)
    )
    full = jnp.concatenate([full, jnp.zeros((ROWS, 128 - NPROJ), F32)], axis=1)

    tiles = []
    for t in range(5):
        if t < 4:
            tiles.append(jnp.transpose(full[t * 128 : t * 128 + 128])[:NPROJ] + base)
        else:
            last = jnp.concatenate([full[512:576], jnp.zeros((64, 128), F32)], axis=0)
            tiles.append(jnp.where(lane < 64, jnp.transpose(last)[:NPROJ] + base, -3e38))
    high = tiles[0]
    for t in range(1, 5):
        high = jnp.maximum(high, tiles[t])
    high = jnp.max(high, axis=0, keepdims=True)
    high = jnp.maximum(high, pltpu.roll(jnp.broadcast_to(high, (8, 128)), 64, 1)[:1])
    total = jnp.exp(tiles[0] - high)
    for t in range(1, 5):
        total += jnp.exp(tiles[t] - high)
    total = jnp.sum(total, axis=0, keepdims=True)
    total = total + pltpu.roll(jnp.broadcast_to(total, (8, 128)), 64, 1)[:1]
    row8 = lax.broadcasted_iota(jnp.int32, (8, 128), 0)
    stat[ref] = jnp.where(row8 == 0, high, total)
    st_copies = []
    for k in range(1, 16):
        st_copies.append(
            copy(stat.at[ref], stat.at[ref], st_s.at[k], st_r.at[k], dev(ref_at=lax.rem(ref + k, 16)))
        )
    for c in st_copies:
        c.start()
    for k in range(1, 16):
        src = lax.rem(ref + 16 - k, 16)
        copy(stat.at[src], stat.at[src], st_s.at[k], st_r.at[k], dev(ref_at=src)).wait_recv()
    highest = stat[0, 0:1, :]
    for b in range(1, 16):
        highest = jnp.maximum(highest, stat[b, 0:1, :])
    whole = jnp.zeros((1, 128), F32)
    for b in range(16):
        whole += stat[b, 1:2, :] * jnp.exp(stat[b, 0:1, :] - highest)
    evidence = highest + jnp.log(whole)
    ev_ref[...] = evidence
    for t in range(5):
        w = jnp.exp(tiles[t] - evidence).astype(BF16)
        if t < 4:
            wts[:, t * 128 : t * 128 + 128] = w
        else:
            wts[:, 512:576] = w[:, :64]
    members_all = jnp.concatenate([members.astype(BF16)] * 4 + [members[:, :64].astype(BF16)], axis=1)
    gsum_ref[...] = lax.dot_general(members_all, wts[...], NT, preferred_element_type=F32)

    for e in range(4):
        for part in range(2):
            if e:
                z_send(e, part).wait_send()
            for way in range(2):
                y_copy(way, e, y, part).wait_send()
        for way in range(2):
            f_copy(way, e, y).wait_send()
    for c in st_copies:
        c.wait_send()


def reduce(smain, shrest, wts, gsum_ref, curve_ref, noise_ref,
    cls_ref, con_ref,
    core_out, core_in, rest_out, rest_in, x_out, x_near_a, x_near_b, x_in, held, z_out, z_relay, z_in, z_core,
    co_s, co_r, xs_s, xs_r, zs_s, zs_r):
    img = lax.axis_index("img")
    ref = lax.axis_index("ref")
    x = lax.div(img, 8)
    h = lax.rem(lax.div(img, 2), 4)
    d = lax.rem(img, 2)
    o = 1 - d
    y = lax.div(ref, 4)
    l = lax.rem(ref, 4)

    def ring(v):
        return lax.rem(v + 4, 4)

    def dev(img_at=img, ref_at=ref):
        return {"img": img_at, "ref": ref_at}

    def at_img(xx, hh, dd):
        return dev(img_at=(xx * 4 + hh) * 2 + dd)

    def copy(src, dst, send, recv, to):
        return pltpu.make_async_remote_copy(
            src_ref=src, dst_ref=dst, send_sem=send, recv_sem=recv, device_id=to, device_id_type=MESH
        )

    barrier = pltpu.get_barrier_semaphore()
    peers = [at_img(x, h, o), at_img(ring(x + 1), h, d), at_img(ring(x - 1), h, d)]
    for hh in (ring(h + 1), ring(h - 1)):
        peers += [at_img(x, hh, d), at_img(x, hh, o)]
    for peer in peers:
        pl.semaphore_signal(barrier, inc=1, device_id=peer, device_id_type=MESH)
    pl.semaphore_wait(barrier, len(peers))
    lane = lax.broadcasted_iota(jnp.int32, (1, 128), 1)

    def noise_row(tile, count):
        return jnp.concatenate([noise_ref[pl.ds(tile + t, 1), :] for t in range(count)], axis=1)


    group_sum = jnp.concatenate([gsum_ref[...], jnp.zeros((GROUPS, 80), F32)], axis=1)
    other = at_img(x, h, o)
    rest_out[0:48, :] = jnp.dot(wts[...], shrest[o], preferred_element_type=F32).astype(BF16)
    rest_out[48:64, :] = group_sum.astype(BF16)
    rest_copy = copy(rest_out, rest_in, co_s.at[4], co_r.at[4], other)
    rest_copy.start()

    order = [ring(x + 2), ring(x + 1), ring(x + 3), x]
    runs = [ring(h + 2), ring(h + 1), ring(h + 3), h]

    def core_copy(i):
        return copy(core_out.at[i], core_in.at[i], co_s.at[i], co_r.at[i], other)

    def other_chunk(i):
        for u in range(4):
            got = jnp.dot(wts[...], smain[4 * order[i] + runs[u], o], preferred_element_type=F32)
            for v in range(2):
                r = PIECE * (2 * u + v)
                core_out[i, r : r + PIECE, :] = got[:, v * 128 : v * 128 + 128].astype(BF16)
        core_copy(i).start()

    other_chunk(0)
    other_chunk(1)

    rest_sum = jnp.dot(wts[...], shrest[d], preferred_element_type=F32)
    rest_copy.wait_recv()
    rest_sum = rest_sum + rest_in[0:48, :].astype(F32)
    group_sum = group_sum + rest_in[48:64, :].astype(F32)

    def left(value, by):
        return pltpu.roll(value, lax.rem(256 - by, 128), 1)

    group_half = left(group_sum, 32 + 24 * d)

    def packed(q):
        out = left(rest_sum[0:16], 32 * q)
        out = jnp.where(lane < 32, out, left(rest_sum[16:32], 32 * q - 32))
        out = jnp.where(lane < 64, out, left(rest_sum[32:48], 32 * q - 64))
        return jnp.where(lane < 96, out, group_half)

    def piece_row(k):
        return 16 + PIECE * k

    def own_chunk(i, store):
        q = order[i]
        core_copy(i).wait_recv()
        for u in range(4):
            got = jnp.dot(wts[...], smain[4 * q + runs[u], d], preferred_element_type=F32)
            for v in range(2):
                k = 2 * u + v
                r = PIECE * k
                store(k, got[:, v * 128 : v * 128 + 128] + core_in[i, r : r + PIECE, :].astype(F32))
        store(-1, packed(q))

    x_up, x_down = at_img(ring(x + 1), h, d), at_img(ring(x - 1), h, d)

    def rows_of(k):
        return slice(0, 16) if k < 0 else slice(piece_row(k), piece_row(k) + PIECE)

    def store_far(k, value):
        x_out[0, rows_of(k), :] = value.astype(BF16)

    own_chunk(0, store_far)
    near_a = copy(x_out.at[0, pl.ds(0, HALF)], x_near_a, xs_s.at[0], xs_r.at[0], x_up)
    near_b = copy(x_out.at[0, pl.ds(HALF, MSG - HALF)], x_near_b, xs_s.at[1], xs_r.at[1], x_down)
    near_a.start()
    near_b.start()

    def store_up(k, value):
        held[rows_of(k), :] = value

    def x_copy(way, part):
        rows = pl.ds(0, FIRST) if part == 0 else pl.ds(FIRST, MSG - FIRST)
        k = 2 + 2 * way + part
        to = x_up if way == 0 else x_down
        return copy(x_out.at[1 + way, rows], x_in.at[way, rows], xs_s.at[k], xs_r.at[k], to)

    other_chunk(2)
    own_chunk(1, store_up)
    x_out[1, HALF:MSG, :] = held[HALF:MSG, :].astype(BF16)
    near_a.wait_recv()
    x_out[1, 0:HALF, :] = (held[0:HALF, :] + x_near_a[...].astype(F32)).astype(BF16)
    x_copy(0, 0).start()
    x_copy(0, 1).start()

    other_chunk(3)
    own_chunk(2, store_up)
    x_out[2, 0:HALF, :] = held[0:HALF, :].astype(BF16)
    x_copy(1, 0).start()
    near_b.wait_recv()
    x_out[2, HALF:MSG, :] = (held[HALF:MSG, :] + x_near_b[...].astype(F32)).astype(BF16)
    x_copy(1, 1).start()

    own_chunk(3, store_up)

    def add_x(part):
        rows = slice(0, FIRST) if part == 0 else slice(FIRST, MSG)
        x_copy(0, part).wait_recv()
        x_copy(1, part).wait_recv()
        held[rows, :] += x_in[0, rows, :].astype(F32) + x_in[1, rows, :].astype(F32)

    add_x(0)

    def piece_of(u, dd):
        return held[pl.ds(pl.multiple_of(16 + PIECE * (2 * u + dd), 16), PIECE), :]

    rest_pack = held[0:16, :]
    h_up, h_down = ring(h + 1), ring(h - 1)

    def fill(slot, value, extra):
        z_out[slot, 0:48, :] = value.astype(BF16)
        z_out[slot, 48:64, :] = extra.astype(BF16)

    fill(0, piece_of(0, 0), rest_pack)
    fill(1, piece_of(0, 1), rest_pack)
    relay_up = copy(z_out.at[0], z_relay.at[0], zs_s.at[0], zs_r.at[0], at_img(x, h_up, d))
    relay_down = copy(z_out.at[1], z_relay.at[1], zs_s.at[1], zs_r.at[1], at_img(x, h_down, d))
    relay_up.start()
    relay_down.start()
    add_x(1)

    def z_copy(slot):
        way, dd = (slot - 2) // 2, (slot - 2) % 2
        to = at_img(x, h_up if way == 0 else h_down, dd)
        return copy(z_out.at[slot], z_in.at[way, d], zs_s.at[slot], zs_r.at[2 + 2 * way + d], to)

    fill(3, piece_of(1, 1), rest_pack)
    z_copy(3).start()
    fill(4, piece_of(2, 0), rest_pack)
    z_copy(4).start()
    fill(6, piece_of(3, o), rest_pack)
    core_last = copy(z_out.at[6], z_core, zs_s.at[6], zs_r.at[6], other)
    core_last.start()
    relay_up.wait_recv()
    fill(
        2,
        piece_of(1, 0) + z_relay[0, 0:48, :].astype(F32),
        rest_pack + z_relay[0, 48:64, :].astype(F32),
    )
    z_copy(2).start()
    relay_down.wait_recv()
    fill(
        5,
        piece_of(2, 1) + z_relay[1, 0:48, :].astype(F32),
        rest_pack + z_relay[1, 48:64, :].astype(F32),
    )
    z_copy(5).start()

    mine = jnp.concatenate([piece_of(3, d), rest_pack], axis=0)
    core_last.wait_recv()
    theirs = z_core[...].astype(F32)
    for way in range(2):
        for c in range(2):
            slot = z_in.at[way, c]
            copy(slot, slot, zs_s.at[2], zs_r.at[2 + 2 * way + c], other).wait_recv()
    local = 2 * h + d
    packs = []
    for c in range(2):
        both = jnp.where(d == c, mine, theirs)
        both = both + z_in[0, c].astype(F32) + z_in[1, c].astype(F32)
        cls_ref[c, :, 0:128] = both[0:48]
        pack = both[48:64]
        packs.append(pack)
        for a in range(3):
            cls_ref[c, 16 * a : 16 * a + 16, 128:256] = left(pack, 32 * a + 4 * local)
    group_all = jnp.where(lane < 24, left(packs[0], 96), left(packs[1], 72))
    group_all = jnp.where(lane < 48, group_all, 0.0)
    span = pl.ds(pl.multiple_of(img * 128, 128), 256)
    turn = lax.rem(256 - 4 * img, 256)
    curve = curve_ref[:, span]
    gain = pltpu.roll(curve * curve * noise_row(img, 2), turn, 1)
    contrast = lax.dot_general(
        jnp.transpose(jnp.concatenate([group_all, jnp.zeros((112, 128), F32)], axis=0))[:NPROJ, :GROUPS],
        gain,
        (((1,), (0,)), ((), ())),
        precision=HIGHEST,
        preferred_element_type=F32,
    )
    con_ref[...] = contrast

    for i in range(4):
        core_copy(i).wait_send()
    for c in (rest_copy, near_a, near_b, relay_up, relay_down, core_last):
        c.wait_send()
    for way in range(2):
        for part in range(2):
            x_copy(way, part).wait_send()
    for slot in range(2, 6):
        z_copy(slot).wait_send()


def on_device(
    images, projections, contrast_curve, noise_weight, defocus_group, shifts, orient_index, orient_prior
):
    rows = jnp.pad(images.transpose(1, 0, 2).reshape(2 * NIMG, 264), ((0, 0), (0, 120)))
    vmem = pl.BlockSpec(memory_space=pltpu.VMEM)
    sem = pltpu.SemaphoreType.DMA
    noise = noise_weight.reshape(NPIX // 128, 128)
    S = jax.ShapeDtypeStruct
    smain, shrest, wts, gsum, ev = pl.pallas_call(
        gather,
        out_shape=(
            S((16, 2, ROWS, 256), BF16),
            S((2, ROWS, 128), BF16),
            S((NPROJ, ROWS), BF16),
            S((GROUPS, NPROJ), F32),
            S((1, 128), F32),
        ),
        in_specs=[vmem, vmem, vmem, vmem, vmem, pl.BlockSpec(memory_space=pltpu.SMEM), vmem, vmem],
        out_specs=(vmem,) * 5,
        scratch_shapes=[
            pltpu.VMEM((16, SHARD, 128), BF16),
            pltpu.VMEM((16, 2, NPROJ, 256), BF16),
            pltpu.VMEM((2, NPROJ, 128), BF16),
            pltpu.VMEM((16, 8, 256), F32),
            pltpu.VMEM((16, 8, 256), F32),
            pltpu.VMEM((8, 128), F32),
            pltpu.VMEM((8, 128), F32),
            pltpu.VMEM((ROWS, NPROJ), F32),
            pltpu.VMEM((16, 8, 128), F32),
            sem((4, 2)),
            sem((4, 2)),
            sem((2, 4, 2)),
            sem((2, 4, 2)),
            sem((2, 4)),
            sem((2, 4)),
            sem((16,)),
            sem((16,)),
        ],
        compiler_params=pltpu.CompilerParams(
            collective_id=0, has_side_effects=True, vmem_limit_bytes=30 * 1024 * 1024
        ),
        name="gather",
    )(
        rows,
        projections.transpose(1, 0, 2),
        contrast_curve,
        noise,
        defocus_group.reshape(1, NIMG),
        shifts.T,
        orient_index.reshape(1, NPROJ),
        orient_prior.reshape(2, 128),
    )
    cls, con = pl.pallas_call(
        reduce,
        out_shape=(S((2, NPROJ, 256), F32), S((NPROJ, 256), F32)),
        in_specs=[vmem] * 6,
        out_specs=(vmem,) * 2,
        scratch_shapes=[
            pltpu.VMEM((4, 8 * PIECE, 128), BF16),
            pltpu.VMEM((4, 8 * PIECE, 128), BF16),
            pltpu.VMEM((64, 128), BF16),
            pltpu.VMEM((64, 128), BF16),
            pltpu.VMEM((3, MSG, 128), BF16),
            pltpu.VMEM((HALF, 128), BF16),
            pltpu.VMEM((MSG - HALF, 128), BF16),
            pltpu.VMEM((2, MSG, 128), BF16),
            pltpu.VMEM((MSG, 128), F32),
            pltpu.VMEM((7, 64, 128), BF16),
            pltpu.VMEM((2, 64, 128), BF16),
            pltpu.VMEM((2, 2, 64, 128), BF16),
            pltpu.VMEM((64, 128), BF16),
            sem((5,)),
            sem((5,)),
            sem((6,)),
            sem((6,)),
            sem((7,)),
            sem((7,)),
        ],
        compiler_params=pltpu.CompilerParams(
            collective_id=1, has_side_effects=True, vmem_limit_bytes=30 * 1024 * 1024
        ),
        name="reduce",
    )(smain, shrest, wts, gsum, contrast_curve, noise)
    return cls[:, :, :132].transpose(1, 0, 2), con[:, :132], ev[0, :NIMG]


def solution(mesh):
    in_specs = (P("img", None, "ref"), P("ref", None, None), P(), P(), P("img"), P(), P("ref"), P())
    out_specs = (P("ref", None, "img"), P("ref", "img"), P("img"))
    return jax.shard_map(
        on_device, mesh=mesh, in_specs=in_specs, out_specs=out_specs, check_vma=False
    )
```

```python
import math

import jax
import jax.numpy as jnp
from jax import lax
from jax.experimental import pallas as pl
from jax.experimental.pallas import tpu as pltpu
from jax.sharding import PartitionSpec as P

MESH = pl.DeviceIdType.MESH
F32 = jnp.float32
BF16 = jnp.bfloat16
HIGHEST = lax.Precision.HIGHEST
NT = (((1,), (1,)), ((), ()))
TN = (((0,), (0,)), ((), ()))

NPIX = 4224
BOX = 128
NSHIFT = 9
NIMG = 64
NPROJ = 48
GROUPS = 16
ROWS = NSHIFT * NIMG
SHARD = 272
PIECE = 48
MSG = 400
HALF = 208
FIRST = 112


def sincos(steps):
    quadrant = lax.shift_right_arithmetic(steps + 16, 5)
    rest = (steps - quadrant * 32).astype(F32) * (2.0 * math.pi / BOX)
    sq = rest * rest
    sin_part = rest * (
        1.0 + sq * (-1.0 / 6 + sq * (1.0 / 120 + sq * (-1.0 / 5040 + sq * (1.0 / 362880))))
    )
    cos_part = 1.0 + sq * (
        -0.5 + sq * (1.0 / 24 + sq * (-1.0 / 720 + sq * (1.0 / 40320 - sq * (1.0 / 3628800))))
    )
    odd = (quadrant & 1) == 1
    flip_sin = (quadrant & 2) == 2
    flip_cos = ((quadrant + 1) & 2) == 2
    sine = jnp.where(odd, cos_part, sin_part)
    cosine = jnp.where(odd, sin_part, cos_part)
    return jnp.where(flip_cos, -cosine, cosine), jnp.where(flip_sin, -sine, sine)


def body(
    img_ref,
    proj_ref,
    curve_ref,
    noise_ref,
    group_ref,
    shift_ref,
    orient_ref,
    prior_ref,
    cls_ref,
    con_ref,
    ev_ref,
    xbuf,
    pmain,
    prest,
    ctab,
    stab,
    crest,
    srest,
    smain,
    shrest,
    score,
    wts,
    stat,
    core_out,
    core_in,
    rest_out,
    rest_in,
    x_out,
    x_near_a,
    x_near_b,
    x_in,
    held,
    z_out,
    z_relay,
    z_in,
    z_core,
    ag_z_s,
    ag_z_r,
    ag_y_s,
    ag_y_r,
    ag_f_s,
    ag_f_r,
    st_s,
    st_r,
    co_s,
    co_r,
    xs_s,
    xs_r,
    zs_s,
    zs_r,
):
    img = lax.axis_index("img")
    ref = lax.axis_index("ref")
    x = lax.div(img, 8)
    h = lax.rem(lax.div(img, 2), 4)
    d = lax.rem(img, 2)
    o = 1 - d
    y = lax.div(ref, 4)
    l = lax.rem(ref, 4)

    def ring(v):
        return lax.rem(v + 4, 4)

    def dev(img_at=img, ref_at=ref):
        return {"img": img_at, "ref": ref_at}

    def at_img(xx, hh, dd):
        return dev(img_at=(xx * 4 + hh) * 2 + dd)

    def copy(src, dst, send, recv, to):
        return pltpu.make_async_remote_copy(
            src_ref=src, dst_ref=dst, send_sem=send, recv_sem=recv, device_id=to, device_id_type=MESH
        )

    barrier = pltpu.get_barrier_semaphore()
    peers = [dev(ref_at=y * 4 + lax.rem(l + k, 4)) for k in range(1, 4)]
    peers += [dev(ref_at=lax.rem(ref + 4 * k, 16)) for k in range(1, 4)]
    peers += [at_img(x, h, o), at_img(ring(x + 1), h, d), at_img(ring(x - 1), h, d)]
    for hh in (ring(h + 1), ring(h - 1)):
        peers += [at_img(x, hh, d), at_img(x, hh, o)]
    for peer in peers:
        pl.semaphore_signal(barrier, inc=1, device_id=peer, device_id_type=MESH)

    lane = lax.broadcasted_iota(jnp.int32, (1, 128), 1)

    def noise_row(tile, count):
        return jnp.concatenate([noise_ref[pl.ds(tile + t, 1), :] for t in range(count)], axis=1)


    group_row = group_ref[...].astype(F32)
    group_row = jnp.concatenate([group_row, group_row], axis=1)
    group_col = jnp.transpose(jnp.broadcast_to(group_row, (128, 128)))[:NIMG, :]
    start = pl.multiple_of(ref * 256, 128)
    turn = lax.rem(384 - 8 * ref, 384)
    curve_here = pltpu.roll(curve_ref[:, pl.ds(start, 384)], turn, 1)
    noise_here = pltpu.roll(jnp.broadcast_to(noise_row(2 * ref, 3), (8, 384)), turn, 1)[:1, :]
    parts = []
    for tile in range(3):
        span = slice(tile * 128, tile * 128 + 128)
        gain = jnp.zeros((NIMG, 128), F32)
        for g in range(GROUPS):
            gain = jnp.where(group_col == float(g), curve_here[g : g + 1, span], gain)
        gain = gain * noise_here[:, span]
        parts.append(img_ref[:, span].astype(F32) * jnp.concatenate([gain, gain], axis=0))
    second = pltpu.roll(jnp.concatenate(parts[1:], axis=1), 252, 1)[:, :128]
    rest = jnp.transpose(jnp.where(lane < 4, parts[1], parts[2]))[:16, :]
    row16 = lax.broadcasted_iota(jnp.int32, (16, 128), 0)
    rest = jnp.where(row16 < 8, rest, 0.0)
    xbuf[ref, 0:128, :] = parts[0].astype(BF16)
    xbuf[ref, 128:256, :] = second.astype(BF16)
    xbuf[ref, 256:272, :] = rest.astype(BF16)

    pl.semaphore_wait(barrier, len(peers))

    columns = [lax.rem(l + 4 - e, 4) for e in range(4)]
    halves = (pl.ds(0, 144), pl.ds(144, 128))

    def shard(yy, e):
        return yy * 4 + columns[e]

    def z_send(e, part):
        block = xbuf.at[ref, halves[part]]
        to = dev(ref_at=y * 4 + lax.rem(l + e, 4))
        return copy(block, block, ag_z_s.at[e, part], ag_z_r.at[e, part], to)

    y_up, y_down, y_far = ring(y + 1), ring(y - 1), ring(y + 2)

    def y_copy(way, e, src_y, part):
        to = dev(ref_at=(y_up if way == 0 else y_down) * 4 + l)
        block = xbuf.at[shard(src_y, e), halves[part]]
        return copy(block, block, ag_y_s.at[way, e, part], ag_y_r.at[way, e, part], to)

    def f_copy(way, e, src_y):
        to = dev(ref_at=(y_up if way == 0 else y_down) * 4 + l)
        block = xbuf.at[shard(src_y, e), halves[way]]
        return copy(block, block, ag_f_s.at[way, e], ag_f_r.at[way, e], to)

    def send_y(e):
        y_copy(0, e, y, 0).start()
        y_copy(1, e, y, 1).start()
        y_copy(0, e, y, 1).start()
        y_copy(1, e, y, 0).start()

    z_send(1, 0).start()
    z_send(3, 0).start()
    send_y(0)
    z_send(1, 1).start()
    z_send(3, 1).start()
    z_send(2, 0).start()
    z_send(2, 1).start()

    def take_z(e):
        for part in range(2):
            block = xbuf.at[shard(y, e), halves[part]]
            copy(block, block, ag_z_s.at[e, part], ag_z_r.at[e, part], dev(ref_at=shard(y, e))).wait_recv()
        send_y(e)

    def take_y(e):
        y_copy(0, e, y_down, 0).wait_recv()
        f_copy(0, e, y_down).start()
        y_copy(1, e, y_up, 1).wait_recv()
        f_copy(1, e, y_up).start()
        y_copy(0, e, y_down, 1).wait_recv()
        y_copy(1, e, y_up, 0).wait_recv()

    def take_far(e):
        f_copy(0, e, y_far).wait_recv()
        f_copy(1, e, y_far).wait_recv()

    def table(pixel, width):
        srow = lax.broadcasted_iota(jnp.int32, (8, width), 0) + 1
        move_x = jnp.zeros((8, width), jnp.int32)
        move_y = jnp.zeros((8, width), jnp.int32)
        for s in range(1, NSHIFT):
            move_x = jnp.where(srow == s, shift_ref[0, s], move_x)
            move_y = jnp.where(srow == s, shift_ref[1, s], move_y)
        freq_x = pixel & (BOX // 2 - 1)
        freq_y = lax.shift_right_logical(pixel, 6) - NPIX // BOX
        return sincos((move_x * freq_x + move_y * freq_y) & (BOX - 1))

    def table_step(b, carry):
        at = lax.broadcasted_iota(jnp.int32, (8, 256), 1)
        pixel = 264 * b + at + jnp.where(at >= 128, 4, 0)
        cosine, sine = table(pixel, 256)
        ctab[b] = cosine
        stab[b] = sine
        return carry

    lax.fori_loop(0, 16, table_step, 0)
    at = lax.broadcasted_iota(jnp.int32, (8, 128), 1)
    cosine, sine = table(132 * lax.shift_right_logical(at, 2) + 128 + (at & 3), 128)
    crest[...] = cosine
    srest[...] = sine

    def proj_step(b, carry):
        out = []
        for c in range(2):
            kept = carry[c]
            for u in range(2):
                n = 2 * b + u
                window = proj_ref[c, :, pl.ds(pl.multiple_of(n * 128, 128), 256)].astype(F32)
                turned = pltpu.roll(window, lax.rem(256 - 4 * n, 256), 1)
                pmain[b, c, :, u * 128 : u * 128 + 128] = turned[:, :128].astype(BF16)
                kept = jnp.where(lax.shift_right_logical(lane, 2) == n, window[:, 128:], kept)
            out.append(kept)
        return tuple(out)

    zero_rest = jnp.zeros((NPROJ, 128), F32)
    rests = lax.fori_loop(0, 16, proj_step, (zero_rest, zero_rest))
    for c in range(2):
        prest[c] = rests[c].astype(BF16)

    take_y(0)
    take_z(1)
    take_z(3)

    def norm_step(t, total):
        span = pl.ds(pl.multiple_of(t * 384, 128), 384)
        re = proj_ref[0, :, span].astype(F32)
        im = proj_ref[1, :, span].astype(F32)
        curve = curve_ref[:, span]
        gain = 0.5 * (curve * curve * noise_row(3 * t, 3))
        power = re * re + im * im
        return total + lax.dot_general(
            two_parts(power), two_parts(gain), NT, preferred_element_type=F32
        )

    def two_parts(value):
        high = value.astype(BF16)
        return jnp.concatenate([high, (value - high.astype(F32)).astype(BF16)], axis=0)

    norm = lax.fori_loop(0, 11, norm_step, jnp.zeros((2 * NPROJ, 2 * GROUPS), F32))
    norm = norm[:NPROJ] + norm[NPROJ:]
    norm = norm[:, :GROUPS] + norm[:, GROUPS:]
    grow = lax.broadcasted_iota(jnp.int32, (GROUPS, 128), 0)
    members = (group_row == grow.astype(F32)).astype(F32)
    penalty = jnp.dot(norm, members, precision=HIGHEST, preferred_element_type=F32)
    orient_row = jnp.concatenate([orient_ref[...].astype(F32), jnp.zeros((1, 80), F32)], axis=1)
    orient_col = jnp.transpose(jnp.broadcast_to(orient_row, (128, 128)))[:NPROJ, :]
    prior = jnp.zeros((NPROJ, 1), F32)
    for half in range(2):
        hit = orient_col == (lane + half * 128).astype(F32)
        prior += jnp.sum(
            jnp.where(hit, prior_ref[half : half + 1, :], 0.0), axis=1, keepdims=True
        )
    base = prior - penalty

    score[...] = jnp.zeros_like(score)

    def process(b):
        for t in range(2):
            span = slice(t * 128, t * 128 + 128)
            re = xbuf[b, t * 128 : t * 128 + 64, :]
            im = xbuf[b, t * 128 + 64 : t * 128 + 128, :]
            smain[b, 0, 0:NIMG, span] = re
            smain[b, 1, 0:NIMG, span] = im
            re = re.astype(F32)
            im = im.astype(F32)
            for s in range(1, NSHIFT):
                rows = slice(s * NIMG, s * NIMG + NIMG)
                cosine = ctab[b, s - 1 : s, span]
                sine = stab[b, s - 1 : s, span]
                smain[b, 0, rows, span] = (re * cosine + im * sine).astype(BF16)
                smain[b, 1, rows, span] = (im * cosine - re * sine).astype(BF16)
        score[...] += lax.dot_general(
            smain[b, 0], pmain[b, 0], NT, preferred_element_type=F32
        ) + lax.dot_general(smain[b, 1], pmain[b, 1], NT, preferred_element_type=F32)

    def process_all(blocks):
        def step(t, carry):
            b = blocks[0]
            for k in range(1, len(blocks)):
                b = jnp.where(t == k, blocks[k], b)
            process(b)
            return carry

        lax.fori_loop(0, len(blocks), step, 0)

    process(shard(y, 0))
    take_z(2)
    take_y(1)
    process_all([shard(y, 1), shard(y_down, 0), shard(y_up, 0)])
    take_y(3)
    take_far(0)
    process_all([shard(y, 3), shard(y_down, 1), shard(y_up, 1), shard(y_far, 0)])
    take_y(2)
    take_far(1)
    process_all([shard(y, 2), shard(y_down, 3), shard(y_up, 3), shard(y_far, 1)])
    process_all([shard(y_down, 2), shard(y_up, 2)])
    take_far(3)
    process(shard(y_far, 3))
    take_far(2)
    process(shard(y_far, 2))

    rest_t = jnp.concatenate([xbuf[b, 256:272, :].astype(F32)[:8] for b in range(16)], axis=0)
    rest_x = jnp.transpose(rest_t)
    re, im = rest_x[:NIMG], rest_x[NIMG:]
    shrest[0, 0:NIMG, :] = re.astype(BF16)
    shrest[1, 0:NIMG, :] = im.astype(BF16)
    for s in range(1, NSHIFT):
        rows = slice(s * NIMG, s * NIMG + NIMG)
        cosine = crest[s - 1 : s, :]
        sine = srest[s - 1 : s, :]
        shrest[0, rows, :] = (re * cosine + im * sine).astype(BF16)
        shrest[1, rows, :] = (im * cosine - re * sine).astype(BF16)
    full = (
        score[...]
        + lax.dot_general(shrest[0], prest[0], NT, preferred_element_type=F32)
        + lax.dot_general(shrest[1], prest[1], NT, preferred_element_type=F32)
    )
    full = jnp.concatenate([full, jnp.zeros((ROWS, 128 - NPROJ), F32)], axis=1)

    tiles = []
    for t in range(5):
        if t < 4:
            tiles.append(jnp.transpose(full[t * 128 : t * 128 + 128])[:NPROJ] + base)
        else:
            last = jnp.concatenate([full[512:576], jnp.zeros((64, 128), F32)], axis=0)
            tiles.append(jnp.where(lane < 64, jnp.transpose(last)[:NPROJ] + base, -3e38))
    high = tiles[0]
    for t in range(1, 5):
        high = jnp.maximum(high, tiles[t])
    high = jnp.max(high, axis=0, keepdims=True)
    high = jnp.maximum(high, pltpu.roll(jnp.broadcast_to(high, (8, 128)), 64, 1)[:1])
    total = jnp.exp(tiles[0] - high)
    for t in range(1, 5):
        total += jnp.exp(tiles[t] - high)
    total = jnp.sum(total, axis=0, keepdims=True)
    total = total + pltpu.roll(jnp.broadcast_to(total, (8, 128)), 64, 1)[:1]
    row8 = lax.broadcasted_iota(jnp.int32, (8, 128), 0)

    def merged(blocks):
        top = blocks[0][0:1, :]
        for block in blocks[1:]:
            top = jnp.maximum(top, block[0:1, :])
        whole = jnp.zeros((1, 128), F32)
        for block in blocks:
            whole += block[1:2, :] * jnp.exp(block[0:1, :] - top)
        return top, whole

    st_copies = []
    for stage in range(2):
        mine_at = l if stage == 0 else y
        stat[stage, mine_at] = jnp.where(row8 == 0, high, total)
        for k in range(1, 4):
            to = y * 4 + lax.rem(l + k, 4) if stage == 0 else lax.rem(ref + 4 * k, 16)
            block = stat.at[stage, mine_at]
            c = copy(block, block, st_s.at[3 * stage + k - 1], st_r.at[3 * stage + k - 1], dev(ref_at=to))
            c.start()
            st_copies.append(c)
        for k in range(1, 4):
            src = lax.rem(mine_at + 4 - k, 4)
            block = stat.at[stage, src]
            come_from = y * 4 + src if stage == 0 else src * 4 + l
            copy(
                block, block, st_s.at[3 * stage + k - 1], st_r.at[3 * stage + k - 1], dev(ref_at=come_from)
            ).wait_recv()
        high, total = merged([stat[stage, b] for b in range(4)])
    evidence = high + jnp.log(total)
    ev_ref[...] = evidence
    for t in range(5):
        w = jnp.exp(tiles[t] - evidence).astype(BF16)
        if t < 4:
            wts[:, t * 128 : t * 128 + 128] = w
        else:
            wts[:, 512:576] = w[:, :64]
    members_all = jnp.concatenate([members.astype(BF16)] * 4 + [members[:, :64].astype(BF16)], axis=1)
    group_sum = lax.dot_general(members_all, wts[...], NT, preferred_element_type=F32)
    group_sum = jnp.concatenate([group_sum, jnp.zeros((GROUPS, 80), F32)], axis=1)

    other = at_img(x, h, o)
    rest_out[0:48, :] = jnp.dot(wts[...], shrest[o], preferred_element_type=F32).astype(BF16)
    rest_out[48:64, :] = group_sum.astype(BF16)
    rest_copy = copy(rest_out, rest_in, co_s.at[4], co_r.at[4], other)
    rest_copy.start()

    order = [ring(x + 2), ring(x + 1), ring(x + 3), x]
    runs = [ring(h + 2), ring(h + 1), ring(h + 3), h]

    def core_copy(i):
        return copy(core_out.at[i], core_in.at[i], co_s.at[i], co_r.at[i], other)

    def other_chunk(i):
        for u in range(4):
            got = jnp.dot(wts[...], smain[4 * order[i] + runs[u], o], preferred_element_type=F32)
            for v in range(2):
                r = PIECE * (2 * u + v)
                core_out[i, r : r + PIECE, :] = got[:, v * 128 : v * 128 + 128].astype(BF16)
        core_copy(i).start()

    other_chunk(0)
    other_chunk(1)

    rest_sum = jnp.dot(wts[...], shrest[d], preferred_element_type=F32)
    rest_copy.wait_recv()
    rest_sum = rest_sum + rest_in[0:48, :].astype(F32)
    group_sum = group_sum + rest_in[48:64, :].astype(F32)

    def left(value, by):
        return pltpu.roll(value, lax.rem(256 - by, 128), 1)

    group_half = left(group_sum, 32 + 24 * d)

    def packed(q):
        out = left(rest_sum[0:16], 32 * q)
        out = jnp.where(lane < 32, out, left(rest_sum[16:32], 32 * q - 32))
        out = jnp.where(lane < 64, out, left(rest_sum[32:48], 32 * q - 64))
        return jnp.where(lane < 96, out, group_half)

    def piece_row(k):
        return 16 + PIECE * k

    def own_chunk(i, store):
        q = order[i]
        core_copy(i).wait_recv()
        for u in range(4):
            got = jnp.dot(wts[...], smain[4 * q + runs[u], d], preferred_element_type=F32)
            for v in range(2):
                k = 2 * u + v
                r = PIECE * k
                store(k, got[:, v * 128 : v * 128 + 128] + core_in[i, r : r + PIECE, :].astype(F32))
        store(-1, packed(q))

    x_up, x_down = at_img(ring(x + 1), h, d), at_img(ring(x - 1), h, d)

    def rows_of(k):
        return slice(0, 16) if k < 0 else slice(piece_row(k), piece_row(k) + PIECE)

    def store_far(k, value):
        x_out[0, rows_of(k), :] = value.astype(BF16)

    own_chunk(0, store_far)
    near_a = copy(x_out.at[0, pl.ds(0, HALF)], x_near_a, xs_s.at[0], xs_r.at[0], x_up)
    near_b = copy(x_out.at[0, pl.ds(HALF, MSG - HALF)], x_near_b, xs_s.at[1], xs_r.at[1], x_down)
    near_a.start()
    near_b.start()

    def store_up(k, value):
        held[rows_of(k), :] = value

    def x_copy(way, part):
        rows = pl.ds(0, FIRST) if part == 0 else pl.ds(FIRST, MSG - FIRST)
        k = 2 + 2 * way + part
        to = x_up if way == 0 else x_down
        return copy(x_out.at[1 + way, rows], x_in.at[way, rows], xs_s.at[k], xs_r.at[k], to)

    other_chunk(2)
    own_chunk(1, store_up)
    x_out[1, HALF:MSG, :] = held[HALF:MSG, :].astype(BF16)
    near_a.wait_recv()
    x_out[1, 0:HALF, :] = (held[0:HALF, :] + x_near_a[...].astype(F32)).astype(BF16)
    x_copy(0, 0).start()
    x_copy(0, 1).start()

    other_chunk(3)
    own_chunk(2, store_up)
    x_out[2, 0:HALF, :] = held[0:HALF, :].astype(BF16)
    x_copy(1, 0).start()
    near_b.wait_recv()
    x_out[2, HALF:MSG, :] = (held[HALF:MSG, :] + x_near_b[...].astype(F32)).astype(BF16)
    x_copy(1, 1).start()

    own_chunk(3, store_up)

    def add_x(part):
        rows = slice(0, FIRST) if part == 0 else slice(FIRST, MSG)
        x_copy(0, part).wait_recv()
        x_copy(1, part).wait_recv()
        held[rows, :] += x_in[0, rows, :].astype(F32) + x_in[1, rows, :].astype(F32)

    add_x(0)

    def piece_of(u, dd):
        return held[pl.ds(pl.multiple_of(16 + PIECE * (2 * u + dd), 16), PIECE), :]

    rest_pack = held[0:16, :]
    h_up, h_down = ring(h + 1), ring(h - 1)

    def fill(slot, value, extra):
        z_out[slot, 0:48, :] = value.astype(BF16)
        z_out[slot, 48:64, :] = extra.astype(BF16)

    fill(0, piece_of(0, 0), rest_pack)
    fill(1, piece_of(0, 1), rest_pack)
    relay_up = copy(z_out.at[0], z_relay.at[0], zs_s.at[0], zs_r.at[0], at_img(x, h_up, d))
    relay_down = copy(z_out.at[1], z_relay.at[1], zs_s.at[1], zs_r.at[1], at_img(x, h_down, d))
    relay_up.start()
    relay_down.start()
    add_x(1)

    def z_copy(slot):
        way, dd = (slot - 2) // 2, (slot - 2) % 2
        to = at_img(x, h_up if way == 0 else h_down, dd)
        return copy(z_out.at[slot], z_in.at[way, d], zs_s.at[slot], zs_r.at[2 + 2 * way + d], to)

    fill(3, piece_of(1, 1), rest_pack)
    z_copy(3).start()
    fill(4, piece_of(2, 0), rest_pack)
    z_copy(4).start()
    fill(6, piece_of(3, o), rest_pack)
    core_last = copy(z_out.at[6], z_core, zs_s.at[6], zs_r.at[6], other)
    core_last.start()
    relay_up.wait_recv()
    fill(
        2,
        piece_of(1, 0) + z_relay[0, 0:48, :].astype(F32),
        rest_pack + z_relay[0, 48:64, :].astype(F32),
    )
    z_copy(2).start()
    relay_down.wait_recv()
    fill(
        5,
        piece_of(2, 1) + z_relay[1, 0:48, :].astype(F32),
        rest_pack + z_relay[1, 48:64, :].astype(F32),
    )
    z_copy(5).start()

    mine = jnp.concatenate([piece_of(3, d), rest_pack], axis=0)
    core_last.wait_recv()
    theirs = z_core[...].astype(F32)
    for way in range(2):
        for c in range(2):
            slot = z_in.at[way, c]
            copy(slot, slot, zs_s.at[2], zs_r.at[2 + 2 * way + c], other).wait_recv()
    local = 2 * h + d
    packs = []
    for c in range(2):
        both = jnp.where(d == c, mine, theirs)
        both = both + z_in[0, c].astype(F32) + z_in[1, c].astype(F32)
        cls_ref[c, :, 0:128] = both[0:48]
        pack = both[48:64]
        packs.append(pack)
        for a in range(3):
            cls_ref[c, 16 * a : 16 * a + 16, 128:256] = left(pack, 32 * a + 4 * local)
    group_all = jnp.where(lane < 24, left(packs[0], 96), left(packs[1], 72))
    group_all = jnp.where(lane < 48, group_all, 0.0)
    span = pl.ds(pl.multiple_of(img * 128, 128), 256)
    turn = lax.rem(256 - 4 * img, 256)
    curve = curve_ref[:, span]
    gain = pltpu.roll(curve * curve * noise_row(img, 2), turn, 1)
    contrast = lax.dot_general(
        jnp.transpose(jnp.concatenate([group_all, jnp.zeros((112, 128), F32)], axis=0))[:NPROJ, :GROUPS],
        gain,
        (((1,), (0,)), ((), ())),
        precision=HIGHEST,
        preferred_element_type=F32,
    )
    con_ref[...] = contrast

    for e in range(4):
        for part in range(2):
            if e:
                z_send(e, part).wait_send()
            for way in range(2):
                y_copy(way, e, y, part).wait_send()
        for way in range(2):
            f_copy(way, e, y).wait_send()
    for c in st_copies:
        c.wait_send()
    for i in range(4):
        core_copy(i).wait_send()
    for c in (rest_copy, near_a, near_b, relay_up, relay_down, core_last):
        c.wait_send()
    for way in range(2):
        for part in range(2):
            x_copy(way, part).wait_send()
    for slot in range(2, 6):
        z_copy(slot).wait_send()


def on_device(
    images, projections, contrast_curve, noise_weight, defocus_group, shifts, orient_index, orient_prior
):
    rows = jnp.pad(images.transpose(1, 0, 2).reshape(2 * NIMG, 264), ((0, 0), (0, 120)))
    vmem = pl.BlockSpec(memory_space=pltpu.VMEM)
    sem = pltpu.SemaphoreType.DMA
    cls, con, ev = pl.pallas_call(
        body,
        out_shape=(
            jax.ShapeDtypeStruct((2, NPROJ, 256), F32),
            jax.ShapeDtypeStruct((NPROJ, 256), F32),
            jax.ShapeDtypeStruct((1, 128), F32),
        ),
        in_specs=[vmem, vmem, vmem, vmem, vmem, pl.BlockSpec(memory_space=pltpu.SMEM), vmem, vmem],
        out_specs=(vmem, vmem, vmem),
        scratch_shapes=[
            pltpu.VMEM((16, SHARD, 128), BF16),
            pltpu.VMEM((16, 2, NPROJ, 256), BF16),
            pltpu.VMEM((2, NPROJ, 128), BF16),
            pltpu.VMEM((16, 8, 256), F32),
            pltpu.VMEM((16, 8, 256), F32),
            pltpu.VMEM((8, 128), F32),
            pltpu.VMEM((8, 128), F32),
            pltpu.VMEM((16, 2, ROWS, 256), BF16),
            pltpu.VMEM((2, ROWS, 128), BF16),
            pltpu.VMEM((ROWS, NPROJ), F32),
            pltpu.VMEM((NPROJ, ROWS), BF16),
            pltpu.VMEM((2, 4, 8, 128), F32),
            pltpu.VMEM((4, 8 * PIECE, 128), BF16),
            pltpu.VMEM((4, 8 * PIECE, 128), BF16),
            pltpu.VMEM((64, 128), BF16),
            pltpu.VMEM((64, 128), BF16),
            pltpu.VMEM((3, MSG, 128), BF16),
            pltpu.VMEM((HALF, 128), BF16),
            pltpu.VMEM((MSG - HALF, 128), BF16),
            pltpu.VMEM((2, MSG, 128), BF16),
            pltpu.VMEM((MSG, 128), F32),
            pltpu.VMEM((7, 64, 128), BF16),
            pltpu.VMEM((2, 64, 128), BF16),
            pltpu.VMEM((2, 2, 64, 128), BF16),
            pltpu.VMEM((64, 128), BF16),
            sem((4, 2)),
            sem((4, 2)),
            sem((2, 4, 2)),
            sem((2, 4, 2)),
            sem((2, 4)),
            sem((2, 4)),
            sem((6,)),
            sem((6,)),
            sem((5,)),
            sem((5,)),
            sem((6,)),
            sem((6,)),
            sem((7,)),
            sem((7,)),
        ],
        compiler_params=pltpu.CompilerParams(
            collective_id=0, has_side_effects=True, vmem_limit_bytes=40 * 1024 * 1024
        ),
        name="expectation",
    )(
        rows,
        projections.transpose(1, 0, 2),
        contrast_curve,
        noise_weight.reshape(NPIX // 128, 128),
        defocus_group.reshape(1, NIMG),
        shifts.T,
        orient_index.reshape(1, NPROJ),
        orient_prior.reshape(2, 128),
    )
    return cls[:, :, :132].transpose(1, 0, 2), con[:, :132], ev[0, :NIMG]


def solution(mesh):
    in_specs = (P("img", None, "ref"), P("ref", None, None), P(), P(), P("img"), P(), P("ref"), P())
    out_specs = (P("ref", None, "img"), P("ref", "img"), P("img"))
    return jax.shard_map(
        on_device, mesh=mesh, in_specs=in_specs, out_specs=out_specs, check_vma=False
    )
```

```python
import math

import jax
import jax.numpy as jnp
from jax import lax
from jax.experimental import pallas as pl
from jax.experimental.pallas import tpu as pltpu
from jax.sharding import PartitionSpec as P

MESH = pl.DeviceIdType.MESH
F32 = jnp.float32
BF16 = jnp.bfloat16
HIGHEST = lax.Precision.HIGHEST
NT = (((1,), (1,)), ((), ()))
TN = (((0,), (0,)), ((), ()))

NPIX = 4224
BOX = 128
NSHIFT = 9
NIMG = 64
NPROJ = 48
GROUPS = 16
ROWS = NSHIFT * NIMG
SHARD = 272
PIECE = 48
MSG = 400
HALF = 208
FIRST = 112


def sincos(steps):
    quadrant = lax.shift_right_arithmetic(steps + 16, 5)
    rest = (steps - quadrant * 32).astype(F32) * (2.0 * math.pi / BOX)
    sq = rest * rest
    sin_part = rest * (
        1.0 + sq * (-1.0 / 6 + sq * (1.0 / 120 + sq * (-1.0 / 5040 + sq * (1.0 / 362880))))
    )
    cos_part = 1.0 + sq * (
        -0.5 + sq * (1.0 / 24 + sq * (-1.0 / 720 + sq * (1.0 / 40320 - sq * (1.0 / 3628800))))
    )
    odd = (quadrant & 1) == 1
    flip_sin = (quadrant & 2) == 2
    flip_cos = ((quadrant + 1) & 2) == 2
    sine = jnp.where(odd, cos_part, sin_part)
    cosine = jnp.where(odd, sin_part, cos_part)
    return jnp.where(flip_cos, -cosine, cosine), jnp.where(flip_sin, -sine, sine)


def body(
    img_ref,
    proj_ref,
    curve_ref,
    noise_ref,
    group_ref,
    shift_ref,
    orient_ref,
    prior_ref,
    cls_ref,
    con_ref,
    ev_ref,
    xbuf,
    pmain,
    prest,
    ctab,
    stab,
    crest,
    srest,
    smain,
    shrest,
    score,
    wts,
    stat,
    core_out,
    core_in,
    rest_out,
    rest_in,
    far_out,
    x_out,
    x_near_a,
    x_near_b,
    x_in,
    held,
    z_out,
    z_relay,
    z_in,
    z_core,
    ag_z_s,
    ag_z_r,
    ag_y_s,
    ag_y_r,
    ag_f_s,
    ag_f_r,
    st_s,
    st_r,
    co_s,
    co_r,
    xs_s,
    xs_r,
    zs_s,
    zs_r,
):
    img = lax.axis_index("img")
    ref = lax.axis_index("ref")
    x = lax.div(img, 8)
    h = lax.rem(lax.div(img, 2), 4)
    d = lax.rem(img, 2)
    o = 1 - d
    y = lax.div(ref, 4)
    l = lax.rem(ref, 4)

    def ring(v):
        return lax.rem(v + 4, 4)

    def dev(img_at=img, ref_at=ref):
        return {"img": img_at, "ref": ref_at}

    def at_img(xx, hh, dd):
        return dev(img_at=(xx * 4 + hh) * 2 + dd)

    def copy(src, dst, send, recv, to):
        return pltpu.make_async_remote_copy(
            src_ref=src, dst_ref=dst, send_sem=send, recv_sem=recv, device_id=to, device_id_type=MESH
        )

    barrier = pltpu.get_barrier_semaphore()
    peers = [dev(ref_at=y * 4 + lax.rem(l + k, 4)) for k in range(1, 4)]
    peers += [dev(ref_at=lax.rem(ref + 4 * k, 16)) for k in range(1, 4)]
    peers += [at_img(x, h, o), at_img(ring(x + 1), h, d), at_img(ring(x - 1), h, d)]
    peers += [at_img(ring(x + 1), h, o), at_img(ring(x - 1), h, o)]
    for hh in (ring(h + 1), ring(h - 1)):
        peers += [at_img(x, hh, d), at_img(x, hh, o)]
    for peer in peers:
        pl.semaphore_signal(barrier, inc=1, device_id=peer, device_id_type=MESH)

    lane = lax.broadcasted_iota(jnp.int32, (1, 128), 1)

    def noise_row(tile, count):
        return jnp.concatenate([noise_ref[pl.ds(tile + t, 1), :] for t in range(count)], axis=1)


    group_row = group_ref[...].astype(F32)
    group_row = jnp.concatenate([group_row, group_row], axis=1)
    group_col = jnp.transpose(jnp.broadcast_to(group_row, (128, 128)))[:NIMG, :]
    start = pl.multiple_of(ref * 256, 128)
    turn = lax.rem(384 - 8 * ref, 384)
    curve_here = pltpu.roll(curve_ref[:, pl.ds(start, 384)], turn, 1)
    noise_here = pltpu.roll(jnp.broadcast_to(noise_row(2 * ref, 3), (8, 384)), turn, 1)[:1, :]
    parts = []
    for tile in range(3):
        span = slice(tile * 128, tile * 128 + 128)
        gain = jnp.zeros((NIMG, 128), F32)
        for g in range(GROUPS):
            gain = jnp.where(group_col == float(g), curve_here[g : g + 1, span], gain)
        gain = gain * noise_here[:, span]
        parts.append(img_ref[:, span].astype(F32) * jnp.concatenate([gain, gain], axis=0))
    second = pltpu.roll(jnp.concatenate(parts[1:], axis=1), 252, 1)[:, :128]
    rest = jnp.transpose(jnp.where(lane < 4, parts[1], parts[2]))[:16, :]
    row16 = lax.broadcasted_iota(jnp.int32, (16, 128), 0)
    rest = jnp.where(row16 < 8, rest, 0.0)
    xbuf[ref, 0:128, :] = parts[0].astype(BF16)
    xbuf[ref, 128:256, :] = second.astype(BF16)
    xbuf[ref, 256:272, :] = rest.astype(BF16)

    pl.semaphore_wait(barrier, len(peers))

    columns = [lax.rem(l + 4 - e, 4) for e in range(4)]
    halves = (pl.ds(0, 144), pl.ds(144, 128))

    def shard(yy, e):
        return yy * 4 + columns[e]

    def z_send(e, part):
        block = xbuf.at[ref, halves[part]]
        to = dev(ref_at=y * 4 + lax.rem(l + e, 4))
        return copy(block, block, ag_z_s.at[e, part], ag_z_r.at[e, part], to)

    y_up, y_down, y_far = ring(y + 1), ring(y - 1), ring(y + 2)

    def y_copy(way, e, src_y, part):
        to = dev(ref_at=(y_up if way == 0 else y_down) * 4 + l)
        block = xbuf.at[shard(src_y, e), halves[part]]
        return copy(block, block, ag_y_s.at[way, e, part], ag_y_r.at[way, e, part], to)

    def f_copy(way, e, src_y):
        to = dev(ref_at=(y_up if way == 0 else y_down) * 4 + l)
        block = xbuf.at[shard(src_y, e), halves[way]]
        return copy(block, block, ag_f_s.at[way, e], ag_f_r.at[way, e], to)

    def send_y(e, part):
        for way in (part, 1 - part):
            y_copy(way, e, y, part).start()

    z_send(1, 0).start()
    z_send(3, 0).start()
    send_y(0, 0)
    send_y(0, 1)
    z_send(1, 1).start()
    z_send(3, 1).start()
    z_send(2, 0).start()
    z_send(2, 1).start()

    def take_z(e):
        for part in range(2):
            block = xbuf.at[shard(y, e), halves[part]]
            copy(block, block, ag_z_s.at[e, part], ag_z_r.at[e, part], dev(ref_at=shard(y, e))).wait_recv()
            send_y(e, part)

    def take_y(e):
        y_copy(0, e, y_down, 0).wait_recv()
        f_copy(0, e, y_down).start()
        y_copy(1, e, y_up, 1).wait_recv()
        f_copy(1, e, y_up).start()
        y_copy(0, e, y_down, 1).wait_recv()
        y_copy(1, e, y_up, 0).wait_recv()

    def take_far(e):
        f_copy(0, e, y_far).wait_recv()
        f_copy(1, e, y_far).wait_recv()

    def table(pixel, width):
        srow = lax.broadcasted_iota(jnp.int32, (8, width), 0) + 1
        move_x = jnp.zeros((8, width), jnp.int32)
        move_y = jnp.zeros((8, width), jnp.int32)
        for s in range(1, NSHIFT):
            move_x = jnp.where(srow == s, shift_ref[0, s], move_x)
            move_y = jnp.where(srow == s, shift_ref[1, s], move_y)
        freq_x = pixel & (BOX // 2 - 1)
        freq_y = lax.shift_right_logical(pixel, 6) - NPIX // BOX
        return sincos((move_x * freq_x + move_y * freq_y) & (BOX - 1))

    def table_step(b, carry):
        at = lax.broadcasted_iota(jnp.int32, (8, 256), 1)
        pixel = 264 * b + at + jnp.where(at >= 128, 4, 0)
        cosine, sine = table(pixel, 256)
        ctab[b] = cosine
        stab[b] = sine
        return carry

    lax.fori_loop(0, 16, table_step, 0)
    at = lax.broadcasted_iota(jnp.int32, (8, 128), 1)
    cosine, sine = table(132 * lax.shift_right_logical(at, 2) + 128 + (at & 3), 128)
    crest[...] = cosine
    srest[...] = sine

    def proj_step(b, carry):
        out = []
        for c in range(2):
            kept = carry[c]
            for u in range(2):
                n = 2 * b + u
                window = proj_ref[c, :, pl.ds(pl.multiple_of(n * 128, 128), 256)].astype(F32)
                turned = pltpu.roll(window, lax.rem(256 - 4 * n, 256), 1)
                pmain[b, c, :, u * 128 : u * 128 + 128] = turned[:, :128].astype(BF16)
                kept = jnp.where(lax.shift_right_logical(lane, 2) == n, window[:, 128:], kept)
            out.append(kept)
        return tuple(out)

    zero_rest = jnp.zeros((NPROJ, 128), F32)
    rests = lax.fori_loop(0, 16, proj_step, (zero_rest, zero_rest))
    for c in range(2):
        prest[c] = rests[c].astype(BF16)

    take_y(0)
    take_z(1)
    take_z(3)

    def norm_step(t, total):
        span = pl.ds(pl.multiple_of(t * 384, 128), 384)
        re = proj_ref[0, :, span].astype(F32)
        im = proj_ref[1, :, span].astype(F32)
        curve = curve_ref[:, span]
        gain = 0.5 * (curve * curve * noise_row(3 * t, 3))
        power = re * re + im * im
        return total + lax.dot_general(
            two_parts(power), two_parts(gain), NT, preferred_element_type=F32
        )

    def two_parts(value):
        high = value.astype(BF16)
        return jnp.concatenate([high, (value - high.astype(F32)).astype(BF16)], axis=0)

    norm = lax.fori_loop(0, 11, norm_step, jnp.zeros((2 * NPROJ, 2 * GROUPS), F32))
    norm = norm[:NPROJ] + norm[NPROJ:]
    norm = norm[:, :GROUPS] + norm[:, GROUPS:]
    grow = lax.broadcasted_iota(jnp.int32, (GROUPS, 128), 0)
    members = (group_row == grow.astype(F32)).astype(F32)
    penalty = jnp.dot(norm, members, precision=HIGHEST, preferred_element_type=F32)
    orient_row = jnp.concatenate([orient_ref[...].astype(F32), jnp.zeros((1, 80), F32)], axis=1)
    orient_col = jnp.transpose(jnp.broadcast_to(orient_row, (128, 128)))[:NPROJ, :]
    prior = jnp.zeros((NPROJ, 1), F32)
    for half in range(2):
        hit = orient_col == (lane + half * 128).astype(F32)
        prior += jnp.sum(
            jnp.where(hit, prior_ref[half : half + 1, :], 0.0), axis=1, keepdims=True
        )
    base = prior - penalty

    score[...] = jnp.zeros_like(score)

    def process(b):
        for t in range(2):
            span = slice(t * 128, t * 128 + 128)
            re = xbuf[b, t * 128 : t * 128 + 64, :]
            im = xbuf[b, t * 128 + 64 : t * 128 + 128, :]
            smain[b, 0, 0:NIMG, span] = re
            smain[b, 1, 0:NIMG, span] = im
            re = re.astype(F32)
            im = im.astype(F32)
            for s in range(1, NSHIFT):
                rows = slice(s * NIMG, s * NIMG + NIMG)
                cosine = ctab[b, s - 1 : s, span]
                sine = stab[b, s - 1 : s, span]
                smain[b, 0, rows, span] = (re * cosine + im * sine).astype(BF16)
                smain[b, 1, rows, span] = (im * cosine - re * sine).astype(BF16)
        score[...] += lax.dot_general(
            smain[b, 0], pmain[b, 0], NT, preferred_element_type=F32
        ) + lax.dot_general(smain[b, 1], pmain[b, 1], NT, preferred_element_type=F32)

    def process_all(blocks):
        def step(t, carry):
            b = blocks[0]
            for k in range(1, len(blocks)):
                b = jnp.where(t == k, blocks[k], b)
            process(b)
            return carry

        lax.fori_loop(0, len(blocks), step, 0)

    process(shard(y, 0))
    take_z(2)
    take_y(1)
    process_all([shard(y, 1), shard(y_down, 0), shard(y_up, 0)])
    take_y(3)
    take_far(0)
    process_all([shard(y, 3), shard(y_down, 1), shard(y_up, 1), shard(y_far, 0)])
    take_y(2)
    take_far(1)
    process_all([shard(y, 2), shard(y_down, 3), shard(y_up, 3), shard(y_far, 1)])
    process_all([shard(y_down, 2), shard(y_up, 2)])
    take_far(3)
    process(shard(y_far, 3))
    take_far(2)
    process(shard(y_far, 2))

    rest_t = jnp.concatenate([xbuf[b, 256:272, :].astype(F32)[:8] for b in range(16)], axis=0)
    rest_x = jnp.transpose(rest_t)
    re, im = rest_x[:NIMG], rest_x[NIMG:]
    shrest[0, 0:NIMG, :] = re.astype(BF16)
    shrest[1, 0:NIMG, :] = im.astype(BF16)
    for s in range(1, NSHIFT):
        rows = slice(s * NIMG, s * NIMG + NIMG)
        cosine = crest[s - 1 : s, :]
        sine = srest[s - 1 : s, :]
        shrest[0, rows, :] = (re * cosine + im * sine).astype(BF16)
        shrest[1, rows, :] = (im * cosine - re * sine).astype(BF16)
    full = (
        score[...]
        + lax.dot_general(shrest[0], prest[0], NT, preferred_element_type=F32)
        + lax.dot_general(shrest[1], prest[1], NT, preferred_element_type=F32)
    )
    full = jnp.concatenate([full, jnp.zeros((ROWS, 128 - NPROJ), F32)], axis=1)

    tiles = []
    for t in range(5):
        if t < 4:
            tiles.append(jnp.transpose(full[t * 128 : t * 128 + 128])[:NPROJ] + base)
        else:
            last = jnp.concatenate([full[512:576], jnp.zeros((64, 128), F32)], axis=0)
            tiles.append(jnp.where(lane < 64, jnp.transpose(last)[:NPROJ] + base, -3e38))
    high = tiles[0]
    for t in range(1, 5):
        high = jnp.maximum(high, tiles[t])
    high = jnp.max(high, axis=0, keepdims=True)
    high = jnp.maximum(high, pltpu.roll(jnp.broadcast_to(high, (8, 128)), 64, 1)[:1])
    total = jnp.exp(tiles[0] - high)
    for t in range(1, 5):
        total += jnp.exp(tiles[t] - high)
    total = jnp.sum(total, axis=0, keepdims=True)
    total = total + pltpu.roll(jnp.broadcast_to(total, (8, 128)), 64, 1)[:1]
    row8 = lax.broadcasted_iota(jnp.int32, (8, 128), 0)

    def merged(blocks):
        top = blocks[0][0:1, :]
        for block in blocks[1:]:
            top = jnp.maximum(top, block[0:1, :])
        whole = jnp.zeros((1, 128), F32)
        for block in blocks:
            whole += block[1:2, :] * jnp.exp(block[0:1, :] - top)
        return top, whole

    st_copies = []
    for stage in range(2):
        mine_at = l if stage == 0 else y
        stat[stage, mine_at] = jnp.where(row8 == 0, high, total)
        for k in range(1, 4):
            to = y * 4 + lax.rem(l + k, 4) if stage == 0 else lax.rem(ref + 4 * k, 16)
            block = stat.at[stage, mine_at]
            c = copy(block, block, st_s.at[3 * stage + k - 1], st_r.at[3 * stage + k - 1], dev(ref_at=to))
            c.start()
            st_copies.append(c)
        for k in range(1, 4):
            src = lax.rem(mine_at + 4 - k, 4)
            block = stat.at[stage, src]
            come_from = y * 4 + src if stage == 0 else src * 4 + l
            copy(
                block, block, st_s.at[3 * stage + k - 1], st_r.at[3 * stage + k - 1], dev(ref_at=come_from)
            ).wait_recv()
        high, total = merged([stat[stage, b] for b in range(4)])
    evidence = high + jnp.log(total)
    ev_ref[...] = evidence
    for t in range(5):
        w = jnp.exp(tiles[t] - evidence).astype(BF16)
        if t < 4:
            wts[:, t * 128 : t * 128 + 128] = w
        else:
            wts[:, 512:576] = w[:, :64]
    members_all = jnp.concatenate([members.astype(BF16)] * 4 + [members[:, :64].astype(BF16)], axis=1)
    group_sum = lax.dot_general(members_all, wts[...], NT, preferred_element_type=F32)
    group_sum = jnp.concatenate([group_sum, jnp.zeros((GROUPS, 80), F32)], axis=1)

    other = at_img(x, h, o)
    rest_mine = jnp.dot(wts[...], shrest[d], preferred_element_type=F32)
    rest_theirs = jnp.dot(wts[...], shrest[o], preferred_element_type=F32)

    order = [ring(x + 2), ring(x + 1), ring(x + 3), x]
    runs = [ring(h + 2), ring(h + 1), ring(h + 3), h]

    def core_copy(i):
        return copy(core_out.at[i], core_in.at[i], co_s.at[i], co_r.at[i], other)

    def other_chunk(i):
        for u in range(4):
            got = jnp.dot(wts[...], smain[4 * order[i] + runs[u], o], preferred_element_type=F32)
            for v in range(2):
                r = PIECE * (2 * u + v)
                core_out[i, r : r + PIECE, :] = got[:, v * 128 : v * 128 + 128].astype(BF16)
        core_copy(i).start()

    def left(value, by):
        return pltpu.roll(value, lax.rem(256 - by, 128), 1)

    def packed(q, rest_tile, group_tile, c):
        out = left(rest_tile[0:16], 32 * q)
        out = jnp.where(lane < 32, out, left(rest_tile[16:32], 32 * q - 32))
        out = jnp.where(lane < 64, out, left(rest_tile[32:48], 32 * q - 64))
        return jnp.where(lane < 96, out, left(group_tile, 32 + 24 * c))

    def piece_row(k):
        return 16 + PIECE * k

    def rows_of(k):
        return slice(0, 16) if k < 0 else slice(piece_row(k), piece_row(k) + PIECE)

    far_copies = []
    for k in range(2):
        c = d if k == 0 else o
        for u in range(4):
            got = jnp.dot(wts[...], smain[4 * order[0] + runs[u], c], preferred_element_type=F32).astype(BF16)
            for v in range(2):
                far_out[k, rows_of(2 * u + v), :] = got[:, v * 128 : v * 128 + 128]
        rest_tile = rest_mine if k == 0 else rest_theirs
        far_out[k, 0:16, :] = packed(order[0], rest_tile, group_sum, c).astype(BF16)
        for way in range(2):
            rows = pl.ds(0, HALF) if way == 0 else pl.ds(HALF, MSG - HALF)
            land = x_near_a if way == 0 else x_near_b
            to = at_img(ring(x + 1) if way == 0 else ring(x - 1), h, c)
            far_copies.append(
                copy(far_out.at[k, rows], land.at[k], xs_s.at[2 * way + k], xs_r.at[2 * way + k], to)
            )
            far_copies[-1].start()

    rest_out[0:48, :] = rest_theirs.astype(BF16)
    rest_out[48:64, :] = group_sum.astype(BF16)
    rest_copy = copy(rest_out, rest_in, co_s.at[4], co_r.at[4], other)
    rest_copy.start()
    for i in range(1, 4):
        other_chunk(i)

    rest_copy.wait_recv()
    rest_sum = rest_mine + rest_in[0:48, :].astype(F32)
    group_sum = group_sum + rest_in[48:64, :].astype(F32)

    def own_chunk(i):
        q = order[i]
        sums = [
            jnp.dot(wts[...], smain[4 * q + runs[u], d], preferred_element_type=F32) for u in range(4)
        ]
        core_copy(i).wait_recv()
        for u in range(4):
            for v in range(2):
                k = 2 * u + v
                r = PIECE * k
                held[rows_of(k), :] = (
                    sums[u][:, v * 128 : v * 128 + 128] + core_in[i, r : r + PIECE, :].astype(F32)
                )
        held[0:16, :] = packed(q, rest_sum, group_sum, d)

    x_up, x_down = at_img(ring(x + 1), h, d), at_img(ring(x - 1), h, d)

    def near_wait(way):
        for k in range(2):
            far_copies[2 * k + way].wait_recv()

    def x_copy(way, part):
        rows = pl.ds(0, FIRST) if part == 0 else pl.ds(FIRST, MSG - FIRST)
        k = 4 + 2 * way + part
        to = x_up if way == 0 else x_down
        return copy(x_out.at[way, rows], x_in.at[way, rows], xs_s.at[k], xs_r.at[k], to)

    own_chunk(1)
    x_out[0, HALF:MSG, :] = held[HALF:MSG, :].astype(BF16)
    near_wait(0)
    x_out[0, 0:HALF, :] = (
        held[0:HALF, :] + x_near_a[0].astype(F32) + x_near_a[1].astype(F32)
    ).astype(BF16)
    x_copy(0, 0).start()
    x_copy(0, 1).start()

    own_chunk(2)
    x_out[1, 0:HALF, :] = held[0:HALF, :].astype(BF16)
    x_copy(1, 0).start()
    near_wait(1)
    x_out[1, HALF:MSG, :] = (
        held[HALF:MSG, :] + x_near_b[0].astype(F32) + x_near_b[1].astype(F32)
    ).astype(BF16)
    x_copy(1, 1).start()

    own_chunk(3)

    def add_x(part):
        rows = slice(0, FIRST) if part == 0 else slice(FIRST, MSG)
        x_copy(0, part).wait_recv()
        x_copy(1, part).wait_recv()
        held[rows, :] += x_in[0, rows, :].astype(F32) + x_in[1, rows, :].astype(F32)

    add_x(0)

    def piece_of(u, dd):
        return held[pl.ds(pl.multiple_of(16 + PIECE * (2 * u + dd), 16), PIECE), :]

    rest_pack = held[0:16, :]
    h_up, h_down = ring(h + 1), ring(h - 1)

    def fill(slot, value, extra):
        z_out[slot, 0:48, :] = value.astype(BF16)
        z_out[slot, 48:64, :] = extra.astype(BF16)

    fill(0, piece_of(0, 0), rest_pack)
    fill(1, piece_of(0, 1), rest_pack)
    relay_up = copy(z_out.at[0], z_relay.at[0], zs_s.at[0], zs_r.at[0], at_img(x, h_up, d))
    relay_down = copy(z_out.at[1], z_relay.at[1], zs_s.at[1], zs_r.at[1], at_img(x, h_down, d))
    relay_up.start()
    relay_down.start()
    add_x(1)

    def z_copy(slot):
        way, dd = (slot - 2) // 2, (slot - 2) % 2
        to = at_img(x, h_up if way == 0 else h_down, dd)
        return copy(z_out.at[slot], z_in.at[way, d], zs_s.at[slot], zs_r.at[2 + 2 * way + d], to)

    fill(3, piece_of(1, 1), rest_pack)
    z_copy(3).start()
    fill(4, piece_of(2, 0), rest_pack)
    z_copy(4).start()
    fill(6, piece_of(3, o), rest_pack)
    core_last = copy(z_out.at[6], z_core, zs_s.at[6], zs_r.at[6], other)
    core_last.start()
    relay_up.wait_recv()
    fill(
        2,
        piece_of(1, 0) + z_relay[0, 0:48, :].astype(F32),
        rest_pack + z_relay[0, 48:64, :].astype(F32),
    )
    z_copy(2).start()
    relay_down.wait_recv()
    fill(
        5,
        piece_of(2, 1) + z_relay[1, 0:48, :].astype(F32),
        rest_pack + z_relay[1, 48:64, :].astype(F32),
    )
    z_copy(5).start()

    mine = jnp.concatenate([piece_of(3, d), rest_pack], axis=0)
    core_last.wait_recv()
    theirs = z_core[...].astype(F32)
    for way in range(2):
        for c in range(2):
            slot = z_in.at[way, c]
            copy(slot, slot, zs_s.at[2], zs_r.at[2 + 2 * way + c], other).wait_recv()
    local = 2 * h + d
    packs = []
    for c in range(2):
        both = jnp.where(d == c, mine, theirs)
        both = both + z_in[0, c].astype(F32) + z_in[1, c].astype(F32)
        cls_ref[c, :, 0:128] = both[0:48]
        pack = both[48:64]
        packs.append(pack)
        for a in range(3):
            cls_ref[c, 16 * a : 16 * a + 16, 128:256] = left(pack, 32 * a + 4 * local)
    group_all = jnp.where(lane < 24, left(packs[0], 96), left(packs[1], 72))
    group_all = jnp.where(lane < 48, group_all, 0.0)
    span = pl.ds(pl.multiple_of(img * 128, 128), 256)
    turn = lax.rem(256 - 4 * img, 256)
    curve = curve_ref[:, span]
    gain = pltpu.roll(curve * curve * noise_row(img, 2), turn, 1)
    contrast = lax.dot_general(
        jnp.transpose(jnp.concatenate([group_all, jnp.zeros((112, 128), F32)], axis=0))[:NPROJ, :GROUPS],
        gain,
        (((1,), (0,)), ((), ())),
        precision=HIGHEST,
        preferred_element_type=F32,
    )
    con_ref[...] = contrast

    for e in range(4):
        for part in range(2):
            if e:
                z_send(e, part).wait_send()
            for way in range(2):
                y_copy(way, e, y, part).wait_send()
        for way in range(2):
            f_copy(way, e, y).wait_send()
    for c in st_copies:
        c.wait_send()
    for i in range(1, 4):
        core_copy(i).wait_send()
    for c in far_copies:
        c.wait_send()
    for c in (rest_copy, relay_up, relay_down, core_last):
        c.wait_send()
    for way in range(2):
        for part in range(2):
            x_copy(way, part).wait_send()
    for slot in range(2, 6):
        z_copy(slot).wait_send()


def on_device(
    images, projections, contrast_curve, noise_weight, defocus_group, shifts, orient_index, orient_prior
):
    rows = jnp.pad(images.transpose(1, 0, 2).reshape(2 * NIMG, 264), ((0, 0), (0, 120)))
    vmem = pl.BlockSpec(memory_space=pltpu.VMEM)
    sem = pltpu.SemaphoreType.DMA
    cls, con, ev = pl.pallas_call(
        body,
        out_shape=(
            jax.ShapeDtypeStruct((2, NPROJ, 256), F32),
            jax.ShapeDtypeStruct((NPROJ, 256), F32),
            jax.ShapeDtypeStruct((1, 128), F32),
        ),
        in_specs=[vmem, vmem, vmem, vmem, vmem, pl.BlockSpec(memory_space=pltpu.SMEM), vmem, vmem],
        out_specs=(vmem, vmem, vmem),
        scratch_shapes=[
            pltpu.VMEM((16, SHARD, 128), BF16),
            pltpu.VMEM((16, 2, NPROJ, 256), BF16),
            pltpu.VMEM((2, NPROJ, 128), BF16),
            pltpu.VMEM((16, 8, 256), F32),
            pltpu.VMEM((16, 8, 256), F32),
            pltpu.VMEM((8, 128), F32),
            pltpu.VMEM((8, 128), F32),
            pltpu.VMEM((16, 2, ROWS, 256), BF16),
            pltpu.VMEM((2, ROWS, 128), BF16),
            pltpu.VMEM((ROWS, NPROJ), F32),
            pltpu.VMEM((NPROJ, ROWS), BF16),
            pltpu.VMEM((2, 4, 8, 128), F32),
            pltpu.VMEM((4, 8 * PIECE, 128), BF16),
            pltpu.VMEM((4, 8 * PIECE, 128), BF16),
            pltpu.VMEM((64, 128), BF16),
            pltpu.VMEM((64, 128), BF16),
            pltpu.VMEM((2, MSG, 128), BF16),
            pltpu.VMEM((2, MSG, 128), BF16),
            pltpu.VMEM((2, HALF, 128), BF16),
            pltpu.VMEM((2, MSG - HALF, 128), BF16),
            pltpu.VMEM((2, MSG, 128), BF16),
            pltpu.VMEM((MSG, 128), F32),
            pltpu.VMEM((7, 64, 128), BF16),
            pltpu.VMEM((2, 64, 128), BF16),
            pltpu.VMEM((2, 2, 64, 128), BF16),
            pltpu.VMEM((64, 128), BF16),
            sem((4, 2)),
            sem((4, 2)),
            sem((2, 4, 2)),
            sem((2, 4, 2)),
            sem((2, 4)),
            sem((2, 4)),
            sem((6,)),
            sem((6,)),
            sem((5,)),
            sem((5,)),
            sem((8,)),
            sem((8,)),
            sem((7,)),
            sem((7,)),
        ],
        compiler_params=pltpu.CompilerParams(
            collective_id=0, has_side_effects=True, vmem_limit_bytes=40 * 1024 * 1024
        ),
        name="expectation",
    )(
        rows,
        projections.transpose(1, 0, 2),
        contrast_curve,
        noise_weight.reshape(NPIX // 128, 128),
        defocus_group.reshape(1, NIMG),
        shifts.T,
        orient_index.reshape(1, NPROJ),
        orient_prior.reshape(2, 128),
    )
    return cls[:, :, :132].transpose(1, 0, 2), con[:, :132], ev[0, :NIMG]


def solution(mesh):
    in_specs = (P("img", None, "ref"), P("ref", None, None), P(), P(), P("img"), P(), P("ref"), P())
    out_specs = (P("ref", None, "img"), P("ref", "img"), P("img"))
    return jax.shard_map(
        on_device, mesh=mesh, in_specs=in_specs, out_specs=out_specs, check_vma=False
    )
```

```python
import math

import jax
import jax.numpy as jnp
from jax import lax
from jax.experimental import pallas as pl
from jax.experimental.pallas import tpu as pltpu
from jax.sharding import PartitionSpec as P

MESH = pl.DeviceIdType.MESH
F32 = jnp.float32
BF16 = jnp.bfloat16
HIGHEST = lax.Precision.HIGHEST
NT = (((1,), (1,)), ((), ()))
TN = (((0,), (0,)), ((), ()))

NPIX = 4224
BOX = 128
NSHIFT = 9
NIMG = 64
NPROJ = 48
GROUPS = 16
ROWS = NSHIFT * NIMG
SHARD = 272
PIECE = 48
MSG = 400
HALF = 208
FIRST = 112


def sincos(steps):
    quadrant = lax.shift_right_arithmetic(steps + 16, 5)
    rest = (steps - quadrant * 32).astype(F32) * (2.0 * math.pi / BOX)
    sq = rest * rest
    sin_part = rest * (
        1.0 + sq * (-1.0 / 6 + sq * (1.0 / 120 + sq * (-1.0 / 5040 + sq * (1.0 / 362880))))
    )
    cos_part = 1.0 + sq * (
        -0.5 + sq * (1.0 / 24 + sq * (-1.0 / 720 + sq * (1.0 / 40320 - sq * (1.0 / 3628800))))
    )
    odd = (quadrant & 1) == 1
    flip_sin = (quadrant & 2) == 2
    flip_cos = ((quadrant + 1) & 2) == 2
    sine = jnp.where(odd, cos_part, sin_part)
    cosine = jnp.where(odd, sin_part, cos_part)
    return jnp.where(flip_cos, -cosine, cosine), jnp.where(flip_sin, -sine, sine)


def body(
    img_hbm,
    proj_hbm,
    curve_hbm,
    noise_hbm,
    group_hbm,
    shift_hbm,
    orient_hbm,
    prior_hbm,
    cls_ref,
    group_out,
    gain_out,
    ev_ref,
    img_ref,
    curve_ref,
    noise_ref,
    group_ref,
    shift_ref,
    proj_ref,
    orient_ref,
    prior_ref,
    xbuf,
    pmain,
    prest,
    ctab,
    stab,
    crest,
    srest,
    smain,
    shrest,
    score,
    wts,
    stat,
    core_out,
    core_in,
    rest_out,
    rest_in,
    far_out,
    x_out,
    x_near_a,
    x_near_b,
    x_in,
    held,
    z_out,
    z_relay,
    z_in,
    z_core,
    ag_z_s,
    ag_z_r,
    ag_y_s,
    ag_y_r,
    ag_f_s,
    ag_f_r,
    st_s,
    st_r,
    co_s,
    co_r,
    xs_s,
    xs_r,
    zs_s,
    zs_r,
    in_s,
):
    img = lax.axis_index("img")
    ref = lax.axis_index("ref")
    x = lax.div(img, 8)
    h = lax.rem(lax.div(img, 2), 4)
    d = lax.rem(img, 2)
    o = 1 - d
    y = lax.div(ref, 4)
    l = lax.rem(ref, 4)

    def ring(v):
        return lax.rem(v + 4, 4)

    def dev(img_at=img, ref_at=ref):
        return {"img": img_at, "ref": ref_at}

    def at_img(xx, hh, dd):
        return dev(img_at=(xx * 4 + hh) * 2 + dd)

    def copy(src, dst, send, recv, to):
        return pltpu.make_async_remote_copy(
            src_ref=src, dst_ref=dst, send_sem=send, recv_sem=recv, device_id=to, device_id_type=MESH
        )

    barrier = pltpu.get_barrier_semaphore()
    peers = [dev(ref_at=y * 4 + lax.rem(l + k, 4)) for k in range(1, 4)]
    peers += [dev(ref_at=lax.rem(ref + 4 * k, 16)) for k in range(1, 4)]
    peers += [at_img(x, h, o), at_img(ring(x + 1), h, d), at_img(ring(x - 1), h, d)]
    peers += [at_img(ring(x + 1), h, o), at_img(ring(x - 1), h, o)]
    for hh in (ring(h + 1), ring(h - 1)):
        peers += [at_img(x, hh, d), at_img(x, hh, o)]
    for peer in peers:
        pl.semaphore_signal(barrier, inc=1, device_id=peer, device_id_type=MESH)

    loads = [
        pltpu.make_async_copy(src, dst, in_s.at[k])
        for k, (src, dst) in enumerate(
            (
                (group_hbm, group_ref),
                (curve_hbm, curve_ref),
                (noise_hbm, noise_ref),
                (img_hbm, img_ref),
                (shift_hbm, shift_ref),
                (proj_hbm, proj_ref),
                (orient_hbm, orient_ref),
                (prior_hbm, prior_ref),
            )
        )
    ]
    for load in loads:
        load.start()
    for load in loads[:4]:
        load.wait()

    lane = lax.broadcasted_iota(jnp.int32, (1, 128), 1)

    def noise_row(tile, count):
        return jnp.concatenate([noise_ref[pl.ds(tile + t, 1), :] for t in range(count)], axis=1)


    group_row = group_ref[...].astype(F32)
    group_row = jnp.concatenate([group_row, group_row], axis=1)
    group_col = jnp.transpose(jnp.broadcast_to(group_row, (128, 128)))[:NIMG, :]
    start = pl.multiple_of(ref * 256, 128)
    turn = lax.rem(384 - 8 * ref, 384)
    curve_here = pltpu.roll(curve_ref[:, pl.ds(start, 384)], turn, 1)
    noise_here = pltpu.roll(jnp.broadcast_to(noise_row(2 * ref, 3), (8, 384)), turn, 1)[:1, :]
    parts = []
    for tile in range(3):
        span = slice(tile * 128, tile * 128 + 128)
        gain = jnp.zeros((NIMG, 128), F32)
        for g in range(GROUPS):
            gain = jnp.where(group_col == float(g), curve_here[g : g + 1, span], gain)
        gain = gain * noise_here[:, span]
        both = []
        for c in range(2):
            if tile < 2:
                pixels = img_ref[:, c, span].astype(F32)
            else:
                pixels = img_ref[:, c, 256:264].astype(F32)
                pixels = jnp.concatenate([pixels, jnp.zeros((NIMG, 120), F32)], axis=1)
            both.append(pixels * gain)
        parts.append(jnp.concatenate(both, axis=0))
    second = pltpu.roll(jnp.concatenate(parts[1:], axis=1), 252, 1)[:, :128]
    rest = jnp.transpose(jnp.where(lane < 4, parts[1], parts[2]))[:16, :]
    row16 = lax.broadcasted_iota(jnp.int32, (16, 128), 0)
    rest = jnp.where(row16 < 8, rest, 0.0)
    xbuf[ref, 0:128, :] = parts[0].astype(BF16)
    xbuf[ref, 128:256, :] = second.astype(BF16)
    xbuf[ref, 256:272, :] = rest.astype(BF16)

    pl.semaphore_wait(barrier, len(peers))

    columns = [lax.rem(l + 4 - e, 4) for e in range(4)]
    halves = (pl.ds(0, 144), pl.ds(144, 128))

    def shard(yy, e):
        return yy * 4 + columns[e]

    def z_send(e, part):
        block = xbuf.at[ref, halves[part]]
        to = dev(ref_at=y * 4 + lax.rem(l + e, 4))
        return copy(block, block, ag_z_s.at[e, part], ag_z_r.at[e, part], to)

    y_up, y_down, y_far = ring(y + 1), ring(y - 1), ring(y + 2)

    def y_copy(way, e, src_y, part):
        to = dev(ref_at=(y_up if way == 0 else y_down) * 4 + l)
        block = xbuf.at[shard(src_y, e), halves[part]]
        return copy(block, block, ag_y_s.at[way, e, part], ag_y_r.at[way, e, part], to)

    def f_copy(way, e, src_y):
        to = dev(ref_at=(y_up if way == 0 else y_down) * 4 + l)
        block = xbuf.at[shard(src_y, e), halves[way]]
        return copy(block, block, ag_f_s.at[way, e], ag_f_r.at[way, e], to)

    def send_y(e, part):
        for way in (part, 1 - part):
            y_copy(way, e, y, part).start()

    z_send(1, 0).start()
    z_send(3, 0).start()
    send_y(0, 0)
    send_y(0, 1)
    z_send(1, 1).start()
    z_send(3, 1).start()
    z_send(2, 0).start()
    z_send(2, 1).start()

    def take_z(e):
        for part in range(2):
            block = xbuf.at[shard(y, e), halves[part]]
            copy(block, block, ag_z_s.at[e, part], ag_z_r.at[e, part], dev(ref_at=shard(y, e))).wait_recv()
            send_y(e, part)

    def take_y(e):
        y_copy(0, e, y_down, 0).wait_recv()
        f_copy(0, e, y_down).start()
        y_copy(1, e, y_up, 1).wait_recv()
        f_copy(1, e, y_up).start()
        y_copy(0, e, y_down, 1).wait_recv()
        y_copy(1, e, y_up, 0).wait_recv()

    def take_far(e):
        f_copy(0, e, y_far).wait_recv()
        f_copy(1, e, y_far).wait_recv()

    loads[4].wait()

    def table(pixel, width):
        srow = lax.broadcasted_iota(jnp.int32, (8, width), 0) + 1
        move_x = jnp.zeros((8, width), jnp.int32)
        move_y = jnp.zeros((8, width), jnp.int32)
        for s in range(1, NSHIFT):
            move_x = jnp.where(srow == s, shift_ref[0, s], move_x)
            move_y = jnp.where(srow == s, shift_ref[1, s], move_y)
        freq_x = pixel & (BOX // 2 - 1)
        freq_y = lax.shift_right_logical(pixel, 6) - NPIX // BOX
        return sincos((move_x * freq_x + move_y * freq_y) & (BOX - 1))

    def table_step(b, carry):
        at = lax.broadcasted_iota(jnp.int32, (8, 256), 1)
        pixel = 264 * b + at + jnp.where(at >= 128, 4, 0)
        cosine, sine = table(pixel, 256)
        ctab[b] = cosine
        stab[b] = sine
        return carry

    lax.fori_loop(0, 16, table_step, 0)
    at = lax.broadcasted_iota(jnp.int32, (8, 128), 1)
    cosine, sine = table(132 * lax.shift_right_logical(at, 2) + 128 + (at & 3), 128)
    crest[...] = cosine
    srest[...] = sine

    for load in loads[5:]:
        load.wait()

    def proj_step(b, carry):
        out = []
        for c in range(2):
            kept = carry[c]
            for u in range(2):
                n = 2 * b + u
                window = proj_ref[:, c, pl.ds(pl.multiple_of(n * 128, 128), 256)].astype(F32)
                turned = pltpu.roll(window, lax.rem(256 - 4 * n, 256), 1)
                pmain[b, c, :, u * 128 : u * 128 + 128] = turned[:, :128].astype(BF16)
                kept = jnp.where(lax.shift_right_logical(lane, 2) == n, window[:, 128:], kept)
            out.append(kept)
        return tuple(out)

    zero_rest = jnp.zeros((NPROJ, 128), F32)
    rests = lax.fori_loop(0, 16, proj_step, (zero_rest, zero_rest))
    for c in range(2):
        prest[c] = rests[c].astype(BF16)

    take_y(0)
    take_z(1)
    take_z(3)

    def norm_step(t, total):
        span = pl.ds(pl.multiple_of(t * 384, 128), 384)
        re = proj_ref[:, 0, span].astype(F32)
        im = proj_ref[:, 1, span].astype(F32)
        curve = curve_ref[:, span]
        gain = 0.5 * (curve * curve * noise_row(3 * t, 3))
        power = re * re + im * im
        return total + lax.dot_general(
            two_parts(power), two_parts(gain), NT, preferred_element_type=F32
        )

    def two_parts(value):
        high = value.astype(BF16)
        return jnp.concatenate([high, (value - high.astype(F32)).astype(BF16)], axis=0)

    norm = lax.fori_loop(0, 11, norm_step, jnp.zeros((2 * NPROJ, 2 * GROUPS), F32))
    norm = norm[:NPROJ] + norm[NPROJ:]
    norm = norm[:, :GROUPS] + norm[:, GROUPS:]
    grow = lax.broadcasted_iota(jnp.int32, (GROUPS, 128), 0)
    members = (group_row == grow.astype(F32)).astype(F32)
    penalty = jnp.dot(norm, members, precision=HIGHEST, preferred_element_type=F32)
    orient_row = jnp.concatenate([orient_ref[...].astype(F32), jnp.zeros((1, 80), F32)], axis=1)
    orient_col = jnp.transpose(jnp.broadcast_to(orient_row, (128, 128)))[:NPROJ, :]
    prior = jnp.zeros((NPROJ, 1), F32)
    for half in range(2):
        hit = orient_col == (lane + half * 128).astype(F32)
        prior += jnp.sum(
            jnp.where(hit, prior_ref[half : half + 1, :], 0.0), axis=1, keepdims=True
        )
    base = prior - penalty
    span = pl.ds(pl.multiple_of(img * 128, 128), 256)
    curve = curve_ref[:, span]
    gain_out[...] = pltpu.roll(curve * curve * noise_row(img, 2), lax.rem(256 - 4 * img, 256), 1)

    score[...] = jnp.zeros_like(score)

    def process(b):
        for t in range(2):
            span = slice(t * 128, t * 128 + 128)
            re = xbuf[b, t * 128 : t * 128 + 64, :]
            im = xbuf[b, t * 128 + 64 : t * 128 + 128, :]
            smain[b, 0, 0:NIMG, span] = re
            smain[b, 1, 0:NIMG, span] = im
            re = re.astype(F32)
            im = im.astype(F32)
            for s in range(1, NSHIFT):
                rows = slice(s * NIMG, s * NIMG + NIMG)
                cosine = ctab[b, s - 1 : s, span]
                sine = stab[b, s - 1 : s, span]
                smain[b, 0, rows, span] = (re * cosine + im * sine).astype(BF16)
                smain[b, 1, rows, span] = (im * cosine - re * sine).astype(BF16)
        score[...] += lax.dot_general(
            smain[b, 0], pmain[b, 0], NT, preferred_element_type=F32
        ) + lax.dot_general(smain[b, 1], pmain[b, 1], NT, preferred_element_type=F32)

    def process_all(blocks):
        def step(t, carry):
            b = blocks[0]
            for k in range(1, len(blocks)):
                b = jnp.where(t == k, blocks[k], b)
            process(b)
            return carry

        lax.fori_loop(0, len(blocks), step, 0)

    take_z(2)
    process_all([shard(y, 0), shard(y, 1)])
    take_y(1)
    process_all([shard(y_down, 0), shard(y_up, 0)])
    take_far(0)
    take_y(3)
    process_all([shard(y_far, 0), shard(y, 3), shard(y_down, 1)])
    take_y(2)
    process_all([shard(y_up, 1), shard(y, 2), shard(y_down, 3), shard(y_up, 3)])
    take_far(1)
    process_all([shard(y_far, 1), shard(y_down, 2), shard(y_up, 2)])
    take_far(3)
    process(shard(y_far, 3))
    take_far(2)
    process(shard(y_far, 2))

    rest_t = jnp.concatenate([xbuf[b, 256:272, :].astype(F32)[:8] for b in range(16)], axis=0)
    rest_x = jnp.transpose(rest_t)
    re, im = rest_x[:NIMG], rest_x[NIMG:]
    shrest[0, 0:NIMG, :] = re.astype(BF16)
    shrest[1, 0:NIMG, :] = im.astype(BF16)
    for s in range(1, NSHIFT):
        rows = slice(s * NIMG, s * NIMG + NIMG)
        cosine = crest[s - 1 : s, :]
        sine = srest[s - 1 : s, :]
        shrest[0, rows, :] = (re * cosine + im * sine).astype(BF16)
        shrest[1, rows, :] = (im * cosine - re * sine).astype(BF16)
    full = (
        score[...]
        + lax.dot_general(shrest[0], prest[0], NT, preferred_element_type=F32)
        + lax.dot_general(shrest[1], prest[1], NT, preferred_element_type=F32)
    )
    full = jnp.concatenate([full, jnp.zeros((ROWS, 128 - NPROJ), F32)], axis=1)

    tiles = []
    for t in range(5):
        if t < 4:
            tiles.append(jnp.transpose(full[t * 128 : t * 128 + 128])[:NPROJ] + base)
        else:
            last = jnp.concatenate([full[512:576], jnp.zeros((64, 128), F32)], axis=0)
            tiles.append(jnp.where(lane < 64, jnp.transpose(last)[:NPROJ] + base, -3e38))
    high = tiles[0]
    for t in range(1, 5):
        high = jnp.maximum(high, tiles[t])
    high = jnp.max(high, axis=0, keepdims=True)
    high = jnp.maximum(high, pltpu.roll(jnp.broadcast_to(high, (8, 128)), 64, 1)[:1])
    total = jnp.exp(tiles[0] - high)
    for t in range(1, 5):
        total += jnp.exp(tiles[t] - high)
    total = jnp.sum(total, axis=0, keepdims=True)
    total = total + pltpu.roll(jnp.broadcast_to(total, (8, 128)), 64, 1)[:1]
    row8 = lax.broadcasted_iota(jnp.int32, (8, 128), 0)

    def merged(blocks):
        top = blocks[0][0:1, :]
        for block in blocks[1:]:
            top = jnp.maximum(top, block[0:1, :])
        whole = jnp.zeros((1, 128), F32)
        for block in blocks:
            whole += block[1:2, :] * jnp.exp(block[0:1, :] - top)
        return top, whole

    st_copies = []
    for stage in range(2):
        mine_at = l if stage == 0 else y
        stat[stage, mine_at] = jnp.where(row8 == 0, high, total)
        for k in range(1, 4):
            to = y * 4 + lax.rem(l + k, 4) if stage == 0 else lax.rem(ref + 4 * k, 16)
            block = stat.at[stage, mine_at]
            c = copy(block, block, st_s.at[3 * stage + k - 1], st_r.at[3 * stage + k - 1], dev(ref_at=to))
            c.start()
            st_copies.append(c)
        for k in range(1, 4):
            src = lax.rem(mine_at + 4 - k, 4)
            block = stat.at[stage, src]
            come_from = y * 4 + src if stage == 0 else src * 4 + l
            copy(
                block, block, st_s.at[3 * stage + k - 1], st_r.at[3 * stage + k - 1], dev(ref_at=come_from)
            ).wait_recv()
        high, total = merged([stat[stage, b] for b in range(4)])
    evidence = high + jnp.log(total)
    ev_ref[...] = evidence
    for t in range(5):
        w = jnp.exp(tiles[t] - evidence).astype(BF16)
        if t < 4:
            wts[:, t * 128 : t * 128 + 128] = w
        else:
            wts[:, 512:576] = w[:, :64]
    members_all = jnp.concatenate([members.astype(BF16)] * 4 + [members[:, :64].astype(BF16)], axis=1)
    group_sum = lax.dot_general(members_all, wts[...], NT, preferred_element_type=F32)
    group_sum = jnp.concatenate([group_sum, jnp.zeros((GROUPS, 80), F32)], axis=1)

    other = at_img(x, h, o)
    rest_mine = jnp.dot(wts[...], shrest[d], preferred_element_type=F32)
    rest_theirs = jnp.dot(wts[...], shrest[o], preferred_element_type=F32)

    order = [ring(x + 2), ring(x + 1), ring(x + 3), x]
    runs = [ring(h + 2), ring(h + 1), ring(h + 3), h]

    def core_copy(i):
        return copy(core_out.at[i], core_in.at[i], co_s.at[i], co_r.at[i], other)

    def other_chunk(i):
        for u in range(4):
            got = jnp.dot(wts[...], smain[4 * order[i] + runs[u], o], preferred_element_type=F32)
            for v in range(2):
                r = PIECE * (2 * u + v)
                core_out[i, r : r + PIECE, :] = got[:, v * 128 : v * 128 + 128].astype(BF16)
        core_copy(i).start()

    def left(value, by):
        return pltpu.roll(value, lax.rem(256 - by, 128), 1)

    def packed(q, rest_tile, group_tile, c):
        out = left(rest_tile[0:16], 32 * q)
        out = jnp.where(lane < 32, out, left(rest_tile[16:32], 32 * q - 32))
        out = jnp.where(lane < 64, out, left(rest_tile[32:48], 32 * q - 64))
        return jnp.where(lane < 96, out, left(group_tile, 32 + 24 * c))

    def piece_row(k):
        return 16 + PIECE * k

    def rows_of(k):
        return slice(0, 16) if k < 0 else slice(piece_row(k), piece_row(k) + PIECE)

    far_copies = []
    for k in range(2):
        c = d if k == 0 else o
        for u in range(4):
            got = jnp.dot(wts[...], smain[4 * order[0] + runs[u], c], preferred_element_type=F32).astype(BF16)
            for v in range(2):
                far_out[k, rows_of(2 * u + v), :] = got[:, v * 128 : v * 128 + 128]
        rest_tile = rest_mine if k == 0 else rest_theirs
        far_out[k, 0:16, :] = packed(order[0], rest_tile, group_sum, c).astype(BF16)
        for way in range(2):
            rows = pl.ds(0, HALF) if way == 0 else pl.ds(HALF, MSG - HALF)
            land = x_near_a if way == 0 else x_near_b
            to = at_img(ring(x + 1) if way == 0 else ring(x - 1), h, c)
            far_copies.append(
                copy(far_out.at[k, rows], land.at[k], xs_s.at[2 * way + k], xs_r.at[2 * way + k], to)
            )
            far_copies[-1].start()

    rest_out[0:48, :] = rest_theirs.astype(BF16)
    rest_out[48:64, :] = group_sum.astype(BF16)
    rest_copy = copy(rest_out, rest_in, co_s.at[4], co_r.at[4], other)
    rest_copy.start()
    for i in range(1, 4):
        other_chunk(i)

    rest_copy.wait_recv()
    rest_sum = rest_mine + rest_in[0:48, :].astype(F32)
    group_sum = group_sum + rest_in[48:64, :].astype(F32)

    def own_chunk(i):
        q = order[i]
        sums = [
            jnp.dot(wts[...], smain[4 * q + runs[u], d], preferred_element_type=F32) for u in range(4)
        ]
        core_copy(i).wait_recv()
        for u in range(4):
            for v in range(2):
                k = 2 * u + v
                r = PIECE * k
                held[rows_of(k), :] = (
                    sums[u][:, v * 128 : v * 128 + 128] + core_in[i, r : r + PIECE, :].astype(F32)
                )
        held[0:16, :] = packed(q, rest_sum, group_sum, d)

    x_up, x_down = at_img(ring(x + 1), h, d), at_img(ring(x - 1), h, d)

    def near_wait(way):
        for k in range(2):
            far_copies[2 * k + way].wait_recv()

    def x_copy(way, part):
        rows = pl.ds(0, FIRST) if part == 0 else pl.ds(FIRST, MSG - FIRST)
        k = 4 + 2 * way + part
        to = x_up if way == 0 else x_down
        return copy(x_out.at[way, rows], x_in.at[way, rows], xs_s.at[k], xs_r.at[k], to)

    own_chunk(1)
    x_out[0, HALF:MSG, :] = held[HALF:MSG, :].astype(BF16)
    near_wait(0)
    x_out[0, 0:HALF, :] = (
        held[0:HALF, :] + x_near_a[0].astype(F32) + x_near_a[1].astype(F32)
    ).astype(BF16)
    x_copy(0, 0).start()
    x_copy(0, 1).start()

    own_chunk(2)
    x_out[1, 0:HALF, :] = held[0:HALF, :].astype(BF16)
    x_copy(1, 0).start()
    near_wait(1)
    x_out[1, HALF:MSG, :] = (
        held[HALF:MSG, :] + x_near_b[0].astype(F32) + x_near_b[1].astype(F32)
    ).astype(BF16)
    x_copy(1, 1).start()

    own_chunk(3)

    def add_x(part):
        rows = slice(0, FIRST) if part == 0 else slice(FIRST, MSG)
        x_copy(0, part).wait_recv()
        x_copy(1, part).wait_recv()
        held[rows, :] += x_in[0, rows, :].astype(F32) + x_in[1, rows, :].astype(F32)

    add_x(0)

    def piece_of(u, dd):
        return held[pl.ds(pl.multiple_of(16 + PIECE * (2 * u + dd), 16), PIECE), :]

    rest_pack = held[0:16, :]
    h_up, h_down = ring(h + 1), ring(h - 1)

    def fill(slot, value, extra):
        z_out[slot, 0:48, :] = value.astype(BF16)
        z_out[slot, 48:64, :] = extra.astype(BF16)

    fill(0, piece_of(0, 0), rest_pack)
    fill(1, piece_of(0, 1), rest_pack)
    relay_up = copy(z_out.at[0], z_relay.at[0], zs_s.at[0], zs_r.at[0], at_img(x, h_up, d))
    relay_down = copy(z_out.at[1], z_relay.at[1], zs_s.at[1], zs_r.at[1], at_img(x, h_down, d))
    relay_up.start()
    relay_down.start()
    add_x(1)

    def z_copy(slot):
        way, dd = (slot - 2) // 2, (slot - 2) % 2
        to = at_img(x, h_up if way == 0 else h_down, dd)
        return copy(z_out.at[slot], z_in.at[way, d], zs_s.at[slot], zs_r.at[2 + 2 * way + d], to)

    fill(3, piece_of(1, 1), rest_pack)
    z_copy(3).start()
    fill(4, piece_of(2, 0), rest_pack)
    z_copy(4).start()
    fill(6, piece_of(3, o), rest_pack)
    core_last = copy(z_out.at[6], z_core, zs_s.at[6], zs_r.at[6], other)
    core_last.start()
    relay_up.wait_recv()
    fill(
        2,
        piece_of(1, 0) + z_relay[0, 0:48, :].astype(F32),
        rest_pack + z_relay[0, 48:64, :].astype(F32),
    )
    z_copy(2).start()
    relay_down.wait_recv()
    fill(
        5,
        piece_of(2, 1) + z_relay[1, 0:48, :].astype(F32),
        rest_pack + z_relay[1, 48:64, :].astype(F32),
    )
    z_copy(5).start()

    mine = jnp.concatenate([piece_of(3, d), rest_pack], axis=0)
    core_last.wait_recv()
    theirs = z_core[...].astype(F32)
    for way in range(2):
        for c in range(2):
            slot = z_in.at[way, c]
            copy(slot, slot, zs_s.at[2], zs_r.at[2 + 2 * way + c], other).wait_recv()
    local = 2 * h + d
    packs = []
    for c in range(2):
        both = jnp.where(d == c, mine, theirs)
        both = both + z_in[0, c].astype(F32) + z_in[1, c].astype(F32)
        cls_ref[c, :, 0:128] = both[0:48]
        pack = both[48:64]
        packs.append(pack)
        for a in range(3):
            cls_ref[c, 16 * a : 16 * a + 16, 128:256] = left(pack, 32 * a + 4 * local)
    group_all = jnp.where(lane < 24, left(packs[0], 96), left(packs[1], 72))
    group_out[...] = jnp.where(lane < 48, group_all, 0.0)

    for e in range(4):
        for part in range(2):
            if e:
                z_send(e, part).wait_send()
            for way in range(2):
                y_copy(way, e, y, part).wait_send()
        for way in range(2):
            f_copy(way, e, y).wait_send()
    for c in st_copies:
        c.wait_send()
    for i in range(1, 4):
        core_copy(i).wait_send()
    for c in far_copies:
        c.wait_send()
    for c in (rest_copy, relay_up, relay_down, core_last):
        c.wait_send()
    for way in range(2):
        for part in range(2):
            x_copy(way, part).wait_send()
    for slot in range(2, 6):
        z_copy(slot).wait_send()


def finish(
    cls_hbm, group_hbm, gain_hbm, ev_hbm, cls_out, con_out, ev_out, cls_ref, group_ref, gain_ref, ev_ref, in_s
):
    loads = [
        pltpu.make_async_copy(src, dst, in_s.at[k])
        for k, (src, dst) in enumerate(
            ((cls_hbm, cls_ref), (group_hbm, group_ref), (gain_hbm, gain_ref), (ev_hbm, ev_ref))
        )
    ]
    for load in loads:
        load.start()
    for load in loads:
        load.wait()
    for c in range(2):
        cls_out[:, c, :] = cls_ref[c, :, 0:132]
    column = jnp.transpose(jnp.concatenate([group_ref[...], jnp.zeros((112, 128), F32)], axis=0))
    con_out[...] = jnp.dot(
        column[:NPROJ, :GROUPS], gain_ref[...], precision=HIGHEST, preferred_element_type=F32
    )[:, :132]
    ev_out[...] = ev_ref[:, :NIMG]


def on_device(
    images, projections, contrast_curve, noise_weight, defocus_group, shifts, orient_index, orient_prior
):
    vmem = pl.BlockSpec(memory_space=pltpu.VMEM)
    sem = pltpu.SemaphoreType.DMA
    hbm = pl.BlockSpec(memory_space=pl.ANY)
    held = pl.pallas_call(
        body,
        out_shape=(
            jax.ShapeDtypeStruct((2, NPROJ, 256), F32),
            jax.ShapeDtypeStruct((GROUPS, 128), F32),
            jax.ShapeDtypeStruct((GROUPS, 256), F32),
            jax.ShapeDtypeStruct((1, 128), F32),
        ),
        in_specs=[hbm] * 8,
        out_specs=(vmem,) * 4,
        scratch_shapes=[
            pltpu.VMEM((NIMG, 2, 264), BF16),
            pltpu.VMEM((GROUPS, NPIX), F32),
            pltpu.VMEM((NPIX // 128, 128), F32),
            pltpu.VMEM((1, NIMG), jnp.int32),
            pltpu.SMEM((2, NSHIFT), jnp.int32),
            pltpu.VMEM((NPROJ, 2, NPIX), BF16),
            pltpu.VMEM((1, NPROJ), jnp.int32),
            pltpu.VMEM((2, 128), F32),
            pltpu.VMEM((16, SHARD, 128), BF16),
            pltpu.VMEM((16, 2, NPROJ, 256), BF16),
            pltpu.VMEM((2, NPROJ, 128), BF16),
            pltpu.VMEM((16, 8, 256), F32),
            pltpu.VMEM((16, 8, 256), F32),
            pltpu.VMEM((8, 128), F32),
            pltpu.VMEM((8, 128), F32),
            pltpu.VMEM((16, 2, ROWS, 256), BF16),
            pltpu.VMEM((2, ROWS, 128), BF16),
            pltpu.VMEM((ROWS, NPROJ), F32),
            pltpu.VMEM((NPROJ, ROWS), BF16),
            pltpu.VMEM((2, 4, 8, 128), F32),
            pltpu.VMEM((4, 8 * PIECE, 128), BF16),
            pltpu.VMEM((4, 8 * PIECE, 128), BF16),
            pltpu.VMEM((64, 128), BF16),
            pltpu.VMEM((64, 128), BF16),
            pltpu.VMEM((2, MSG, 128), BF16),
            pltpu.VMEM((2, MSG, 128), BF16),
            pltpu.VMEM((2, HALF, 128), BF16),
            pltpu.VMEM((2, MSG - HALF, 128), BF16),
            pltpu.VMEM((2, MSG, 128), BF16),
            pltpu.VMEM((MSG, 128), F32),
            pltpu.VMEM((7, 64, 128), BF16),
            pltpu.VMEM((2, 64, 128), BF16),
            pltpu.VMEM((2, 2, 64, 128), BF16),
            pltpu.VMEM((64, 128), BF16),
            sem((4, 2)),
            sem((4, 2)),
            sem((2, 4, 2)),
            sem((2, 4, 2)),
            sem((2, 4)),
            sem((2, 4)),
            sem((6,)),
            sem((6,)),
            sem((5,)),
            sem((5,)),
            sem((8,)),
            sem((8,)),
            sem((7,)),
            sem((7,)),
            sem((8,)),
        ],
        compiler_params=pltpu.CompilerParams(
            collective_id=0, has_side_effects=True, vmem_limit_bytes=60 * 1024 * 1024
        ),
        name="expectation",
    )(
        images,
        projections,
        contrast_curve,
        noise_weight.reshape(NPIX // 128, 128),
        defocus_group.reshape(1, NIMG),
        shifts.T,
        orient_index.reshape(1, NPROJ),
        orient_prior.reshape(2, 128),
    )
    cls, con, ev = pl.pallas_call(
        finish,
        out_shape=(
            jax.ShapeDtypeStruct((NPROJ, 2, 132), F32),
            jax.ShapeDtypeStruct((NPROJ, 132), F32),
            jax.ShapeDtypeStruct((1, NIMG), F32),
        ),
        in_specs=[hbm] * 4,
        out_specs=(vmem,) * 3,
        scratch_shapes=[
            pltpu.VMEM((2, NPROJ, 256), F32),
            pltpu.VMEM((GROUPS, 128), F32),
            pltpu.VMEM((GROUPS, 256), F32),
            pltpu.VMEM((1, 128), F32),
            sem((4,)),
        ],
        compiler_params=pltpu.CompilerParams(vmem_limit_bytes=60 * 1024 * 1024),
        name="finish",
    )(*held)
    return cls, con, ev.reshape(NIMG)


def solution(mesh):
    in_specs = (P("img", None, "ref"), P("ref", None, None), P(), P(), P("img"), P(), P("ref"), P())
    out_specs = (P("ref", None, "img"), P("ref", "img"), P("img"))
    return jax.shard_map(
        on_device, mesh=mesh, in_specs=in_specs, out_specs=out_specs, check_vma=False
    )
```

```python
import math

import jax
import jax.numpy as jnp
from jax import lax
from jax.experimental import pallas as pl
from jax.experimental.pallas import tpu as pltpu
from jax.sharding import PartitionSpec as P

MESH = pl.DeviceIdType.MESH
F32 = jnp.float32
BF16 = jnp.bfloat16
HIGHEST = lax.Precision.HIGHEST
NT = (((1,), (1,)), ((), ()))
TN = (((0,), (0,)), ((), ()))

NPIX = 4224
BOX = 128
NSHIFT = 9
NIMG = 64
NPROJ = 48
GROUPS = 16
ROWS = NSHIFT * NIMG
SHARD = 272
PIECE = 48
MSG = 400
HALF = 208
FIRST = 112


def sincos(steps):
    quadrant = lax.shift_right_arithmetic(steps + 16, 5)
    rest = (steps - quadrant * 32).astype(F32) * (2.0 * math.pi / BOX)
    sq = rest * rest
    sin_part = rest * (
        1.0 + sq * (-1.0 / 6 + sq * (1.0 / 120 + sq * (-1.0 / 5040 + sq * (1.0 / 362880))))
    )
    cos_part = 1.0 + sq * (
        -0.5 + sq * (1.0 / 24 + sq * (-1.0 / 720 + sq * (1.0 / 40320 - sq * (1.0 / 3628800))))
    )
    odd = (quadrant & 1) == 1
    flip_sin = (quadrant & 2) == 2
    flip_cos = ((quadrant + 1) & 2) == 2
    sine = jnp.where(odd, cos_part, sin_part)
    cosine = jnp.where(odd, sin_part, cos_part)
    return jnp.where(flip_cos, -cosine, cosine), jnp.where(flip_sin, -sine, sine)


def body(
    img_hbm,
    proj_hbm,
    curve_hbm,
    noise_hbm,
    group_hbm,
    shift_hbm,
    orient_hbm,
    prior_hbm,
    cls_ref,
    group_out,
    gain_out,
    ev_ref,
    img_ref,
    curve_ref,
    noise_ref,
    group_ref,
    shift_ref,
    proj_ref,
    planes,
    orient_ref,
    prior_ref,
    xbuf,
    pmain,
    prest,
    ctab,
    stab,
    crest,
    srest,
    smain,
    shrest,
    score,
    wts,
    stat,
    core_out,
    core_in,
    rest_out,
    rest_in,
    far_out,
    x_out,
    x_near_a,
    x_near_b,
    x_in,
    held,
    z_out,
    z_relay,
    z_in,
    z_core,
    ag_z_s,
    ag_z_r,
    ag_y_s,
    ag_y_r,
    ag_f_s,
    ag_f_r,
    st_s,
    st_r,
    co_s,
    co_r,
    xs_s,
    xs_r,
    zs_s,
    zs_r,
    in_s,
):
    img = lax.axis_index("img")
    ref = lax.axis_index("ref")
    x = lax.div(img, 8)
    h = lax.rem(lax.div(img, 2), 4)
    d = lax.rem(img, 2)
    o = 1 - d
    y = lax.div(ref, 4)
    l = lax.rem(ref, 4)

    def ring(v):
        return lax.rem(v + 4, 4)

    def dev(img_at=img, ref_at=ref):
        return {"img": img_at, "ref": ref_at}

    def at_img(xx, hh, dd):
        return dev(img_at=(xx * 4 + hh) * 2 + dd)

    def copy(src, dst, send, recv, to):
        return pltpu.make_async_remote_copy(
            src_ref=src, dst_ref=dst, send_sem=send, recv_sem=recv, device_id=to, device_id_type=MESH
        )

    barrier = pltpu.get_barrier_semaphore()
    peers = [dev(ref_at=y * 4 + lax.rem(l + k, 4)) for k in range(1, 4)]
    peers += [dev(ref_at=lax.rem(ref + 4 * k, 16)) for k in range(1, 4)]
    peers += [at_img(x, h, o), at_img(ring(x + 1), h, d), at_img(ring(x - 1), h, d)]
    peers += [at_img(ring(x + 1), h, o), at_img(ring(x - 1), h, o)]
    for hh in (ring(h + 1), ring(h - 1)):
        peers += [at_img(x, hh, d), at_img(x, hh, o)]
    for peer in peers:
        pl.semaphore_signal(barrier, inc=1, device_id=peer, device_id_type=MESH)

    loads = [
        pltpu.make_async_copy(src, dst, in_s.at[k])
        for k, (src, dst) in enumerate(
            (
                (group_hbm, group_ref),
                (curve_hbm, curve_ref),
                (noise_hbm, noise_ref),
                (img_hbm, img_ref),
                (shift_hbm, shift_ref),
                (proj_hbm, proj_ref),
                (orient_hbm, orient_ref),
                (prior_hbm, prior_ref),
            )
        )
    ]
    for load in loads:
        load.start()
    for load in loads[:4]:
        load.wait()

    lane = lax.broadcasted_iota(jnp.int32, (1, 128), 1)

    def noise_row(tile, count):
        return jnp.concatenate([noise_ref[pl.ds(tile + t, 1), :] for t in range(count)], axis=1)


    group_row = group_ref[...].astype(F32)
    group_row = jnp.concatenate([group_row, group_row], axis=1)
    group_col = jnp.transpose(jnp.broadcast_to(group_row, (128, 128)))[:NIMG, :]
    start = pl.multiple_of(ref * 256, 128)
    turn = lax.rem(384 - 8 * ref, 384)
    curve_here = pltpu.roll(curve_ref[:, pl.ds(start, 384)], turn, 1)
    noise_here = pltpu.roll(jnp.broadcast_to(noise_row(2 * ref, 3), (8, 384)), turn, 1)[:1, :]
    parts = []
    for tile in range(3):
        span = slice(tile * 128, tile * 128 + 128)
        gain = jnp.zeros((NIMG, 128), F32)
        for g in range(GROUPS):
            gain = jnp.where(group_col == float(g), curve_here[g : g + 1, span], gain)
        gain = gain * noise_here[:, span]
        both = []
        for c in range(2):
            if tile < 2:
                pixels = img_ref[:, c, span].astype(F32)
            else:
                pixels = img_ref[:, c, 256:264].astype(F32)
                pixels = jnp.concatenate([pixels, jnp.zeros((NIMG, 120), F32)], axis=1)
            both.append(pixels * gain)
        parts.append(jnp.concatenate(both, axis=0))
    second = pltpu.roll(jnp.concatenate(parts[1:], axis=1), 252, 1)[:, :128]
    rest = jnp.transpose(jnp.where(lane < 4, parts[1], parts[2]))[:16, :]
    row16 = lax.broadcasted_iota(jnp.int32, (16, 128), 0)
    rest = jnp.where(row16 < 8, rest, 0.0)
    xbuf[ref, 0:128, :] = parts[0].astype(BF16)
    xbuf[ref, 128:256, :] = second.astype(BF16)
    xbuf[ref, 256:272, :] = rest.astype(BF16)

    pl.semaphore_wait(barrier, len(peers))

    columns = [lax.rem(l + 4 - e, 4) for e in range(4)]
    halves = (pl.ds(0, 144), pl.ds(144, 128))

    def shard(yy, e):
        return yy * 4 + columns[e]

    def z_send(e, part):
        block = xbuf.at[ref, halves[part]]
        to = dev(ref_at=y * 4 + lax.rem(l + e, 4))
        return copy(block, block, ag_z_s.at[e, part], ag_z_r.at[e, part], to)

    y_up, y_down, y_far = ring(y + 1), ring(y - 1), ring(y + 2)

    def y_copy(way, e, src_y, part):
        to = dev(ref_at=(y_up if way == 0 else y_down) * 4 + l)
        block = xbuf.at[shard(src_y, e), halves[part]]
        return copy(block, block, ag_y_s.at[way, e, part], ag_y_r.at[way, e, part], to)

    def f_copy(way, e, src_y):
        to = dev(ref_at=(y_up if way == 0 else y_down) * 4 + l)
        block = xbuf.at[shard(src_y, e), halves[way]]
        return copy(block, block, ag_f_s.at[way, e], ag_f_r.at[way, e], to)

    def send_y(e, part):
        for way in (part, 1 - part):
            y_copy(way, e, y, part).start()

    z_send(1, 0).start()
    z_send(3, 0).start()
    send_y(0, 0)
    send_y(0, 1)
    z_send(1, 1).start()
    z_send(3, 1).start()

    def take_z(e, part):
        block = xbuf.at[shard(y, e), halves[part]]
        copy(block, block, ag_z_s.at[e, part], ag_z_r.at[e, part], dev(ref_at=shard(y, e))).wait_recv()
        send_y(e, part)

    def take_y(e):
        y_copy(0, e, y_down, 0).wait_recv()
        f_copy(0, e, y_down).start()
        y_copy(1, e, y_up, 1).wait_recv()
        f_copy(1, e, y_up).start()
        y_copy(0, e, y_down, 1).wait_recv()
        y_copy(1, e, y_up, 0).wait_recv()

    def take_far(e):
        f_copy(0, e, y_far).wait_recv()
        f_copy(1, e, y_far).wait_recv()

    loads[4].wait()

    def table(pixel, width):
        srow = lax.broadcasted_iota(jnp.int32, (8, width), 0) + 1
        move_x = jnp.zeros((8, width), jnp.int32)
        move_y = jnp.zeros((8, width), jnp.int32)
        for s in range(1, NSHIFT):
            move_x = jnp.where(srow == s, shift_ref[0, s], move_x)
            move_y = jnp.where(srow == s, shift_ref[1, s], move_y)
        freq_x = pixel & (BOX // 2 - 1)
        freq_y = lax.shift_right_logical(pixel, 6) - NPIX // BOX
        return sincos((move_x * freq_x + move_y * freq_y) & (BOX - 1))

    def table_step(b, carry):
        at = lax.broadcasted_iota(jnp.int32, (8, 256), 1)
        pixel = 264 * b + at + jnp.where(at >= 128, 4, 0)
        cosine, sine = table(pixel, 256)
        ctab[b] = cosine
        stab[b] = sine
        return carry

    lax.fori_loop(0, 16, table_step, 0)
    at = lax.broadcasted_iota(jnp.int32, (8, 128), 1)
    cosine, sine = table(132 * lax.shift_right_logical(at, 2) + 128 + (at & 3), 128)
    crest[...] = cosine
    srest[...] = sine

    z_send(2, 0).start()
    z_send(2, 1).start()

    for load in loads[5:]:
        load.wait()

    def plane_step(t, carry):
        span = pl.ds(pl.multiple_of(t * 384, 128), 384)
        for c in range(2):
            planes[c, :, span] = proj_ref[:, c, span]
        return carry

    lax.fori_loop(0, 11, plane_step, 0)
    take_y(0)


    def proj_step(b, carry):
        out = []
        for c in range(2):
            kept = carry[c]
            for u in range(2):
                n = 2 * b + u
                window = planes[c, :, pl.ds(pl.multiple_of(n * 128, 128), 256)].astype(F32)
                turned = pltpu.roll(window, lax.rem(256 - 4 * n, 256), 1)
                pmain[b, c, :, u * 128 : u * 128 + 128] = turned[:, :128].astype(BF16)
                kept = jnp.where(lax.shift_right_logical(lane, 2) == n, window[:, 128:], kept)
            out.append(kept)
        return tuple(out)

    zero_rest = jnp.zeros((NPROJ, 128), F32)
    rests = lax.fori_loop(0, 8, proj_step, (zero_rest, zero_rest))
    for part in range(2):
        take_z(1, part)
        take_z(3, part)
    rests = lax.fori_loop(8, 16, proj_step, rests)
    for c in range(2):
        prest[c] = rests[c].astype(BF16)


    def norm_step(t, total):
        span = pl.ds(pl.multiple_of(t * 384, 128), 384)
        re = planes[0, :, span].astype(F32)
        im = planes[1, :, span].astype(F32)
        curve = curve_ref[:, span]
        gain = 0.5 * (curve * curve * noise_row(3 * t, 3))
        power = re * re + im * im
        return total + lax.dot_general(
            two_parts(power), two_parts(gain), NT, preferred_element_type=F32
        )

    def two_parts(value):
        high = value.astype(BF16)
        return jnp.concatenate([high, (value - high.astype(F32)).astype(BF16)], axis=0)

    norm = lax.fori_loop(0, 11, norm_step, jnp.zeros((2 * NPROJ, 2 * GROUPS), F32))
    norm = norm[:NPROJ] + norm[NPROJ:]
    norm = norm[:, :GROUPS] + norm[:, GROUPS:]
    grow = lax.broadcasted_iota(jnp.int32, (GROUPS, 128), 0)
    members = (group_row == grow.astype(F32)).astype(F32)
    penalty = jnp.dot(norm, members, precision=HIGHEST, preferred_element_type=F32)
    orient_row = jnp.concatenate([orient_ref[...].astype(F32), jnp.zeros((1, 80), F32)], axis=1)
    orient_col = jnp.transpose(jnp.broadcast_to(orient_row, (128, 128)))[:NPROJ, :]
    prior = jnp.zeros((NPROJ, 1), F32)
    for half in range(2):
        hit = orient_col == (lane + half * 128).astype(F32)
        prior += jnp.sum(
            jnp.where(hit, prior_ref[half : half + 1, :], 0.0), axis=1, keepdims=True
        )
    base = prior - penalty
    span = pl.ds(pl.multiple_of(img * 128, 128), 256)
    curve = curve_ref[:, span]
    gain_out[...] = pltpu.roll(curve * curve * noise_row(img, 2), lax.rem(256 - 4 * img, 256), 1)

    score[...] = jnp.zeros_like(score)

    def process(b):
        for t in range(2):
            span = slice(t * 128, t * 128 + 128)
            re = xbuf[b, t * 128 : t * 128 + 64, :]
            im = xbuf[b, t * 128 + 64 : t * 128 + 128, :]
            smain[b, 0, 0:NIMG, span] = re
            smain[b, 1, 0:NIMG, span] = im
            re = re.astype(F32)
            im = im.astype(F32)
            for s in range(1, NSHIFT):
                rows = slice(s * NIMG, s * NIMG + NIMG)
                cosine = ctab[b, s - 1 : s, span]
                sine = stab[b, s - 1 : s, span]
                smain[b, 0, rows, span] = (re * cosine + im * sine).astype(BF16)
                smain[b, 1, rows, span] = (im * cosine - re * sine).astype(BF16)
        score[...] += lax.dot_general(
            smain[b, 0], pmain[b, 0], NT, preferred_element_type=F32
        ) + lax.dot_general(smain[b, 1], pmain[b, 1], NT, preferred_element_type=F32)

    def process_all(blocks):
        def step(t, carry):
            b = blocks[0]
            for k in range(1, len(blocks)):
                b = jnp.where(t == k, blocks[k], b)
            process(b)
            return carry

        lax.fori_loop(0, len(blocks), step, 0)

    take_z(2, 0)
    take_z(2, 1)
    process_all([shard(y, 0), shard(y, 1)])
    take_y(1)
    process_all([shard(y_down, 0), shard(y_up, 0)])
    take_far(0)
    take_y(3)
    process_all([shard(y_far, 0), shard(y, 3), shard(y_down, 1)])
    take_y(2)
    process_all([shard(y_up, 1), shard(y, 2), shard(y_down, 3), shard(y_up, 3)])
    take_far(1)
    process_all([shard(y_far, 1), shard(y_down, 2), shard(y_up, 2)])
    take_far(3)
    process(shard(y_far, 3))
    take_far(2)
    process(shard(y_far, 2))

    rest_t = jnp.concatenate([xbuf[b, 256:272, :].astype(F32)[:8] for b in range(16)], axis=0)
    rest_x = jnp.transpose(rest_t)
    re, im = rest_x[:NIMG], rest_x[NIMG:]
    shrest[0, 0:NIMG, :] = re.astype(BF16)
    shrest[1, 0:NIMG, :] = im.astype(BF16)
    for s in range(1, NSHIFT):
        rows = slice(s * NIMG, s * NIMG + NIMG)
        cosine = crest[s - 1 : s, :]
        sine = srest[s - 1 : s, :]
        shrest[0, rows, :] = (re * cosine + im * sine).astype(BF16)
        shrest[1, rows, :] = (im * cosine - re * sine).astype(BF16)
    full = (
        score[...]
        + lax.dot_general(shrest[0], prest[0], NT, preferred_element_type=F32)
        + lax.dot_general(shrest[1], prest[1], NT, preferred_element_type=F32)
    )
    full = jnp.concatenate([full, jnp.zeros((ROWS, 128 - NPROJ), F32)], axis=1)

    tiles = []
    for t in range(5):
        if t < 4:
            tiles.append(jnp.transpose(full[t * 128 : t * 128 + 128])[:NPROJ] + base)
        else:
            last = jnp.concatenate([full[512:576], jnp.zeros((64, 128), F32)], axis=0)
            tiles.append(jnp.where(lane < 64, jnp.transpose(last)[:NPROJ] + base, -3e38))
    high = tiles[0]
    for t in range(1, 5):
        high = jnp.maximum(high, tiles[t])
    high = jnp.max(high, axis=0, keepdims=True)
    high = jnp.maximum(high, pltpu.roll(jnp.broadcast_to(high, (8, 128)), 64, 1)[:1])
    total = jnp.exp(tiles[0] - high)
    for t in range(1, 5):
        total += jnp.exp(tiles[t] - high)
    total = jnp.sum(total, axis=0, keepdims=True)
    total = total + pltpu.roll(jnp.broadcast_to(total, (8, 128)), 64, 1)[:1]
    row8 = lax.broadcasted_iota(jnp.int32, (8, 128), 0)

    def merged(blocks):
        top = blocks[0][0:1, :]
        for block in blocks[1:]:
            top = jnp.maximum(top, block[0:1, :])
        whole = jnp.zeros((1, 128), F32)
        for block in blocks:
            whole += block[1:2, :] * jnp.exp(block[0:1, :] - top)
        return top, whole

    st_copies = []
    for stage in range(2):
        mine_at = l if stage == 0 else y
        stat[stage, mine_at] = jnp.where(row8 == 0, high, total)
        for k in range(1, 4):
            to = y * 4 + lax.rem(l + k, 4) if stage == 0 else lax.rem(ref + 4 * k, 16)
            block = stat.at[stage, mine_at]
            c = copy(block, block, st_s.at[3 * stage + k - 1], st_r.at[3 * stage + k - 1], dev(ref_at=to))
            c.start()
            st_copies.append(c)
        for k in range(1, 4):
            src = lax.rem(mine_at + 4 - k, 4)
            block = stat.at[stage, src]
            come_from = y * 4 + src if stage == 0 else src * 4 + l
            copy(
                block, block, st_s.at[3 * stage + k - 1], st_r.at[3 * stage + k - 1], dev(ref_at=come_from)
            ).wait_recv()
        high, total = merged([stat[stage, b] for b in range(4)])
    evidence = high + jnp.log(total)
    ev_ref[...] = evidence
    for t in range(5):
        w = jnp.exp(tiles[t] - evidence).astype(BF16)
        if t < 4:
            wts[:, t * 128 : t * 128 + 128] = w
        else:
            wts[:, 512:576] = w[:, :64]
    members_all = jnp.concatenate([members.astype(BF16)] * 4 + [members[:, :64].astype(BF16)], axis=1)
    group_sum = lax.dot_general(members_all, wts[...], NT, preferred_element_type=F32)
    group_sum = jnp.concatenate([group_sum, jnp.zeros((GROUPS, 80), F32)], axis=1)

    other = at_img(x, h, o)
    rest_mine = jnp.dot(wts[...], shrest[d], preferred_element_type=F32)
    rest_theirs = jnp.dot(wts[...], shrest[o], preferred_element_type=F32)

    order = [ring(x + 2), ring(x + 1), ring(x + 3), x]
    runs = [ring(h + 2), ring(h + 1), ring(h + 3), h]

    def core_copy(i):
        return copy(core_out.at[i], core_in.at[i], co_s.at[i], co_r.at[i], other)

    def other_chunk(i):
        for u in range(4):
            got = jnp.dot(wts[...], smain[4 * order[i] + runs[u], o], preferred_element_type=F32)
            for v in range(2):
                r = PIECE * (2 * u + v)
                core_out[i, r : r + PIECE, :] = got[:, v * 128 : v * 128 + 128].astype(BF16)
        core_copy(i).start()

    def left(value, by):
        return pltpu.roll(value, lax.rem(256 - by, 128), 1)

    def packed(q, rest_tile, group_tile, c):
        out = left(rest_tile[0:16], 32 * q)
        out = jnp.where(lane < 32, out, left(rest_tile[16:32], 32 * q - 32))
        out = jnp.where(lane < 64, out, left(rest_tile[32:48], 32 * q - 64))
        return jnp.where(lane < 96, out, left(group_tile, 32 + 24 * c))

    def piece_row(k):
        return 16 + PIECE * k

    def rows_of(k):
        return slice(0, 16) if k < 0 else slice(piece_row(k), piece_row(k) + PIECE)

    far_copies = []
    for k in range(2):
        c = d if k == 0 else o
        for u in range(4):
            got = jnp.dot(wts[...], smain[4 * order[0] + runs[u], c], preferred_element_type=F32).astype(BF16)
            for v in range(2):
                far_out[k, rows_of(2 * u + v), :] = got[:, v * 128 : v * 128 + 128]
        rest_tile = rest_mine if k == 0 else rest_theirs
        far_out[k, 0:16, :] = packed(order[0], rest_tile, group_sum, c).astype(BF16)
        for way in range(2):
            rows = pl.ds(0, HALF) if way == 0 else pl.ds(HALF, MSG - HALF)
            land = x_near_a if way == 0 else x_near_b
            to = at_img(ring(x + 1) if way == 0 else ring(x - 1), h, c)
            far_copies.append(
                copy(far_out.at[k, rows], land.at[k], xs_s.at[2 * way + k], xs_r.at[2 * way + k], to)
            )
            far_copies[-1].start()

    rest_out[0:48, :] = rest_theirs.astype(BF16)
    rest_out[48:64, :] = group_sum.astype(BF16)
    rest_copy = copy(rest_out, rest_in, co_s.at[4], co_r.at[4], other)
    rest_copy.start()
    for i in range(1, 4):
        other_chunk(i)

    rest_copy.wait_recv()
    rest_sum = rest_mine + rest_in[0:48, :].astype(F32)
    group_sum = group_sum + rest_in[48:64, :].astype(F32)

    def own_chunk(i):
        q = order[i]
        sums = [
            jnp.dot(wts[...], smain[4 * q + runs[u], d], preferred_element_type=F32) for u in range(4)
        ]
        core_copy(i).wait_recv()
        for u in range(4):
            for v in range(2):
                k = 2 * u + v
                r = PIECE * k
                held[rows_of(k), :] = (
                    sums[u][:, v * 128 : v * 128 + 128] + core_in[i, r : r + PIECE, :].astype(F32)
                )
        held[0:16, :] = packed(q, rest_sum, group_sum, d)

    x_up, x_down = at_img(ring(x + 1), h, d), at_img(ring(x - 1), h, d)

    def near_wait(way):
        for k in range(2):
            far_copies[2 * k + way].wait_recv()

    def x_copy(way, part):
        rows = pl.ds(0, FIRST) if part == 0 else pl.ds(FIRST, MSG - FIRST)
        k = 4 + 2 * way + part
        to = x_up if way == 0 else x_down
        return copy(x_out.at[way, rows], x_in.at[way, rows], xs_s.at[k], xs_r.at[k], to)

    own_chunk(1)
    x_out[0, HALF:MSG, :] = held[HALF:MSG, :].astype(BF16)
    near_wait(0)
    x_out[0, 0:HALF, :] = (
        held[0:HALF, :] + x_near_a[0].astype(F32) + x_near_a[1].astype(F32)
    ).astype(BF16)
    x_copy(0, 0).start()
    x_copy(0, 1).start()

    own_chunk(2)
    x_out[1, 0:HALF, :] = held[0:HALF, :].astype(BF16)
    x_copy(1, 0).start()
    near_wait(1)
    x_out[1, HALF:MSG, :] = (
        held[HALF:MSG, :] + x_near_b[0].astype(F32) + x_near_b[1].astype(F32)
    ).astype(BF16)
    x_copy(1, 1).start()

    own_chunk(3)

    def add_x(part):
        rows = slice(0, FIRST) if part == 0 else slice(FIRST, MSG)
        x_copy(0, part).wait_recv()
        x_copy(1, part).wait_recv()
        held[rows, :] += x_in[0, rows, :].astype(F32) + x_in[1, rows, :].astype(F32)

    add_x(0)

    def piece_of(u, dd):
        return held[pl.ds(pl.multiple_of(16 + PIECE * (2 * u + dd), 16), PIECE), :]

    rest_pack = held[0:16, :]
    h_up, h_down = ring(h + 1), ring(h - 1)

    def fill(slot, value, extra):
        z_out[slot, 0:48, :] = value.astype(BF16)
        z_out[slot, 48:64, :] = extra.astype(BF16)

    fill(0, piece_of(0, 0), rest_pack)
    fill(1, piece_of(0, 1), rest_pack)
    relay_up = copy(z_out.at[0], z_relay.at[0], zs_s.at[0], zs_r.at[0], at_img(x, h_up, d))
    relay_down = copy(z_out.at[1], z_relay.at[1], zs_s.at[1], zs_r.at[1], at_img(x, h_down, d))
    relay_up.start()
    relay_down.start()
    add_x(1)

    def z_copy(slot):
        way, dd = (slot - 2) // 2, (slot - 2) % 2
        to = at_img(x, h_up if way == 0 else h_down, dd)
        return copy(z_out.at[slot], z_in.at[way, d], zs_s.at[slot], zs_r.at[2 + 2 * way + d], to)

    fill(3, piece_of(1, 1), rest_pack)
    z_copy(3).start()
    fill(4, piece_of(2, 0), rest_pack)
    z_copy(4).start()
    fill(6, piece_of(3, o), rest_pack)
    core_last = copy(z_out.at[6], z_core, zs_s.at[6], zs_r.at[6], other)
    core_last.start()
    relay_up.wait_recv()
    fill(
        2,
        piece_of(1, 0) + z_relay[0, 0:48, :].astype(F32),
        rest_pack + z_relay[0, 48:64, :].astype(F32),
    )
    z_copy(2).start()
    relay_down.wait_recv()
    fill(
        5,
        piece_of(2, 1) + z_relay[1, 0:48, :].astype(F32),
        rest_pack + z_relay[1, 48:64, :].astype(F32),
    )
    z_copy(5).start()

    mine = jnp.concatenate([piece_of(3, d), rest_pack], axis=0)
    core_last.wait_recv()
    theirs = z_core[...].astype(F32)
    for way in range(2):
        for c in range(2):
            slot = z_in.at[way, c]
            copy(slot, slot, zs_s.at[2], zs_r.at[2 + 2 * way + c], other).wait_recv()
    local = 2 * h + d
    packs = []
    for c in range(2):
        both = jnp.where(d == c, mine, theirs)
        both = both + z_in[0, c].astype(F32) + z_in[1, c].astype(F32)
        cls_ref[c, :, 0:128] = both[0:48]
        pack = both[48:64]
        packs.append(pack)
        for a in range(3):
            cls_ref[c, 16 * a : 16 * a + 16, 128:256] = left(pack, 32 * a + 4 * local)
    group_all = jnp.where(lane < 24, left(packs[0], 96), left(packs[1], 72))
    group_out[...] = jnp.where(lane < 48, group_all, 0.0)

    for e in range(4):
        for part in range(2):
            if e:
                z_send(e, part).wait_send()
            for way in range(2):
                y_copy(way, e, y, part).wait_send()
        for way in range(2):
            f_copy(way, e, y).wait_send()
    for c in st_copies:
        c.wait_send()
    for i in range(1, 4):
        core_copy(i).wait_send()
    for c in far_copies:
        c.wait_send()
    for c in (rest_copy, relay_up, relay_down, core_last):
        c.wait_send()
    for way in range(2):
        for part in range(2):
            x_copy(way, part).wait_send()
    for slot in range(2, 6):
        z_copy(slot).wait_send()


def finish(
    cls_hbm, group_hbm, gain_hbm, ev_hbm, cls_out, con_out, ev_out, cls_ref, group_ref, gain_ref, ev_ref, in_s
):
    loads = [
        pltpu.make_async_copy(src, dst, in_s.at[k])
        for k, (src, dst) in enumerate(
            ((cls_hbm, cls_ref), (group_hbm, group_ref), (gain_hbm, gain_ref), (ev_hbm, ev_ref))
        )
    ]
    for load in loads:
        load.start()
    for load in loads:
        load.wait()
    for c in range(2):
        cls_out[:, c, :] = cls_ref[c, :, 0:132]
    column = jnp.transpose(jnp.concatenate([group_ref[...], jnp.zeros((112, 128), F32)], axis=0))
    con_out[...] = jnp.dot(
        column[:NPROJ, :GROUPS], gain_ref[...], precision=HIGHEST, preferred_element_type=F32
    )[:, :132]
    ev_out[...] = ev_ref[:, :NIMG]


def on_device(
    images, projections, contrast_curve, noise_weight, defocus_group, shifts, orient_index, orient_prior
):
    vmem = pl.BlockSpec(memory_space=pltpu.VMEM)
    sem = pltpu.SemaphoreType.DMA
    hbm = pl.BlockSpec(memory_space=pl.ANY)
    held = pl.pallas_call(
        body,
        out_shape=(
            jax.ShapeDtypeStruct((2, NPROJ, 256), F32),
            jax.ShapeDtypeStruct((GROUPS, 128), F32),
            jax.ShapeDtypeStruct((GROUPS, 256), F32),
            jax.ShapeDtypeStruct((1, 128), F32),
        ),
        in_specs=[hbm] * 8,
        out_specs=(vmem,) * 4,
        scratch_shapes=[
            pltpu.VMEM((NIMG, 2, 264), BF16),
            pltpu.VMEM((GROUPS, NPIX), F32),
            pltpu.VMEM((NPIX // 128, 128), F32),
            pltpu.VMEM((1, NIMG), jnp.int32),
            pltpu.SMEM((2, NSHIFT), jnp.int32),
            pltpu.VMEM((NPROJ, 2, NPIX), BF16),
            pltpu.VMEM((2, NPROJ, NPIX), BF16),
            pltpu.VMEM((1, NPROJ), jnp.int32),
            pltpu.VMEM((2, 128), F32),
            pltpu.VMEM((16, SHARD, 128), BF16),
            pltpu.VMEM((16, 2, NPROJ, 256), BF16),
            pltpu.VMEM((2, NPROJ, 128), BF16),
            pltpu.VMEM((16, 8, 256), F32),
            pltpu.VMEM((16, 8, 256), F32),
            pltpu.VMEM((8, 128), F32),
            pltpu.VMEM((8, 128), F32),
            pltpu.VMEM((16, 2, ROWS, 256), BF16),
            pltpu.VMEM((2, ROWS, 128), BF16),
            pltpu.VMEM((ROWS, NPROJ), F32),
            pltpu.VMEM((NPROJ, ROWS), BF16),
            pltpu.VMEM((2, 4, 8, 128), F32),
            pltpu.VMEM((4, 8 * PIECE, 128), BF16),
            pltpu.VMEM((4, 8 * PIECE, 128), BF16),
            pltpu.VMEM((64, 128), BF16),
            pltpu.VMEM((64, 128), BF16),
            pltpu.VMEM((2, MSG, 128), BF16),
            pltpu.VMEM((2, MSG, 128), BF16),
            pltpu.VMEM((2, HALF, 128), BF16),
            pltpu.VMEM((2, MSG - HALF, 128), BF16),
            pltpu.VMEM((2, MSG, 128), BF16),
            pltpu.VMEM((MSG, 128), F32),
            pltpu.VMEM((7, 64, 128), BF16),
            pltpu.VMEM((2, 64, 128), BF16),
            pltpu.VMEM((2, 2, 64, 128), BF16),
            pltpu.VMEM((64, 128), BF16),
            sem((4, 2)),
            sem((4, 2)),
            sem((2, 4, 2)),
            sem((2, 4, 2)),
            sem((2, 4)),
            sem((2, 4)),
            sem((6,)),
            sem((6,)),
            sem((5,)),
            sem((5,)),
            sem((8,)),
            sem((8,)),
            sem((7,)),
            sem((7,)),
            sem((8,)),
        ],
        compiler_params=pltpu.CompilerParams(
            collective_id=0, has_side_effects=True, vmem_limit_bytes=60 * 1024 * 1024
        ),
        name="expectation",
    )(
        images,
        projections,
        contrast_curve,
        noise_weight.reshape(NPIX // 128, 128),
        defocus_group.reshape(1, NIMG),
        shifts.T,
        orient_index.reshape(1, NPROJ),
        orient_prior.reshape(2, 128),
    )
    cls, con, ev = pl.pallas_call(
        finish,
        out_shape=(
            jax.ShapeDtypeStruct((NPROJ, 2, 132), F32),
            jax.ShapeDtypeStruct((NPROJ, 132), F32),
            jax.ShapeDtypeStruct((1, NIMG), F32),
        ),
        in_specs=[hbm] * 4,
        out_specs=(vmem,) * 3,
        scratch_shapes=[
            pltpu.VMEM((2, NPROJ, 256), F32),
            pltpu.VMEM((GROUPS, 128), F32),
            pltpu.VMEM((GROUPS, 256), F32),
            pltpu.VMEM((1, 128), F32),
            sem((4,)),
        ],
        compiler_params=pltpu.CompilerParams(vmem_limit_bytes=60 * 1024 * 1024),
        name="finish",
    )(*held)
    return cls, con, ev.reshape(NIMG)


def solution(mesh):
    in_specs = (P("img", None, "ref"), P("ref", None, None), P(), P(), P("img"), P(), P("ref"), P())
    out_specs = (P("ref", None, "img"), P("ref", "img"), P("img"))
    return jax.shard_map(
        on_device, mesh=mesh, in_specs=in_specs, out_specs=out_specs, check_vma=False
    )
```

```python
import math

import jax
import jax.numpy as jnp
from jax import lax
from jax.experimental import pallas as pl
from jax.experimental.pallas import tpu as pltpu
from jax.sharding import PartitionSpec as P

MESH = pl.DeviceIdType.MESH
F32 = jnp.float32
BF16 = jnp.bfloat16
HIGHEST = lax.Precision.HIGHEST
NT = (((1,), (1,)), ((), ()))
TN = (((0,), (0,)), ((), ()))

NPIX = 4224
BOX = 128
NSHIFT = 9
NIMG = 64
NPROJ = 48
GROUPS = 16
ROWS = NSHIFT * NIMG
SHARD = 272
PIECE = 48
MSG = 400
HALF = 208
FIRST = 112


def sincos(steps):
    quadrant = lax.shift_right_arithmetic(steps + 16, 5)
    rest = (steps - quadrant * 32).astype(F32) * (2.0 * math.pi / BOX)
    sq = rest * rest
    sin_part = rest * (
        1.0 + sq * (-1.0 / 6 + sq * (1.0 / 120 + sq * (-1.0 / 5040 + sq * (1.0 / 362880))))
    )
    cos_part = 1.0 + sq * (
        -0.5 + sq * (1.0 / 24 + sq * (-1.0 / 720 + sq * (1.0 / 40320 - sq * (1.0 / 3628800))))
    )
    odd = (quadrant & 1) == 1
    flip_sin = (quadrant & 2) == 2
    flip_cos = ((quadrant + 1) & 2) == 2
    sine = jnp.where(odd, cos_part, sin_part)
    cosine = jnp.where(odd, sin_part, cos_part)
    return jnp.where(flip_cos, -cosine, cosine), jnp.where(flip_sin, -sine, sine)


def body(
    img_hbm,
    proj_hbm,
    curve_hbm,
    noise_hbm,
    group_hbm,
    shift_hbm,
    orient_hbm,
    prior_hbm,
    cls_ref,
    group_out,
    gain_out,
    ev_ref,
    img_ref,
    curve_ref,
    noise_ref,
    group_ref,
    shift_ref,
    proj_ref,
    planes,
    orient_ref,
    prior_ref,
    xbuf,
    pmain,
    prest,
    ctab,
    stab,
    crest,
    srest,
    smain,
    shrest,
    score,
    wts,
    stat,
    core_out,
    core_in,
    rest_out,
    rest_in,
    far_out,
    x_out,
    x_near_a,
    x_near_b,
    x_in,
    held,
    z_out,
    z_relay,
    z_in,
    z_core,
    ag_z_s,
    ag_z_r,
    ag_y_s,
    ag_y_r,
    ag_f_s,
    ag_f_r,
    st_s,
    st_r,
    co_s,
    co_r,
    xs_s,
    xs_r,
    zs_s,
    zs_r,
    in_s,
):
    img = lax.axis_index("img")
    ref = lax.axis_index("ref")
    x = lax.div(img, 8)
    h = lax.rem(lax.div(img, 2), 4)
    d = lax.rem(img, 2)
    o = 1 - d
    y = lax.div(ref, 4)
    l = lax.rem(ref, 4)

    def ring(v):
        return lax.rem(v + 4, 4)

    def dev(img_at=img, ref_at=ref):
        return {"img": img_at, "ref": ref_at}

    def at_img(xx, hh, dd):
        return dev(img_at=(xx * 4 + hh) * 2 + dd)

    def copy(src, dst, send, recv, to):
        return pltpu.make_async_remote_copy(
            src_ref=src, dst_ref=dst, send_sem=send, recv_sem=recv, device_id=to, device_id_type=MESH
        )

    barrier = pltpu.get_barrier_semaphore()
    peers = [dev(ref_at=y * 4 + lax.rem(l + k, 4)) for k in range(1, 4)]
    peers += [dev(ref_at=lax.rem(ref + 4 * k, 16)) for k in range(1, 4)]
    peers += [at_img(x, h, o), at_img(ring(x + 1), h, d), at_img(ring(x - 1), h, d)]
    peers += [at_img(ring(x + 1), h, o), at_img(ring(x - 1), h, o)]
    for hh in (ring(h + 1), ring(h - 1)):
        peers += [at_img(x, hh, d), at_img(x, hh, o)]
    for peer in peers:
        pl.semaphore_signal(barrier, inc=1, device_id=peer, device_id_type=MESH)

    loads = [
        pltpu.make_async_copy(src, dst, in_s.at[k])
        for k, (src, dst) in enumerate(
            (
                (group_hbm, group_ref),
                (curve_hbm, curve_ref),
                (noise_hbm, noise_ref),
                (img_hbm, img_ref),
                (shift_hbm, shift_ref),
                (proj_hbm, proj_ref),
                (orient_hbm, orient_ref),
                (prior_hbm, prior_ref),
            )
        )
    ]
    for load in loads:
        load.start()
    for load in loads[:4]:
        load.wait()

    lane = lax.broadcasted_iota(jnp.int32, (1, 128), 1)

    def noise_row(tile, count):
        return jnp.concatenate([noise_ref[pl.ds(tile + t, 1), :] for t in range(count)], axis=1)


    group_row = group_ref[...].astype(F32)
    group_row = jnp.concatenate([group_row, group_row], axis=1)
    group_col = jnp.transpose(jnp.broadcast_to(group_row, (128, 128)))[:NIMG, :]
    start = pl.multiple_of(ref * 256, 128)
    turn = lax.rem(384 - 8 * ref, 384)
    curve_here = pltpu.roll(curve_ref[:, pl.ds(start, 384)], turn, 1)
    noise_here = pltpu.roll(jnp.broadcast_to(noise_row(2 * ref, 3), (8, 384)), turn, 1)[:1, :]
    parts = []
    for tile in range(3):
        span = slice(tile * 128, tile * 128 + 128)
        gain = jnp.zeros((NIMG, 128), F32)
        for g in range(GROUPS):
            gain = jnp.where(group_col == float(g), curve_here[g : g + 1, span], gain)
        gain = gain * noise_here[:, span]
        both = []
        for c in range(2):
            if tile < 2:
                pixels = img_ref[:, c, span].astype(F32)
            else:
                pixels = img_ref[:, c, 256:264].astype(F32)
                pixels = jnp.concatenate([pixels, jnp.zeros((NIMG, 120), F32)], axis=1)
            both.append(pixels * gain)
        parts.append(jnp.concatenate(both, axis=0))
    second = pltpu.roll(jnp.concatenate(parts[1:], axis=1), 252, 1)[:, :128]
    rest = jnp.transpose(jnp.where(lane < 4, parts[1], parts[2]))[:16, :]
    row16 = lax.broadcasted_iota(jnp.int32, (16, 128), 0)
    rest = jnp.where(row16 < 8, rest, 0.0)
    xbuf[ref, 0:128, :] = parts[0].astype(BF16)
    xbuf[ref, 128:256, :] = second.astype(BF16)
    xbuf[ref, 256:272, :] = rest.astype(BF16)

    pl.semaphore_wait(barrier, len(peers))

    columns = [lax.rem(l + 4 - e, 4) for e in range(4)]
    halves = (pl.ds(0, 144), pl.ds(144, 128))

    def shard(yy, e):
        return yy * 4 + columns[e]

    def z_send(e, part):
        block = xbuf.at[ref, halves[part]]
        to = dev(ref_at=y * 4 + lax.rem(l + e, 4))
        return copy(block, block, ag_z_s.at[e, part], ag_z_r.at[e, part], to)

    y_up, y_down, y_far = ring(y + 1), ring(y - 1), ring(y + 2)

    def y_copy(way, e, src_y, part):
        to = dev(ref_at=(y_up if way == 0 else y_down) * 4 + l)
        block = xbuf.at[shard(src_y, e), halves[part]]
        return copy(block, block, ag_y_s.at[way, e, part], ag_y_r.at[way, e, part], to)

    def f_copy(way, e, src_y):
        to = dev(ref_at=(y_up if way == 0 else y_down) * 4 + l)
        block = xbuf.at[shard(src_y, e), halves[way]]
        return copy(block, block, ag_f_s.at[way, e], ag_f_r.at[way, e], to)

    def send_y(e, part):
        for way in (part, 1 - part):
            y_copy(way, e, y, part).start()

    def near_z():
        for part in range(2):
            z_send(1, part).start()
            z_send(3, part).start()

    @pl.when(d == 0)
    def _():
        near_z()

    send_y(0, 0)
    send_y(0, 1)

    def take_z(e, part):
        block = xbuf.at[shard(y, e), halves[part]]
        copy(block, block, ag_z_s.at[e, part], ag_z_r.at[e, part], dev(ref_at=shard(y, e))).wait_recv()
        send_y(e, part)

    def take_y(e):
        y_copy(0, e, y_down, 0).wait_recv()
        f_copy(0, e, y_down).start()
        y_copy(1, e, y_up, 1).wait_recv()
        f_copy(1, e, y_up).start()
        y_copy(0, e, y_down, 1).wait_recv()
        y_copy(1, e, y_up, 0).wait_recv()

    def take_far(e):
        f_copy(0, e, y_far).wait_recv()
        f_copy(1, e, y_far).wait_recv()

    loads[4].wait()

    def table(pixel, width):
        srow = lax.broadcasted_iota(jnp.int32, (8, width), 0) + 1
        move_x = jnp.zeros((8, width), jnp.int32)
        move_y = jnp.zeros((8, width), jnp.int32)
        for s in range(1, NSHIFT):
            move_x = jnp.where(srow == s, shift_ref[0, s], move_x)
            move_y = jnp.where(srow == s, shift_ref[1, s], move_y)
        freq_x = pixel & (BOX // 2 - 1)
        freq_y = lax.shift_right_logical(pixel, 6) - NPIX // BOX
        return sincos((move_x * freq_x + move_y * freq_y) & (BOX - 1))

    def table_step(b, carry):
        at = lax.broadcasted_iota(jnp.int32, (8, 256), 1)
        pixel = 264 * b + at + jnp.where(at >= 128, 4, 0)
        cosine, sine = table(pixel, 256)
        ctab[b] = cosine
        stab[b] = sine
        return carry

    lax.fori_loop(0, 16, table_step, 0)
    at = lax.broadcasted_iota(jnp.int32, (8, 128), 1)
    cosine, sine = table(132 * lax.shift_right_logical(at, 2) + 128 + (at & 3), 128)
    crest[...] = cosine
    srest[...] = sine

    @pl.when(d == 1)
    def _():
        near_z()

    @pl.when(d == 0)
    def _():
        for part in range(2):
            z_send(2, part).start()

    for load in loads[5:]:
        load.wait()

    def plane_step(t, carry):
        span = pl.ds(pl.multiple_of(t * 384, 128), 384)
        for c in range(2):
            planes[c, :, span] = proj_ref[:, c, span]
        return carry

    lax.fori_loop(0, 11, plane_step, 0)

    @pl.when(d == 1)
    def _():
        for part in range(2):
            z_send(2, part).start()

    take_y(0)


    def proj_step(b, carry):
        out = []
        for c in range(2):
            kept = carry[c]
            for u in range(2):
                n = 2 * b + u
                window = planes[c, :, pl.ds(pl.multiple_of(n * 128, 128), 256)].astype(F32)
                turned = pltpu.roll(window, lax.rem(256 - 4 * n, 256), 1)
                pmain[b, c, :, u * 128 : u * 128 + 128] = turned[:, :128].astype(BF16)
                kept = jnp.where(lax.shift_right_logical(lane, 2) == n, window[:, 128:], kept)
            out.append(kept)
        return tuple(out)

    zero_rest = jnp.zeros((NPROJ, 128), F32)
    rests = lax.fori_loop(0, 8, proj_step, (zero_rest, zero_rest))
    for part in range(2):
        take_z(1, part)
        take_z(3, part)
    rests = lax.fori_loop(8, 16, proj_step, rests)
    for c in range(2):
        prest[c] = rests[c].astype(BF16)


    def norm_step(t, total):
        span = pl.ds(pl.multiple_of(t * 384, 128), 384)
        re = planes[0, :, span].astype(F32)
        im = planes[1, :, span].astype(F32)
        curve = curve_ref[:, span]
        gain = 0.5 * (curve * curve * noise_row(3 * t, 3))
        power = re * re + im * im
        return total + lax.dot_general(
            two_parts(power), two_parts(gain), NT, preferred_element_type=F32
        )

    def two_parts(value):
        high = value.astype(BF16)
        return jnp.concatenate([high, (value - high.astype(F32)).astype(BF16)], axis=0)

    norm = lax.fori_loop(0, 11, norm_step, jnp.zeros((2 * NPROJ, 2 * GROUPS), F32))
    norm = norm[:NPROJ] + norm[NPROJ:]
    norm = norm[:, :GROUPS] + norm[:, GROUPS:]
    grow = lax.broadcasted_iota(jnp.int32, (GROUPS, 128), 0)
    members = (group_row == grow.astype(F32)).astype(F32)
    penalty = jnp.dot(norm, members, precision=HIGHEST, preferred_element_type=F32)
    orient_row = jnp.concatenate([orient_ref[...].astype(F32), jnp.zeros((1, 80), F32)], axis=1)
    orient_col = jnp.transpose(jnp.broadcast_to(orient_row, (128, 128)))[:NPROJ, :]
    prior = jnp.zeros((NPROJ, 1), F32)
    for half in range(2):
        hit = orient_col == (lane + half * 128).astype(F32)
        prior += jnp.sum(
            jnp.where(hit, prior_ref[half : half + 1, :], 0.0), axis=1, keepdims=True
        )
    base = prior - penalty
    span = pl.ds(pl.multiple_of(img * 128, 128), 256)
    curve = curve_ref[:, span]
    gain_out[...] = pltpu.roll(curve * curve * noise_row(img, 2), lax.rem(256 - 4 * img, 256), 1)

    score[...] = jnp.zeros_like(score)

    def process(b):
        for t in range(2):
            span = slice(t * 128, t * 128 + 128)
            re = xbuf[b, t * 128 : t * 128 + 64, :]
            im = xbuf[b, t * 128 + 64 : t * 128 + 128, :]
            smain[b, 0, 0:NIMG, span] = re
            smain[b, 1, 0:NIMG, span] = im
            re = re.astype(F32)
            im = im.astype(F32)
            for s in range(1, NSHIFT):
                rows = slice(s * NIMG, s * NIMG + NIMG)
                cosine = ctab[b, s - 1 : s, span]
                sine = stab[b, s - 1 : s, span]
                smain[b, 0, rows, span] = (re * cosine + im * sine).astype(BF16)
                smain[b, 1, rows, span] = (im * cosine - re * sine).astype(BF16)
        score[...] += lax.dot_general(
            smain[b, 0], pmain[b, 0], NT, preferred_element_type=F32
        ) + lax.dot_general(smain[b, 1], pmain[b, 1], NT, preferred_element_type=F32)

    def process_all(blocks):
        def step(t, carry):
            b = blocks[0]
            for k in range(1, len(blocks)):
                b = jnp.where(t == k, blocks[k], b)
            process(b)
            return carry

        lax.fori_loop(0, len(blocks), step, 0)

    take_z(2, 0)
    take_z(2, 1)
    process_all([shard(y, 0), shard(y, 1)])
    take_y(1)
    process_all([shard(y_down, 0), shard(y_up, 0)])
    take_far(0)
    take_y(3)
    process_all([shard(y_far, 0), shard(y, 3), shard(y_down, 1)])
    take_y(2)
    process_all([shard(y_up, 1), shard(y, 2), shard(y_down, 3), shard(y_up, 3)])
    take_far(1)
    process_all([shard(y_far, 1), shard(y_down, 2), shard(y_up, 2)])
    take_far(3)
    process(shard(y_far, 3))
    take_far(2)
    process(shard(y_far, 2))

    rest_t = jnp.concatenate([xbuf[b, 256:272, :].astype(F32)[:8] for b in range(16)], axis=0)
    rest_x = jnp.transpose(rest_t)
    re, im = rest_x[:NIMG], rest_x[NIMG:]
    shrest[0, 0:NIMG, :] = re.astype(BF16)
    shrest[1, 0:NIMG, :] = im.astype(BF16)
    for s in range(1, NSHIFT):
        rows = slice(s * NIMG, s * NIMG + NIMG)
        cosine = crest[s - 1 : s, :]
        sine = srest[s - 1 : s, :]
        shrest[0, rows, :] = (re * cosine + im * sine).astype(BF16)
        shrest[1, rows, :] = (im * cosine - re * sine).astype(BF16)
    full = (
        score[...]
        + lax.dot_general(shrest[0], prest[0], NT, preferred_element_type=F32)
        + lax.dot_general(shrest[1], prest[1], NT, preferred_element_type=F32)
    )
    full = jnp.concatenate([full, jnp.zeros((ROWS, 128 - NPROJ), F32)], axis=1)

    tiles = []
    for t in range(5):
        if t < 4:
            tiles.append(jnp.transpose(full[t * 128 : t * 128 + 128])[:NPROJ] + base)
        else:
            last = jnp.concatenate([full[512:576], jnp.zeros((64, 128), F32)], axis=0)
            tiles.append(jnp.where(lane < 64, jnp.transpose(last)[:NPROJ] + base, -3e38))
    high = tiles[0]
    for t in range(1, 5):
        high = jnp.maximum(high, tiles[t])
    high = jnp.max(high, axis=0, keepdims=True)
    high = jnp.maximum(high, pltpu.roll(jnp.broadcast_to(high, (8, 128)), 64, 1)[:1])
    total = jnp.exp(tiles[0] - high)
    for t in range(1, 5):
        total += jnp.exp(tiles[t] - high)
    total = jnp.sum(total, axis=0, keepdims=True)
    total = total + pltpu.roll(jnp.broadcast_to(total, (8, 128)), 64, 1)[:1]
    row8 = lax.broadcasted_iota(jnp.int32, (8, 128), 0)

    def merged(blocks):
        top = blocks[0][0:1, :]
        for block in blocks[1:]:
            top = jnp.maximum(top, block[0:1, :])
        whole = jnp.zeros((1, 128), F32)
        for block in blocks:
            whole += block[1:2, :] * jnp.exp(block[0:1, :] - top)
        return top, whole

    st_copies = []
    for stage in range(2):
        mine_at = l if stage == 0 else y
        stat[stage, mine_at] = jnp.where(row8 == 0, high, total)
        for k in range(1, 4):
            to = y * 4 + lax.rem(l + k, 4) if stage == 0 else lax.rem(ref + 4 * k, 16)
            block = stat.at[stage, mine_at]
            c = copy(block, block, st_s.at[3 * stage + k - 1], st_r.at[3 * stage + k - 1], dev(ref_at=to))
            c.start()
            st_copies.append(c)
        for k in range(1, 4):
            src = lax.rem(mine_at + 4 - k, 4)
            block = stat.at[stage, src]
            come_from = y * 4 + src if stage == 0 else src * 4 + l
            copy(
                block, block, st_s.at[3 * stage + k - 1], st_r.at[3 * stage + k - 1], dev(ref_at=come_from)
            ).wait_recv()
        high, total = merged([stat[stage, b] for b in range(4)])
    evidence = high + jnp.log(total)
    ev_ref[...] = evidence
    for t in range(5):
        w = jnp.exp(tiles[t] - evidence).astype(BF16)
        if t < 4:
            wts[:, t * 128 : t * 128 + 128] = w
        else:
            wts[:, 512:576] = w[:, :64]
    members_all = jnp.concatenate([members.astype(BF16)] * 4 + [members[:, :64].astype(BF16)], axis=1)
    group_sum = lax.dot_general(members_all, wts[...], NT, preferred_element_type=F32)
    group_sum = jnp.concatenate([group_sum, jnp.zeros((GROUPS, 80), F32)], axis=1)

    other = at_img(x, h, o)
    rest_mine = jnp.dot(wts[...], shrest[d], preferred_element_type=F32)
    rest_theirs = jnp.dot(wts[...], shrest[o], preferred_element_type=F32)

    order = [ring(x + 2), ring(x + 1), ring(x + 3), x]
    runs = [ring(h + 2), ring(h + 1), ring(h + 3), h]

    def core_copy(i):
        return copy(core_out.at[i], core_in.at[i], co_s.at[i], co_r.at[i], other)

    def other_chunk(i):
        for u in range(4):
            got = jnp.dot(wts[...], smain[4 * order[i] + runs[u], o], preferred_element_type=F32)
            for v in range(2):
                r = PIECE * (2 * u + v)
                core_out[i, r : r + PIECE, :] = got[:, v * 128 : v * 128 + 128].astype(BF16)
        core_copy(i).start()

    def left(value, by):
        return pltpu.roll(value, lax.rem(256 - by, 128), 1)

    def packed(q, rest_tile, group_tile, c):
        out = left(rest_tile[0:16], 32 * q)
        out = jnp.where(lane < 32, out, left(rest_tile[16:32], 32 * q - 32))
        out = jnp.where(lane < 64, out, left(rest_tile[32:48], 32 * q - 64))
        return jnp.where(lane < 96, out, left(group_tile, 32 + 24 * c))

    def piece_row(k):
        return 16 + PIECE * k

    def rows_of(k):
        return slice(0, 16) if k < 0 else slice(piece_row(k), piece_row(k) + PIECE)

    far_copies = []
    for k in range(2):
        c = d if k == 0 else o
        for u in range(4):
            got = jnp.dot(wts[...], smain[4 * order[0] + runs[u], c], preferred_element_type=F32).astype(BF16)
            for v in range(2):
                far_out[k, rows_of(2 * u + v), :] = got[:, v * 128 : v * 128 + 128]
        rest_tile = rest_mine if k == 0 else rest_theirs
        far_out[k, 0:16, :] = packed(order[0], rest_tile, group_sum, c).astype(BF16)
        for way in range(2):
            rows = pl.ds(0, HALF) if way == 0 else pl.ds(HALF, MSG - HALF)
            land = x_near_a if way == 0 else x_near_b
            to = at_img(ring(x + 1) if way == 0 else ring(x - 1), h, c)
            far_copies.append(
                copy(far_out.at[k, rows], land.at[k], xs_s.at[2 * way + k], xs_r.at[2 * way + k], to)
            )
            far_copies[-1].start()

    rest_out[0:48, :] = rest_theirs.astype(BF16)
    rest_out[48:64, :] = group_sum.astype(BF16)
    rest_copy = copy(rest_out, rest_in, co_s.at[4], co_r.at[4], other)
    rest_copy.start()
    for i in range(1, 4):
        other_chunk(i)

    rest_copy.wait_recv()
    rest_sum = rest_mine + rest_in[0:48, :].astype(F32)
    group_sum = group_sum + rest_in[48:64, :].astype(F32)

    def own_chunk(i):
        q = order[i]
        sums = [
            jnp.dot(wts[...], smain[4 * q + runs[u], d], preferred_element_type=F32) for u in range(4)
        ]
        core_copy(i).wait_recv()
        for u in range(4):
            for v in range(2):
                k = 2 * u + v
                r = PIECE * k
                held[rows_of(k), :] = (
                    sums[u][:, v * 128 : v * 128 + 128] + core_in[i, r : r + PIECE, :].astype(F32)
                )
        held[0:16, :] = packed(q, rest_sum, group_sum, d)

    x_up, x_down = at_img(ring(x + 1), h, d), at_img(ring(x - 1), h, d)

    def near_wait(way):
        for k in range(2):
            far_copies[2 * k + way].wait_recv()

    def x_copy(way, part):
        rows = pl.ds(0, FIRST) if part == 0 else pl.ds(FIRST, MSG - FIRST)
        k = 4 + 2 * way + part
        to = x_up if way == 0 else x_down
        return copy(x_out.at[way, rows], x_in.at[way, rows], xs_s.at[k], xs_r.at[k], to)

    own_chunk(1)
    x_out[0, HALF:MSG, :] = held[HALF:MSG, :].astype(BF16)
    near_wait(0)
    x_out[0, 0:HALF, :] = (
        held[0:HALF, :] + x_near_a[0].astype(F32) + x_near_a[1].astype(F32)
    ).astype(BF16)
    x_copy(0, 0).start()
    x_copy(0, 1).start()

    own_chunk(2)
    x_out[1, 0:HALF, :] = held[0:HALF, :].astype(BF16)
    x_copy(1, 0).start()
    near_wait(1)
    x_out[1, HALF:MSG, :] = (
        held[HALF:MSG, :] + x_near_b[0].astype(F32) + x_near_b[1].astype(F32)
    ).astype(BF16)
    x_copy(1, 1).start()

    own_chunk(3)

    def add_x(part):
        rows = slice(0, FIRST) if part == 0 else slice(FIRST, MSG)
        x_copy(0, part).wait_recv()
        x_copy(1, part).wait_recv()
        held[rows, :] += x_in[0, rows, :].astype(F32) + x_in[1, rows, :].astype(F32)

    add_x(0)

    def piece_of(u, dd):
        return held[pl.ds(pl.multiple_of(16 + PIECE * (2 * u + dd), 16), PIECE), :]

    rest_pack = held[0:16, :]
    h_up, h_down = ring(h + 1), ring(h - 1)

    def fill(slot, value, extra):
        z_out[slot, 0:48, :] = value.astype(BF16)
        z_out[slot, 48:64, :] = extra.astype(BF16)

    fill(0, piece_of(0, 0), rest_pack)
    fill(1, piece_of(0, 1), rest_pack)
    relay_up = copy(z_out.at[0], z_relay.at[0], zs_s.at[0], zs_r.at[0], at_img(x, h_up, d))
    relay_down = copy(z_out.at[1], z_relay.at[1], zs_s.at[1], zs_r.at[1], at_img(x, h_down, d))
    relay_up.start()
    relay_down.start()
    add_x(1)

    def z_copy(slot):
        way, dd = (slot - 2) // 2, (slot - 2) % 2
        to = at_img(x, h_up if way == 0 else h_down, dd)
        return copy(z_out.at[slot], z_in.at[way, d], zs_s.at[slot], zs_r.at[2 + 2 * way + d], to)

    fill(3, piece_of(1, 1), rest_pack)
    z_copy(3).start()
    fill(4, piece_of(2, 0), rest_pack)
    z_copy(4).start()
    fill(6, piece_of(3, o), rest_pack)
    core_last = copy(z_out.at[6], z_core, zs_s.at[6], zs_r.at[6], other)
    core_last.start()
    relay_up.wait_recv()
    fill(
        2,
        piece_of(1, 0) + z_relay[0, 0:48, :].astype(F32),
        rest_pack + z_relay[0, 48:64, :].astype(F32),
    )
    z_copy(2).start()
    relay_down.wait_recv()
    fill(
        5,
        piece_of(2, 1) + z_relay[1, 0:48, :].astype(F32),
        rest_pack + z_relay[1, 48:64, :].astype(F32),
    )
    z_copy(5).start()

    mine = jnp.concatenate([piece_of(3, d), rest_pack], axis=0)
    core_last.wait_recv()
    theirs = z_core[...].astype(F32)
    for way in range(2):
        for c in range(2):
            slot = z_in.at[way, c]
            copy(slot, slot, zs_s.at[2], zs_r.at[2 + 2 * way + c], other).wait_recv()
    local = 2 * h + d
    packs = []
    for c in range(2):
        both = jnp.where(d == c, mine, theirs)
        both = both + z_in[0, c].astype(F32) + z_in[1, c].astype(F32)
        cls_ref[c, :, 0:128] = both[0:48]
        pack = both[48:64]
        packs.append(pack)
        for a in range(3):
            cls_ref[c, 16 * a : 16 * a + 16, 128:256] = left(pack, 32 * a + 4 * local)
    group_all = jnp.where(lane < 24, left(packs[0], 96), left(packs[1], 72))
    group_out[...] = jnp.where(lane < 48, group_all, 0.0)

    for e in range(4):
        for part in range(2):
            if e:
                z_send(e, part).wait_send()
            for way in range(2):
                y_copy(way, e, y, part).wait_send()
        for way in range(2):
            f_copy(way, e, y).wait_send()
    for c in st_copies:
        c.wait_send()
    for i in range(1, 4):
        core_copy(i).wait_send()
    for c in far_copies:
        c.wait_send()
    for c in (rest_copy, relay_up, relay_down, core_last):
        c.wait_send()
    for way in range(2):
        for part in range(2):
            x_copy(way, part).wait_send()
    for slot in range(2, 6):
        z_copy(slot).wait_send()


def finish(
    cls_hbm, group_hbm, gain_hbm, ev_hbm, cls_out, con_out, ev_out, cls_ref, group_ref, gain_ref, ev_ref, in_s
):
    loads = [
        pltpu.make_async_copy(src, dst, in_s.at[k])
        for k, (src, dst) in enumerate(
            ((cls_hbm, cls_ref), (group_hbm, group_ref), (gain_hbm, gain_ref), (ev_hbm, ev_ref))
        )
    ]
    for load in loads:
        load.start()
    for load in loads:
        load.wait()
    for c in range(2):
        cls_out[:, c, :] = cls_ref[c, :, 0:132]
    column = jnp.transpose(jnp.concatenate([group_ref[...], jnp.zeros((112, 128), F32)], axis=0))
    con_out[...] = jnp.dot(
        column[:NPROJ, :GROUPS], gain_ref[...], precision=HIGHEST, preferred_element_type=F32
    )[:, :132]
    ev_out[...] = ev_ref[:, :NIMG]


def on_device(
    images, projections, contrast_curve, noise_weight, defocus_group, shifts, orient_index, orient_prior
):
    vmem = pl.BlockSpec(memory_space=pltpu.VMEM)
    sem = pltpu.SemaphoreType.DMA
    hbm = pl.BlockSpec(memory_space=pl.ANY)
    held = pl.pallas_call(
        body,
        out_shape=(
            jax.ShapeDtypeStruct((2, NPROJ, 256), F32),
            jax.ShapeDtypeStruct((GROUPS, 128), F32),
            jax.ShapeDtypeStruct((GROUPS, 256), F32),
            jax.ShapeDtypeStruct((1, 128), F32),
        ),
        in_specs=[hbm] * 8,
        out_specs=(vmem,) * 4,
        scratch_shapes=[
            pltpu.VMEM((NIMG, 2, 264), BF16),
            pltpu.VMEM((GROUPS, NPIX), F32),
            pltpu.VMEM((NPIX // 128, 128), F32),
            pltpu.VMEM((1, NIMG), jnp.int32),
            pltpu.SMEM((2, NSHIFT), jnp.int32),
            pltpu.VMEM((NPROJ, 2, NPIX), BF16),
            pltpu.VMEM((2, NPROJ, NPIX), BF16),
            pltpu.VMEM((1, NPROJ), jnp.int32),
            pltpu.VMEM((2, 128), F32),
            pltpu.VMEM((16, SHARD, 128), BF16),
            pltpu.VMEM((16, 2, NPROJ, 256), BF16),
            pltpu.VMEM((2, NPROJ, 128), BF16),
            pltpu.VMEM((16, 8, 256), F32),
            pltpu.VMEM((16, 8, 256), F32),
            pltpu.VMEM((8, 128), F32),
            pltpu.VMEM((8, 128), F32),
            pltpu.VMEM((16, 2, ROWS, 256), BF16),
            pltpu.VMEM((2, ROWS, 128), BF16),
            pltpu.VMEM((ROWS, NPROJ), F32),
            pltpu.VMEM((NPROJ, ROWS), BF16),
            pltpu.VMEM((2, 4, 8, 128), F32),
            pltpu.VMEM((4, 8 * PIECE, 128), BF16),
            pltpu.VMEM((4, 8 * PIECE, 128), BF16),
            pltpu.VMEM((64, 128), BF16),
            pltpu.VMEM((64, 128), BF16),
            pltpu.VMEM((2, MSG, 128), BF16),
            pltpu.VMEM((2, MSG, 128), BF16),
            pltpu.VMEM((2, HALF, 128), BF16),
            pltpu.VMEM((2, MSG - HALF, 128), BF16),
            pltpu.VMEM((2, MSG, 128), BF16),
            pltpu.VMEM((MSG, 128), F32),
            pltpu.VMEM((7, 64, 128), BF16),
            pltpu.VMEM((2, 64, 128), BF16),
            pltpu.VMEM((2, 2, 64, 128), BF16),
            pltpu.VMEM((64, 128), BF16),
            sem((4, 2)),
            sem((4, 2)),
            sem((2, 4, 2)),
            sem((2, 4, 2)),
            sem((2, 4)),
            sem((2, 4)),
            sem((6,)),
            sem((6,)),
            sem((5,)),
            sem((5,)),
            sem((8,)),
            sem((8,)),
            sem((7,)),
            sem((7,)),
            sem((8,)),
        ],
        compiler_params=pltpu.CompilerParams(
            collective_id=0, has_side_effects=True, vmem_limit_bytes=60 * 1024 * 1024
        ),
        name="expectation",
    )(
        images,
        projections,
        contrast_curve,
        noise_weight.reshape(NPIX // 128, 128),
        defocus_group.reshape(1, NIMG),
        shifts.T,
        orient_index.reshape(1, NPROJ),
        orient_prior.reshape(2, 128),
    )
    cls, con, ev = pl.pallas_call(
        finish,
        out_shape=(
            jax.ShapeDtypeStruct((NPROJ, 2, 132), F32),
            jax.ShapeDtypeStruct((NPROJ, 132), F32),
            jax.ShapeDtypeStruct((1, NIMG), F32),
        ),
        in_specs=[hbm] * 4,
        out_specs=(vmem,) * 3,
        scratch_shapes=[
            pltpu.VMEM((2, NPROJ, 256), F32),
            pltpu.VMEM((GROUPS, 128), F32),
            pltpu.VMEM((GROUPS, 256), F32),
            pltpu.VMEM((1, 128), F32),
            sem((4,)),
        ],
        compiler_params=pltpu.CompilerParams(vmem_limit_bytes=60 * 1024 * 1024),
        name="finish",
    )(*held)
    return cls, con, ev.reshape(NIMG)


def solution(mesh):
    in_specs = (P("img", None, "ref"), P("ref", None, None), P(), P(), P("img"), P(), P("ref"), P())
    out_specs = (P("ref", None, "img"), P("ref", "img"), P("img"))
    return jax.shard_map(
        on_device, mesh=mesh, in_specs=in_specs, out_specs=out_specs, check_vma=False
    )
```

```python
import math

import jax
import jax.numpy as jnp
from jax import lax
from jax.experimental import pallas as pl
from jax.experimental.pallas import tpu as pltpu
from jax.sharding import PartitionSpec as P

MESH = pl.DeviceIdType.MESH
F32 = jnp.float32
BF16 = jnp.bfloat16
HIGHEST = lax.Precision.HIGHEST
NT = (((1,), (1,)), ((), ()))
TN = (((0,), (0,)), ((), ()))

NPIX = 4224
BOX = 128
NSHIFT = 9
NIMG = 64
NPROJ = 48
GROUPS = 16
ROWS = NSHIFT * NIMG
SHARD = 272
PIECE = 48
MSG = 400
HALF = 208
FIRST = 112


def sincos(steps):
    quadrant = lax.shift_right_arithmetic(steps + 16, 5)
    rest = (steps - quadrant * 32).astype(F32) * (2.0 * math.pi / BOX)
    sq = rest * rest
    sin_part = rest * (
        1.0 + sq * (-1.0 / 6 + sq * (1.0 / 120 + sq * (-1.0 / 5040 + sq * (1.0 / 362880))))
    )
    cos_part = 1.0 + sq * (
        -0.5 + sq * (1.0 / 24 + sq * (-1.0 / 720 + sq * (1.0 / 40320 - sq * (1.0 / 3628800))))
    )
    odd = (quadrant & 1) == 1
    flip_sin = (quadrant & 2) == 2
    flip_cos = ((quadrant + 1) & 2) == 2
    sine = jnp.where(odd, cos_part, sin_part)
    cosine = jnp.where(odd, sin_part, cos_part)
    return jnp.where(flip_cos, -cosine, cosine), jnp.where(flip_sin, -sine, sine)


def body(
    img_hbm,
    proj_hbm,
    curve_hbm,
    noise_hbm,
    group_hbm,
    shift_hbm,
    orient_hbm,
    prior_hbm,
    cls_ref,
    group_out,
    gain_out,
    ev_ref,
    img_ref,
    curve_ref,
    noise_ref,
    group_ref,
    shift_ref,
    proj_ref,
    planes,
    orient_ref,
    prior_ref,
    xbuf,
    pmain,
    prest,
    ctab,
    stab,
    crest,
    srest,
    smain,
    shrest,
    score,
    tile_sum,
    wts,
    stat,
    core_out,
    core_in,
    rest_out,
    rest_in,
    far_out,
    x_out,
    x_near,
    x_in,
    held,
    z_out,
    z_relay,
    z_in,
    z_core,
    ag_z_s,
    ag_z_r,
    ag_y_s,
    ag_y_r,
    ag_f_s,
    ag_f_r,
    st_s,
    st_r,
    co_s,
    co_r,
    xs_s,
    xs_r,
    zs_s,
    zs_r,
    in_s,
):
    img = lax.axis_index("img")
    ref = lax.axis_index("ref")
    x = lax.div(img, 8)
    h = lax.rem(lax.div(img, 2), 4)
    d = lax.rem(img, 2)
    o = 1 - d
    y = lax.div(ref, 4)
    l = lax.rem(ref, 4)

    def ring(v):
        return lax.rem(v + 4, 4)

    def dev(img_at=img, ref_at=ref):
        return {"img": img_at, "ref": ref_at}

    def at_img(xx, hh, dd):
        return dev(img_at=(xx * 4 + hh) * 2 + dd)

    def copy(src, dst, send, recv, to):
        return pltpu.make_async_remote_copy(
            src_ref=src, dst_ref=dst, send_sem=send, recv_sem=recv, device_id=to, device_id_type=MESH
        )

    barrier = pltpu.get_barrier_semaphore()
    peers = [dev(ref_at=y * 4 + lax.rem(l + k, 4)) for k in range(1, 4)]
    peers += [dev(ref_at=lax.rem(ref + 4 * k, 16)) for k in range(1, 4)]
    peers += [at_img(x, h, o), at_img(ring(x + 1), h, d), at_img(ring(x - 1), h, d)]
    peers += [at_img(ring(x + 1), h, o), at_img(ring(x - 1), h, o)]
    for hh in (ring(h + 1), ring(h - 1)):
        peers += [at_img(x, hh, d), at_img(x, hh, o)]
    for peer in peers:
        pl.semaphore_signal(barrier, inc=1, device_id=peer, device_id_type=MESH)

    loads = [
        pltpu.make_async_copy(src, dst, in_s.at[k])
        for k, (src, dst) in enumerate(
            (
                (group_hbm, group_ref),
                (curve_hbm, curve_ref),
                (noise_hbm, noise_ref),
                (img_hbm, img_ref),
                (shift_hbm, shift_ref),
                (proj_hbm, proj_ref),
                (orient_hbm, orient_ref),
                (prior_hbm, prior_ref),
            )
        )
    ]
    for load in loads:
        load.start()
    for load in loads[:4]:
        load.wait()

    lane = lax.broadcasted_iota(jnp.int32, (1, 128), 1)

    def noise_row(tile, count):
        return jnp.concatenate([noise_ref[pl.ds(tile + t, 1), :] for t in range(count)], axis=1)


    group_row = group_ref[...].astype(F32)
    group_row = jnp.concatenate([group_row, group_row], axis=1)
    group_col = jnp.transpose(jnp.broadcast_to(group_row, (128, 128)))[:NIMG, :]
    start = pl.multiple_of(ref * 256, 128)
    turn = lax.rem(384 - 8 * ref, 384)
    curve_here = pltpu.roll(curve_ref[:, pl.ds(start, 384)], turn, 1)
    noise_here = pltpu.roll(jnp.broadcast_to(noise_row(2 * ref, 3), (8, 384)), turn, 1)[:1, :]
    parts = []
    for tile in range(3):
        span = slice(tile * 128, tile * 128 + 128)
        gain = jnp.zeros((NIMG, 128), F32)
        for g in range(GROUPS):
            gain = jnp.where(group_col == float(g), curve_here[g : g + 1, span], gain)
        gain = gain * noise_here[:, span]
        both = []
        for c in range(2):
            if tile < 2:
                pixels = img_ref[:, c, span].astype(F32)
            else:
                pixels = img_ref[:, c, 256:264].astype(F32)
                pixels = jnp.concatenate([pixels, jnp.zeros((NIMG, 120), F32)], axis=1)
            both.append(pixels * gain)
        parts.append(jnp.concatenate(both, axis=0))
    second = pltpu.roll(jnp.concatenate(parts[1:], axis=1), 252, 1)[:, :128]
    rest = jnp.transpose(jnp.where(lane < 4, parts[1], parts[2]))[:16, :]
    row16 = lax.broadcasted_iota(jnp.int32, (16, 128), 0)
    rest = jnp.where(row16 < 8, rest, 0.0)
    xbuf[ref, 0:128, :] = parts[0].astype(BF16)
    xbuf[ref, 128:256, :] = second.astype(BF16)
    xbuf[ref, 256:272, :] = rest.astype(BF16)

    pl.semaphore_wait(barrier, len(peers))

    columns = [lax.rem(l + 4 - e, 4) for e in range(4)]
    halves = (pl.ds(0, 144), pl.ds(144, 128))

    def shard(yy, e):
        return yy * 4 + columns[e]

    def z_send(e, part):
        block = xbuf.at[ref, halves[part]]
        to = dev(ref_at=y * 4 + lax.rem(l + e, 4))
        return copy(block, block, ag_z_s.at[e, part], ag_z_r.at[e, part], to)

    y_up, y_down, y_far = ring(y + 1), ring(y - 1), ring(y + 2)

    def y_copy(way, e, src_y, part):
        to = dev(ref_at=(y_up if way == 0 else y_down) * 4 + l)
        block = xbuf.at[shard(src_y, e), halves[part]]
        return copy(block, block, ag_y_s.at[way, e, part], ag_y_r.at[way, e, part], to)

    def f_copy(way, e, src_y):
        to = dev(ref_at=(y_up if way == 0 else y_down) * 4 + l)
        block = xbuf.at[shard(src_y, e), halves[way]]
        return copy(block, block, ag_f_s.at[way, e], ag_f_r.at[way, e], to)

    def send_y(e, part):
        for way in (part, 1 - part):
            y_copy(way, e, y, part).start()

    def near_z():
        for part in range(2):
            z_send(1, part).start()
            z_send(3, part).start()

    @pl.when(d == 0)
    def _():
        near_z()

    send_y(0, 0)
    send_y(0, 1)

    def take_z(e, part):
        block = xbuf.at[shard(y, e), halves[part]]
        copy(block, block, ag_z_s.at[e, part], ag_z_r.at[e, part], dev(ref_at=shard(y, e))).wait_recv()
        send_y(e, part)

    def take_y(e):
        y_copy(0, e, y_down, 0).wait_recv()
        f_copy(0, e, y_down).start()
        y_copy(1, e, y_up, 1).wait_recv()
        f_copy(1, e, y_up).start()
        y_copy(0, e, y_down, 1).wait_recv()
        y_copy(1, e, y_up, 0).wait_recv()

    def take_far(e):
        f_copy(0, e, y_far).wait_recv()
        f_copy(1, e, y_far).wait_recv()

    loads[4].wait()

    def table(pixel, width):
        srow = lax.broadcasted_iota(jnp.int32, (8, width), 0) + 1
        move_x = jnp.zeros((8, width), jnp.int32)
        move_y = jnp.zeros((8, width), jnp.int32)
        for s in range(1, NSHIFT):
            move_x = jnp.where(srow == s, shift_ref[0, s], move_x)
            move_y = jnp.where(srow == s, shift_ref[1, s], move_y)
        freq_x = pixel & (BOX // 2 - 1)
        freq_y = lax.shift_right_logical(pixel, 6) - NPIX // BOX
        return sincos((move_x * freq_x + move_y * freq_y) & (BOX - 1))

    def table_step(b, carry):
        at = lax.broadcasted_iota(jnp.int32, (8, 256), 1)
        pixel = 264 * b + at + jnp.where(at >= 128, 4, 0)
        cosine, sine = table(pixel, 256)
        ctab[b] = cosine
        stab[b] = sine
        return carry

    lax.fori_loop(0, 16, table_step, 0)
    at = lax.broadcasted_iota(jnp.int32, (8, 128), 1)
    cosine, sine = table(132 * lax.shift_right_logical(at, 2) + 128 + (at & 3), 128)
    crest[...] = cosine
    srest[...] = sine

    @pl.when(d == 1)
    def _():
        near_z()

    @pl.when(d == 0)
    def _():
        for part in range(2):
            z_send(2, part).start()

    for load in loads[5:]:
        load.wait()

    def plane_step(t, carry):
        span = pl.ds(pl.multiple_of(t * 384, 128), 384)
        for c in range(2):
            planes[c, :, span] = proj_ref[:, c, span]
        return carry

    lax.fori_loop(0, 11, plane_step, 0)

    @pl.when(d == 1)
    def _():
        for part in range(2):
            z_send(2, part).start()

    take_y(0)


    def proj_step(b, carry):
        out = []
        for c in range(2):
            kept = carry[c]
            for u in range(2):
                n = 2 * b + u
                window = planes[c, :, pl.ds(pl.multiple_of(n * 128, 128), 256)].astype(F32)
                turned = pltpu.roll(window, lax.rem(256 - 4 * n, 256), 1)
                pmain[b, c, :, u * 128 : u * 128 + 128] = turned[:, :128].astype(BF16)
                kept = jnp.where(lax.shift_right_logical(lane, 2) == n, window[:, 128:], kept)
            out.append(kept)
        return tuple(out)

    zero_rest = jnp.zeros((NPROJ, 128), F32)
    rests = lax.fori_loop(0, 8, proj_step, (zero_rest, zero_rest))
    for part in range(2):
        take_z(1, part)
        take_z(3, part)
    rests = lax.fori_loop(8, 16, proj_step, rests)
    for c in range(2):
        prest[c] = rests[c].astype(BF16)


    def norm_step(t, total):
        span = pl.ds(pl.multiple_of(t * 384, 128), 384)
        re = planes[0, :, span].astype(F32)
        im = planes[1, :, span].astype(F32)
        curve = curve_ref[:, span]
        gain = 0.5 * (curve * curve * noise_row(3 * t, 3))
        power = re * re + im * im
        return total + lax.dot_general(
            two_parts(power), two_parts(gain), NT, preferred_element_type=F32
        )

    def two_parts(value):
        high = value.astype(BF16)
        return jnp.concatenate([high, (value - high.astype(F32)).astype(BF16)], axis=0)

    norm = lax.fori_loop(0, 11, norm_step, jnp.zeros((2 * NPROJ, 2 * GROUPS), F32))
    norm = norm[:NPROJ] + norm[NPROJ:]
    norm = norm[:, :GROUPS] + norm[:, GROUPS:]
    grow = lax.broadcasted_iota(jnp.int32, (GROUPS, 128), 0)
    members = (group_row == grow.astype(F32)).astype(F32)
    penalty = jnp.dot(norm, members, precision=HIGHEST, preferred_element_type=F32)
    orient_row = jnp.concatenate([orient_ref[...].astype(F32), jnp.zeros((1, 80), F32)], axis=1)
    orient_col = jnp.transpose(jnp.broadcast_to(orient_row, (128, 128)))[:NPROJ, :]
    prior = jnp.zeros((NPROJ, 1), F32)
    for half in range(2):
        hit = orient_col == (lane + half * 128).astype(F32)
        prior += jnp.sum(
            jnp.where(hit, prior_ref[half : half + 1, :], 0.0), axis=1, keepdims=True
        )
    base = prior - penalty
    span = pl.ds(pl.multiple_of(img * 128, 128), 256)
    curve = curve_ref[:, span]
    gain_out[...] = pltpu.roll(curve * curve * noise_row(img, 2), lax.rem(256 - 4 * img, 256), 1)

    score[...] = jnp.zeros_like(score)

    def process(b, last=False):
        for t in range(2):
            span = slice(t * 128, t * 128 + 128)
            re = xbuf[b, t * 128 : t * 128 + 64, :]
            im = xbuf[b, t * 128 + 64 : t * 128 + 128, :]
            smain[b, 0, 0:NIMG, span] = re
            smain[b, 1, 0:NIMG, span] = im
            re = re.astype(F32)
            im = im.astype(F32)
            for s in range(1, NSHIFT):
                rows = slice(s * NIMG, s * NIMG + NIMG)
                cosine = ctab[b, s - 1 : s, span]
                sine = stab[b, s - 1 : s, span]
                smain[b, 0, rows, span] = (re * cosine + im * sine).astype(BF16)
                smain[b, 1, rows, span] = (im * cosine - re * sine).astype(BF16)
        if last:
            return lax.dot_general(
                pmain[b, 0], smain[b, 0], NT, preferred_element_type=F32
            ) + lax.dot_general(pmain[b, 1], smain[b, 1], NT, preferred_element_type=F32)
        score[...] += lax.dot_general(
            smain[b, 0], pmain[b, 0], NT, preferred_element_type=F32
        ) + lax.dot_general(smain[b, 1], pmain[b, 1], NT, preferred_element_type=F32)

    def process_all(blocks):
        def step(t, carry):
            b = blocks[0]
            for k in range(1, len(blocks)):
                b = jnp.where(t == k, blocks[k], b)
            process(b)
            return carry

        lax.fori_loop(0, len(blocks), step, 0)

    take_z(2, 0)
    take_z(2, 1)
    process_all([shard(y, 0), shard(y, 1)])
    take_y(1)
    process_all([shard(y_down, 0), shard(y_up, 0)])
    take_far(0)
    take_y(3)
    process_all([shard(y_far, 0), shard(y, 3), shard(y_down, 1)])
    take_y(2)
    process_all([shard(y_up, 1), shard(y, 2), shard(y_down, 3), shard(y_up, 3)])
    take_far(1)
    process_all([shard(y_far, 1), shard(y_down, 2), shard(y_up, 2)])
    take_far(3)
    process(shard(y_far, 3))
    full = jnp.concatenate([score[...], jnp.zeros((ROWS, 128 - NPROJ), F32)], axis=1)
    for t in range(5):
        if t < 4:
            turned = full[t * 128 : t * 128 + 128]
        else:
            turned = jnp.concatenate([full[512:576], jnp.zeros((64, 128), F32)], axis=0)
        tile_sum[t] = jnp.transpose(turned)[:NPROJ] + base
    take_far(2)
    last_part = process(shard(y_far, 2), last=True)

    rest_t = jnp.concatenate([xbuf[b, 256:272, :].astype(F32)[:8] for b in range(16)], axis=0)
    rest_x = jnp.transpose(rest_t)
    re, im = rest_x[:NIMG], rest_x[NIMG:]
    shrest[0, 0:NIMG, :] = re.astype(BF16)
    shrest[1, 0:NIMG, :] = im.astype(BF16)
    for s in range(1, NSHIFT):
        rows = slice(s * NIMG, s * NIMG + NIMG)
        cosine = crest[s - 1 : s, :]
        sine = srest[s - 1 : s, :]
        shrest[0, rows, :] = (re * cosine + im * sine).astype(BF16)
        shrest[1, rows, :] = (im * cosine - re * sine).astype(BF16)
    last_part += lax.dot_general(
        prest[0], shrest[0], NT, preferred_element_type=F32
    ) + lax.dot_general(prest[1], shrest[1], NT, preferred_element_type=F32)
    tiles = []
    for t in range(5):
        if t < 4:
            tiles.append(tile_sum[t] + last_part[:, t * 128 : t * 128 + 128])
        else:
            end = jnp.concatenate([last_part[:, 512:576]] * 2, axis=1)
            tiles.append(jnp.where(lane < 64, tile_sum[t] + end, -3e38))
    high = tiles[0]
    for t in range(1, 5):
        high = jnp.maximum(high, tiles[t])
    high = jnp.max(high, axis=0, keepdims=True)
    high = jnp.maximum(high, pltpu.roll(jnp.broadcast_to(high, (8, 128)), 64, 1)[:1])
    total = jnp.exp(tiles[0] - high)
    for t in range(1, 5):
        total += jnp.exp(tiles[t] - high)
    total = jnp.sum(total, axis=0, keepdims=True)
    total = total + pltpu.roll(jnp.broadcast_to(total, (8, 128)), 64, 1)[:1]
    row8 = lax.broadcasted_iota(jnp.int32, (8, 128), 0)

    def merged(blocks):
        top = blocks[0][0:1, :]
        for block in blocks[1:]:
            top = jnp.maximum(top, block[0:1, :])
        whole = jnp.zeros((1, 128), F32)
        for block in blocks:
            whole += block[1:2, :] * jnp.exp(block[0:1, :] - top)
        return top, whole

    st_copies = []
    for stage in range(2):
        mine_at = l if stage == 0 else y
        stat[stage, mine_at] = jnp.where(row8 == 0, high, total)
        for k in range(1, 4):
            to = y * 4 + lax.rem(l + k, 4) if stage == 0 else lax.rem(ref + 4 * k, 16)
            block = stat.at[stage, mine_at]
            c = copy(block, block, st_s.at[3 * stage + k - 1], st_r.at[3 * stage + k - 1], dev(ref_at=to))
            c.start()
            st_copies.append(c)
        for k in range(1, 4):
            src = lax.rem(mine_at + 4 - k, 4)
            block = stat.at[stage, src]
            come_from = y * 4 + src if stage == 0 else src * 4 + l
            copy(
                block, block, st_s.at[3 * stage + k - 1], st_r.at[3 * stage + k - 1], dev(ref_at=come_from)
            ).wait_recv()
        high, total = merged([stat[stage, b] for b in range(4)])
    evidence = high + jnp.log(total)
    ev_ref[...] = evidence
    for t in range(5):
        w = jnp.exp(tiles[t] - evidence).astype(BF16)
        if t < 4:
            wts[:, t * 128 : t * 128 + 128] = w
        else:
            wts[:, 512:576] = w[:, :64]
    members_all = jnp.concatenate([members.astype(BF16)] * 4 + [members[:, :64].astype(BF16)], axis=1)
    group_sum = lax.dot_general(members_all, wts[...], NT, preferred_element_type=F32)
    group_sum = jnp.concatenate([group_sum, jnp.zeros((GROUPS, 80), F32)], axis=1)

    other = at_img(x, h, o)
    rest_mine = jnp.dot(wts[...], shrest[d], preferred_element_type=F32)
    rest_theirs = jnp.dot(wts[...], shrest[o], preferred_element_type=F32)

    order = [ring(x + 2), ring(x + 1), ring(x + 3), x]
    runs = [ring(h + 2), ring(h + 1), ring(h + 3), h]

    def core_copy(i):
        return copy(core_out.at[i], core_in.at[i], co_s.at[i], co_r.at[i], other)

    def other_chunk(i):
        for u in range(4):
            got = jnp.dot(wts[...], smain[4 * order[i] + runs[u], o], preferred_element_type=F32)
            for v in range(2):
                r = PIECE * (2 * u + v)
                core_out[i, r : r + PIECE, :] = got[:, v * 128 : v * 128 + 128].astype(BF16)
        core_copy(i).start()

    def left(value, by):
        return pltpu.roll(value, lax.rem(256 - by, 128), 1)

    def packed(q, rest_tile, group_tile, c):
        out = left(rest_tile[0:16], 32 * q)
        out = jnp.where(lane < 32, out, left(rest_tile[16:32], 32 * q - 32))
        out = jnp.where(lane < 64, out, left(rest_tile[32:48], 32 * q - 64))
        return jnp.where(lane < 96, out, left(group_tile, 32 + 24 * c))

    def piece_row(k):
        return 16 + PIECE * k

    def rows_of(k):
        return slice(0, 16) if k < 0 else slice(piece_row(k), piece_row(k) + PIECE)

    far_spans = (slice(0, FIRST), slice(FIRST, HALF), slice(HALF, MSG))

    def far_copy(k, part):
        span = far_spans[part]
        rows = pl.ds(span.start, span.stop - span.start)
        c = d if k == 0 else o
        to = at_img(ring(x + 1) if part < 2 else ring(x - 1), h, c)
        at = 2 * part + k
        return copy(far_out.at[k, rows], x_near.at[k, rows], xs_s.at[at], xs_r.at[at], to)

    def far_sums(k, runs_of):
        for u in runs_of:
            got = jnp.dot(
                wts[...], smain[4 * order[0] + runs[u], d if k == 0 else o], preferred_element_type=F32
            ).astype(BF16)
            for v in range(2):
                far_out[k, rows_of(2 * u + v), :] = got[:, v * 128 : v * 128 + 128]

    for k in range(2):
        far_sums(k, (0,))
        rest_tile = rest_mine if k == 0 else rest_theirs
        far_out[k, 0:16, :] = packed(order[0], rest_tile, group_sum, d if k == 0 else o).astype(BF16)
        far_copy(k, 0).start()
    for k in range(2):
        far_sums(k, (1, 2, 3))
        far_copy(k, 2).start()
        far_copy(k, 1).start()

    rest_out[0:48, :] = rest_theirs.astype(BF16)
    rest_out[48:64, :] = group_sum.astype(BF16)
    rest_copy = copy(rest_out, rest_in, co_s.at[4], co_r.at[4], other)
    rest_copy.start()
    for i in range(1, 4):
        other_chunk(i)

    rest_copy.wait_recv()
    rest_sum = rest_mine + rest_in[0:48, :].astype(F32)
    group_sum = group_sum + rest_in[48:64, :].astype(F32)

    def own_chunk(i):
        q = order[i]
        sums = [
            jnp.dot(wts[...], smain[4 * q + runs[u], d], preferred_element_type=F32) for u in range(4)
        ]
        core_copy(i).wait_recv()
        for u in range(4):
            for v in range(2):
                k = 2 * u + v
                r = PIECE * k
                held[rows_of(k), :] = (
                    sums[u][:, v * 128 : v * 128 + 128] + core_in[i, r : r + PIECE, :].astype(F32)
                )
        held[0:16, :] = packed(q, rest_sum, group_sum, d)

    x_up, x_down = at_img(ring(x + 1), h, d), at_img(ring(x - 1), h, d)

    def near_sum(part):
        span = far_spans[part]
        for k in range(2):
            far_copy(k, part).wait_recv()
        both = x_near[0, span, :].astype(F32) + x_near[1, span, :].astype(F32)
        return (held[span, :] + both).astype(BF16)

    def x_copy(way, part):
        rows = pl.ds(0, FIRST) if part == 0 else pl.ds(FIRST, MSG - FIRST)
        k = 6 + 2 * way + part
        to = x_up if way == 0 else x_down
        return copy(x_out.at[way, rows], x_in.at[way, rows], xs_s.at[k], xs_r.at[k], to)

    own_chunk(1)
    x_out[0, 0:FIRST, :] = near_sum(0)
    x_copy(0, 0).start()
    x_out[0, HALF:MSG, :] = held[HALF:MSG, :].astype(BF16)
    x_out[0, FIRST:HALF, :] = near_sum(1)
    x_copy(0, 1).start()

    own_chunk(2)
    x_out[1, 0:HALF, :] = held[0:HALF, :].astype(BF16)
    x_copy(1, 0).start()
    x_out[1, HALF:MSG, :] = near_sum(2)
    x_copy(1, 1).start()

    own_chunk(3)

    def add_x(part):
        rows = slice(0, FIRST) if part == 0 else slice(FIRST, MSG)
        x_copy(0, part).wait_recv()
        x_copy(1, part).wait_recv()
        held[rows, :] += x_in[0, rows, :].astype(F32) + x_in[1, rows, :].astype(F32)

    add_x(0)

    def piece_of(u, dd):
        return held[pl.ds(pl.multiple_of(16 + PIECE * (2 * u + dd), 16), PIECE), :]

    rest_pack = held[0:16, :]
    h_up, h_down = ring(h + 1), ring(h - 1)

    def fill(slot, value, extra):
        z_out[slot, 0:48, :] = value.astype(BF16)
        z_out[slot, 48:64, :] = extra.astype(BF16)

    fill(0, piece_of(0, 0), rest_pack)
    fill(1, piece_of(0, 1), rest_pack)
    relay_up = copy(z_out.at[0], z_relay.at[0], zs_s.at[0], zs_r.at[0], at_img(x, h_up, d))
    relay_down = copy(z_out.at[1], z_relay.at[1], zs_s.at[1], zs_r.at[1], at_img(x, h_down, d))
    relay_up.start()
    relay_down.start()
    add_x(1)

    def z_copy(slot):
        way, dd = (slot - 2) // 2, (slot - 2) % 2
        to = at_img(x, h_up if way == 0 else h_down, dd)
        return copy(z_out.at[slot], z_in.at[way, d], zs_s.at[slot], zs_r.at[2 + 2 * way + d], to)

    fill(3, piece_of(1, 1), rest_pack)
    z_copy(3).start()
    fill(4, piece_of(2, 0), rest_pack)
    z_copy(4).start()
    fill(6, piece_of(3, o), rest_pack)
    core_last = copy(z_out.at[6], z_core, zs_s.at[6], zs_r.at[6], other)
    core_last.start()
    relay_up.wait_recv()
    fill(
        2,
        piece_of(1, 0) + z_relay[0, 0:48, :].astype(F32),
        rest_pack + z_relay[0, 48:64, :].astype(F32),
    )
    z_copy(2).start()
    relay_down.wait_recv()
    fill(
        5,
        piece_of(2, 1) + z_relay[1, 0:48, :].astype(F32),
        rest_pack + z_relay[1, 48:64, :].astype(F32),
    )
    z_copy(5).start()

    mine = jnp.concatenate([piece_of(3, d), rest_pack], axis=0)
    core_last.wait_recv()
    theirs = z_core[...].astype(F32)
    for way in range(2):
        for c in range(2):
            slot = z_in.at[way, c]
            copy(slot, slot, zs_s.at[2], zs_r.at[2 + 2 * way + c], other).wait_recv()
    local = 2 * h + d
    packs = []
    for c in range(2):
        both = jnp.where(d == c, mine, theirs)
        both = both + z_in[0, c].astype(F32) + z_in[1, c].astype(F32)
        cls_ref[c, :, 0:128] = both[0:48]
        pack = both[48:64]
        packs.append(pack)
        for a in range(3):
            cls_ref[c, 16 * a : 16 * a + 16, 128:256] = left(pack, 32 * a + 4 * local)
    group_all = jnp.where(lane < 24, left(packs[0], 96), left(packs[1], 72))
    group_out[...] = jnp.where(lane < 48, group_all, 0.0)

    for e in range(4):
        for part in range(2):
            if e:
                z_send(e, part).wait_send()
            for way in range(2):
                y_copy(way, e, y, part).wait_send()
        for way in range(2):
            f_copy(way, e, y).wait_send()
    for c in st_copies:
        c.wait_send()
    for i in range(1, 4):
        core_copy(i).wait_send()
    for k in range(2):
        for part in range(3):
            far_copy(k, part).wait_send()
    for c in (rest_copy, relay_up, relay_down, core_last):
        c.wait_send()
    for way in range(2):
        for part in range(2):
            x_copy(way, part).wait_send()
    for slot in range(2, 6):
        z_copy(slot).wait_send()


def finish(
    cls_hbm, group_hbm, gain_hbm, ev_hbm, cls_out, con_out, ev_out, cls_ref, group_ref, gain_ref, ev_ref, in_s
):
    loads = [
        pltpu.make_async_copy(src, dst, in_s.at[k])
        for k, (src, dst) in enumerate(
            ((cls_hbm, cls_ref), (group_hbm, group_ref), (gain_hbm, gain_ref), (ev_hbm, ev_ref))
        )
    ]
    for load in loads:
        load.start()
    for load in loads:
        load.wait()
    for c in range(2):
        cls_out[:, c, :] = cls_ref[c, :, 0:132]
    column = jnp.transpose(jnp.concatenate([group_ref[...], jnp.zeros((112, 128), F32)], axis=0))
    con_out[...] = jnp.dot(
        column[:NPROJ, :GROUPS], gain_ref[...], precision=HIGHEST, preferred_element_type=F32
    )[:, :132]
    ev_out[...] = ev_ref[:, :NIMG]


def on_device(
    images, projections, contrast_curve, noise_weight, defocus_group, shifts, orient_index, orient_prior
):
    vmem = pl.BlockSpec(memory_space=pltpu.VMEM)
    sem = pltpu.SemaphoreType.DMA
    hbm = pl.BlockSpec(memory_space=pl.ANY)
    held = pl.pallas_call(
        body,
        out_shape=(
            jax.ShapeDtypeStruct((2, NPROJ, 256), F32),
            jax.ShapeDtypeStruct((GROUPS, 128), F32),
            jax.ShapeDtypeStruct((GROUPS, 256), F32),
            jax.ShapeDtypeStruct((1, 128), F32),
        ),
        in_specs=[hbm] * 8,
        out_specs=(vmem,) * 4,
        scratch_shapes=[
            pltpu.VMEM((NIMG, 2, 264), BF16),
            pltpu.VMEM((GROUPS, NPIX), F32),
            pltpu.VMEM((NPIX // 128, 128), F32),
            pltpu.VMEM((1, NIMG), jnp.int32),
            pltpu.SMEM((2, NSHIFT), jnp.int32),
            pltpu.VMEM((NPROJ, 2, NPIX), BF16),
            pltpu.VMEM((2, NPROJ, NPIX), BF16),
            pltpu.VMEM((1, NPROJ), jnp.int32),
            pltpu.VMEM((2, 128), F32),
            pltpu.VMEM((16, SHARD, 128), BF16),
            pltpu.VMEM((16, 2, NPROJ, 256), BF16),
            pltpu.VMEM((2, NPROJ, 128), BF16),
            pltpu.VMEM((16, 8, 256), F32),
            pltpu.VMEM((16, 8, 256), F32),
            pltpu.VMEM((8, 128), F32),
            pltpu.VMEM((8, 128), F32),
            pltpu.VMEM((16, 2, ROWS, 256), BF16),
            pltpu.VMEM((2, ROWS, 128), BF16),
            pltpu.VMEM((ROWS, NPROJ), F32),
            pltpu.VMEM((5, NPROJ, 128), F32),
            pltpu.VMEM((NPROJ, ROWS), BF16),
            pltpu.VMEM((2, 4, 8, 128), F32),
            pltpu.VMEM((4, 8 * PIECE, 128), BF16),
            pltpu.VMEM((4, 8 * PIECE, 128), BF16),
            pltpu.VMEM((64, 128), BF16),
            pltpu.VMEM((64, 128), BF16),
            pltpu.VMEM((2, MSG, 128), BF16),
            pltpu.VMEM((2, MSG, 128), BF16),
            pltpu.VMEM((2, MSG, 128), BF16),
            pltpu.VMEM((2, MSG, 128), BF16),
            pltpu.VMEM((MSG, 128), F32),
            pltpu.VMEM((7, 64, 128), BF16),
            pltpu.VMEM((2, 64, 128), BF16),
            pltpu.VMEM((2, 2, 64, 128), BF16),
            pltpu.VMEM((64, 128), BF16),
            sem((4, 2)),
            sem((4, 2)),
            sem((2, 4, 2)),
            sem((2, 4, 2)),
            sem((2, 4)),
            sem((2, 4)),
            sem((6,)),
            sem((6,)),
            sem((5,)),
            sem((5,)),
            sem((10,)),
            sem((10,)),
            sem((7,)),
            sem((7,)),
            sem((8,)),
        ],
        compiler_params=pltpu.CompilerParams(
            collective_id=0, has_side_effects=True, vmem_limit_bytes=60 * 1024 * 1024
        ),
        name="expectation",
    )(
        images,
        projections,
        contrast_curve,
        noise_weight.reshape(NPIX // 128, 128),
        defocus_group.reshape(1, NIMG),
        shifts.T,
        orient_index.reshape(1, NPROJ),
        orient_prior.reshape(2, 128),
    )
    cls, con, ev = pl.pallas_call(
        finish,
        out_shape=(
            jax.ShapeDtypeStruct((NPROJ, 2, 132), F32),
            jax.ShapeDtypeStruct((NPROJ, 132), F32),
            jax.ShapeDtypeStruct((1, NIMG), F32),
        ),
        in_specs=[hbm] * 4,
        out_specs=(vmem,) * 3,
        scratch_shapes=[
            pltpu.VMEM((2, NPROJ, 256), F32),
            pltpu.VMEM((GROUPS, 128), F32),
            pltpu.VMEM((GROUPS, 256), F32),
            pltpu.VMEM((1, 128), F32),
            sem((4,)),
        ],
        compiler_params=pltpu.CompilerParams(vmem_limit_bytes=60 * 1024 * 1024),
        name="finish",
    )(*held)
    return cls, con, ev.reshape(NIMG)


def solution(mesh):
    in_specs = (P("img", None, "ref"), P("ref", None, None), P(), P(), P("img"), P(), P("ref"), P())
    out_specs = (P("ref", None, "img"), P("ref", "img"), P("img"))
    return jax.shard_map(
        on_device, mesh=mesh, in_specs=in_specs, out_specs=out_specs, check_vma=False
    )
```

```python
import math

import jax
import jax.numpy as jnp
from jax import lax
from jax.experimental import pallas as pl
from jax.experimental.pallas import tpu as pltpu
from jax.sharding import PartitionSpec as P

MESH = pl.DeviceIdType.MESH
F32 = jnp.float32
BF16 = jnp.bfloat16
HIGHEST = lax.Precision.HIGHEST
NT = (((1,), (1,)), ((), ()))
TN = (((0,), (0,)), ((), ()))

NPIX = 4224
BOX = 128
NSHIFT = 9
NIMG = 64
NPROJ = 48
GROUPS = 16
ROWS = NSHIFT * NIMG
SHARD = 272
PIECE = 48
MSG = 400
HALF = 208
FIRST = 112


def sincos(steps):
    quadrant = lax.shift_right_arithmetic(steps + 16, 5)
    rest = (steps - quadrant * 32).astype(F32) * (2.0 * math.pi / BOX)
    sq = rest * rest
    sin_part = rest * (
        1.0 + sq * (-1.0 / 6 + sq * (1.0 / 120 + sq * (-1.0 / 5040 + sq * (1.0 / 362880))))
    )
    cos_part = 1.0 + sq * (
        -0.5 + sq * (1.0 / 24 + sq * (-1.0 / 720 + sq * (1.0 / 40320 - sq * (1.0 / 3628800))))
    )
    odd = (quadrant & 1) == 1
    flip_sin = (quadrant & 2) == 2
    flip_cos = ((quadrant + 1) & 2) == 2
    sine = jnp.where(odd, cos_part, sin_part)
    cosine = jnp.where(odd, sin_part, cos_part)
    return jnp.where(flip_cos, -cosine, cosine), jnp.where(flip_sin, -sine, sine)


def body(
    img_hbm,
    proj_hbm,
    curve_hbm,
    noise_hbm,
    group_hbm,
    shift_hbm,
    orient_hbm,
    prior_hbm,
    cls_ref,
    group_out,
    gain_out,
    ev_ref,
    img_ref,
    curve_ref,
    noise_ref,
    group_ref,
    shift_ref,
    proj_ref,
    planes,
    orient_ref,
    prior_ref,
    xbuf,
    pmain,
    prest,
    ctab,
    stab,
    crest,
    srest,
    smain,
    shrest,
    score,
    tile_sum,
    wts,
    stat,
    core_out,
    core_in,
    rest_out,
    rest_in,
    far_out,
    x_out,
    x_near,
    x_in,
    held,
    z_out,
    z_relay,
    z_in,
    z_core,
    ag_z_s,
    ag_z_r,
    ag_y_s,
    ag_y_r,
    ag_f_s,
    ag_f_r,
    st_s,
    st_r,
    co_s,
    co_r,
    xs_s,
    xs_r,
    zs_s,
    zs_r,
    in_s,
):
    img = lax.axis_index("img")
    ref = lax.axis_index("ref")
    x = lax.div(img, 8)
    h = lax.rem(lax.div(img, 2), 4)
    d = lax.rem(img, 2)
    o = 1 - d
    y = lax.div(ref, 4)
    l = lax.rem(ref, 4)

    def ring(v):
        return lax.rem(v + 4, 4)

    def dev(img_at=img, ref_at=ref):
        return {"img": img_at, "ref": ref_at}

    def at_img(xx, hh, dd):
        return dev(img_at=(xx * 4 + hh) * 2 + dd)

    def copy(src, dst, send, recv, to):
        return pltpu.make_async_remote_copy(
            src_ref=src, dst_ref=dst, send_sem=send, recv_sem=recv, device_id=to, device_id_type=MESH
        )

    barrier = pltpu.get_barrier_semaphore()
    peers = [dev(ref_at=y * 4 + lax.rem(l + k, 4)) for k in range(1, 4)]
    peers += [dev(ref_at=lax.rem(ref + 4 * k, 16)) for k in range(1, 4)]
    peers += [at_img(x, h, o), at_img(ring(x + 1), h, d), at_img(ring(x - 1), h, d)]
    peers += [at_img(ring(x + 1), h, o), at_img(ring(x - 1), h, o)]
    for hh in (ring(h + 1), ring(h - 1)):
        peers += [at_img(x, hh, d), at_img(x, hh, o)]
    for peer in peers:
        pl.semaphore_signal(barrier, inc=1, device_id=peer, device_id_type=MESH)

    loads = [
        pltpu.make_async_copy(src, dst, in_s.at[k])
        for k, (src, dst) in enumerate(
            (
                (group_hbm, group_ref),
                (curve_hbm, curve_ref),
                (noise_hbm, noise_ref),
                (img_hbm, img_ref),
                (shift_hbm, shift_ref),
                (proj_hbm, proj_ref),
                (orient_hbm, orient_ref),
                (prior_hbm, prior_ref),
            )
        )
    ]
    for load in loads:
        load.start()
    for load in loads[:4]:
        load.wait()

    lane = lax.broadcasted_iota(jnp.int32, (1, 128), 1)

    def noise_row(tile, count):
        return jnp.concatenate([noise_ref[pl.ds(tile + t, 1), :] for t in range(count)], axis=1)


    group_row = group_ref[...].astype(F32)
    group_row = jnp.concatenate([group_row, group_row], axis=1)
    group_col = jnp.transpose(jnp.broadcast_to(group_row, (128, 128)))[:NIMG, :]
    start = pl.multiple_of(ref * 256, 128)
    turn = lax.rem(384 - 8 * ref, 384)
    curve_here = pltpu.roll(curve_ref[:, pl.ds(start, 384)], turn, 1)
    noise_here = pltpu.roll(jnp.broadcast_to(noise_row(2 * ref, 3), (8, 384)), turn, 1)[:1, :]
    parts = []
    for tile in range(3):
        span = slice(tile * 128, tile * 128 + 128)
        gain = jnp.zeros((NIMG, 128), F32)
        for g in range(GROUPS):
            gain = jnp.where(group_col == float(g), curve_here[g : g + 1, span], gain)
        gain = gain * noise_here[:, span]
        both = []
        for c in range(2):
            if tile < 2:
                pixels = img_ref[:, c, span].astype(F32)
            else:
                pixels = img_ref[:, c, 256:264].astype(F32)
                pixels = jnp.concatenate([pixels, jnp.zeros((NIMG, 120), F32)], axis=1)
            both.append(pixels * gain)
        parts.append(jnp.concatenate(both, axis=0))
    second = pltpu.roll(jnp.concatenate(parts[1:], axis=1), 252, 1)[:, :128]
    rest = jnp.transpose(jnp.where(lane < 4, parts[1], parts[2]))[:16, :]
    row16 = lax.broadcasted_iota(jnp.int32, (16, 128), 0)
    rest = jnp.where(row16 < 8, rest, 0.0)
    xbuf[ref, 0:128, :] = parts[0].astype(BF16)
    xbuf[ref, 128:256, :] = second.astype(BF16)
    xbuf[ref, 256:272, :] = rest.astype(BF16)

    pl.semaphore_wait(barrier, len(peers))

    near = jnp.where(l == 0, 3, 1)
    next_near = 4 - near
    halves = (pl.ds(0, 144), pl.ds(144, 128))

    def shard(yy, e):
        return yy * 4 + lax.rem(l + 4 - e, 4)

    def z_send(e, part):
        block = xbuf.at[ref, halves[part]]
        to = dev(ref_at=y * 4 + lax.rem(l + e, 4))
        return copy(block, block, ag_z_s.at[e, part], ag_z_r.at[e, part], to)

    y_up, y_down, y_far = ring(y + 1), ring(y - 1), ring(y + 2)

    def y_copy(way, e, src_y, part):
        to = dev(ref_at=(y_up if way == 0 else y_down) * 4 + l)
        block = xbuf.at[shard(src_y, e), halves[part]]
        return copy(block, block, ag_y_s.at[way, e, part], ag_y_r.at[way, e, part], to)

    def f_copy(way, e, src_y):
        to = dev(ref_at=(y_up if way == 0 else y_down) * 4 + l)
        block = xbuf.at[shard(src_y, e), halves[way]]
        return copy(block, block, ag_f_s.at[way, e], ag_f_r.at[way, e], to)

    def send_y(e, part):
        for way in (part, 1 - part):
            y_copy(way, e, y, part).start()

    def near_z():
        for part in range(2):
            z_send(1, part).start()
            z_send(3, part).start()

    @pl.when(d == 0)
    def _():
        near_z()

    send_y(0, 0)
    send_y(0, 1)

    def take_z(e, part):
        block = xbuf.at[shard(y, e), halves[part]]
        copy(block, block, ag_z_s.at[e, part], ag_z_r.at[e, part], dev(ref_at=shard(y, e))).wait_recv()
        send_y(e, part)

    def take_y(e):
        y_copy(0, e, y_down, 0).wait_recv()
        f_copy(0, e, y_down).start()
        y_copy(1, e, y_up, 1).wait_recv()
        f_copy(1, e, y_up).start()
        y_copy(0, e, y_down, 1).wait_recv()
        y_copy(1, e, y_up, 0).wait_recv()

    def take_far(e):
        f_copy(0, e, y_far).wait_recv()
        f_copy(1, e, y_far).wait_recv()

    loads[4].wait()

    def table(pixel, width):
        srow = lax.broadcasted_iota(jnp.int32, (8, width), 0) + 1
        move_x = jnp.zeros((8, width), jnp.int32)
        move_y = jnp.zeros((8, width), jnp.int32)
        for s in range(1, NSHIFT):
            move_x = jnp.where(srow == s, shift_ref[0, s], move_x)
            move_y = jnp.where(srow == s, shift_ref[1, s], move_y)
        freq_x = pixel & (BOX // 2 - 1)
        freq_y = lax.shift_right_logical(pixel, 6) - NPIX // BOX
        return sincos((move_x * freq_x + move_y * freq_y) & (BOX - 1))

    def table_step(b, carry):
        at = lax.broadcasted_iota(jnp.int32, (8, 256), 1)
        pixel = 264 * b + at + jnp.where(at >= 128, 4, 0)
        cosine, sine = table(pixel, 256)
        ctab[b] = cosine
        stab[b] = sine
        return carry

    lax.fori_loop(0, 16, table_step, 0)
    at = lax.broadcasted_iota(jnp.int32, (8, 128), 1)
    cosine, sine = table(132 * lax.shift_right_logical(at, 2) + 128 + (at & 3), 128)
    crest[...] = cosine
    srest[...] = sine

    @pl.when(d == 1)
    def _():
        near_z()

    @pl.when(d == 0)
    def _():
        for part in range(2):
            z_send(2, part).start()

    for load in loads[5:]:
        load.wait()

    def plane_step(t, carry):
        span = pl.ds(pl.multiple_of(t * 384, 128), 384)
        for c in range(2):
            planes[c, :, span] = proj_ref[:, c, span]
        return carry

    lax.fori_loop(0, 11, plane_step, 0)

    @pl.when(d == 1)
    def _():
        for part in range(2):
            z_send(2, part).start()

    for part in range(2):
        take_z(near, part)
    for part in range(2):
        take_z(next_near, part)
    take_y(0)


    def proj_step(b, carry):
        out = []
        for c in range(2):
            kept = carry[c]
            for u in range(2):
                n = 2 * b + u
                window = planes[c, :, pl.ds(pl.multiple_of(n * 128, 128), 256)].astype(F32)
                turned = pltpu.roll(window, lax.rem(256 - 4 * n, 256), 1)
                pmain[b, c, :, u * 128 : u * 128 + 128] = turned[:, :128].astype(BF16)
                kept = jnp.where(lax.shift_right_logical(lane, 2) == n, window[:, 128:], kept)
            out.append(kept)
        return tuple(out)

    zero_rest = jnp.zeros((NPROJ, 128), F32)
    rests = lax.fori_loop(0, 16, proj_step, (zero_rest, zero_rest))
    for c in range(2):
        prest[c] = rests[c].astype(BF16)


    def norm_step(t, total):
        span = pl.ds(pl.multiple_of(t * 384, 128), 384)
        re = planes[0, :, span].astype(F32)
        im = planes[1, :, span].astype(F32)
        curve = curve_ref[:, span]
        gain = 0.5 * (curve * curve * noise_row(3 * t, 3))
        power = re * re + im * im
        return total + lax.dot_general(
            two_parts(power), two_parts(gain), NT, preferred_element_type=F32
        )

    def two_parts(value):
        high = value.astype(BF16)
        return jnp.concatenate([high, (value - high.astype(F32)).astype(BF16)], axis=0)

    norm = lax.fori_loop(0, 11, norm_step, jnp.zeros((2 * NPROJ, 2 * GROUPS), F32))
    norm = norm[:NPROJ] + norm[NPROJ:]
    norm = norm[:, :GROUPS] + norm[:, GROUPS:]
    grow = lax.broadcasted_iota(jnp.int32, (GROUPS, 128), 0)
    members = (group_row == grow.astype(F32)).astype(F32)
    penalty = jnp.dot(norm, members, precision=HIGHEST, preferred_element_type=F32)
    orient_row = jnp.concatenate([orient_ref[...].astype(F32), jnp.zeros((1, 80), F32)], axis=1)
    orient_col = jnp.transpose(jnp.broadcast_to(orient_row, (128, 128)))[:NPROJ, :]
    prior = jnp.zeros((NPROJ, 1), F32)
    for half in range(2):
        hit = orient_col == (lane + half * 128).astype(F32)
        prior += jnp.sum(
            jnp.where(hit, prior_ref[half : half + 1, :], 0.0), axis=1, keepdims=True
        )
    base = prior - penalty
    span = pl.ds(pl.multiple_of(img * 128, 128), 256)
    curve = curve_ref[:, span]
    gain_out[...] = pltpu.roll(curve * curve * noise_row(img, 2), lax.rem(256 - 4 * img, 256), 1)

    score[...] = jnp.zeros_like(score)

    def process(b, last=False):
        for t in range(2):
            span = slice(t * 128, t * 128 + 128)
            re = xbuf[b, t * 128 : t * 128 + 64, :]
            im = xbuf[b, t * 128 + 64 : t * 128 + 128, :]
            smain[b, 0, 0:NIMG, span] = re
            smain[b, 1, 0:NIMG, span] = im
            re = re.astype(F32)
            im = im.astype(F32)
            for s in range(1, NSHIFT):
                rows = slice(s * NIMG, s * NIMG + NIMG)
                cosine = ctab[b, s - 1 : s, span]
                sine = stab[b, s - 1 : s, span]
                smain[b, 0, rows, span] = (re * cosine + im * sine).astype(BF16)
                smain[b, 1, rows, span] = (im * cosine - re * sine).astype(BF16)
        if last:
            return lax.dot_general(
                pmain[b, 0], smain[b, 0], NT, preferred_element_type=F32
            ) + lax.dot_general(pmain[b, 1], smain[b, 1], NT, preferred_element_type=F32)
        score[...] += lax.dot_general(
            smain[b, 0], pmain[b, 0], NT, preferred_element_type=F32
        ) + lax.dot_general(smain[b, 1], pmain[b, 1], NT, preferred_element_type=F32)

    def process_all(blocks):
        def step(t, carry):
            b = blocks[0]
            for k in range(1, len(blocks)):
                b = jnp.where(t == k, blocks[k], b)
            process(b)
            return carry

        lax.fori_loop(0, len(blocks), step, 0)

    take_z(2, 0)
    take_z(2, 1)
    process_all([shard(y, 0), shard(y, near)])
    take_y(near)
    process_all([shard(y_down, 0), shard(y_up, 0)])
    take_far(0)
    take_y(next_near)
    process_all([shard(y_far, 0), shard(y, next_near), shard(y_down, near)])
    take_y(2)
    process_all([shard(y_up, near), shard(y, 2), shard(y_down, next_near), shard(y_up, next_near)])
    take_far(near)
    process_all([shard(y_far, near), shard(y_down, 2), shard(y_up, 2)])
    take_far(next_near)
    process(shard(y_far, next_near))
    full = jnp.concatenate([score[...], jnp.zeros((ROWS, 128 - NPROJ), F32)], axis=1)
    for t in range(5):
        if t < 4:
            turned = full[t * 128 : t * 128 + 128]
        else:
            turned = jnp.concatenate([full[512:576], jnp.zeros((64, 128), F32)], axis=0)
        tile_sum[t] = jnp.transpose(turned)[:NPROJ] + base
    take_far(2)
    last_part = process(shard(y_far, 2), last=True)

    rest_t = jnp.concatenate([xbuf[b, 256:272, :].astype(F32)[:8] for b in range(16)], axis=0)
    rest_x = jnp.transpose(rest_t)
    re, im = rest_x[:NIMG], rest_x[NIMG:]
    shrest[0, 0:NIMG, :] = re.astype(BF16)
    shrest[1, 0:NIMG, :] = im.astype(BF16)
    for s in range(1, NSHIFT):
        rows = slice(s * NIMG, s * NIMG + NIMG)
        cosine = crest[s - 1 : s, :]
        sine = srest[s - 1 : s, :]
        shrest[0, rows, :] = (re * cosine + im * sine).astype(BF16)
        shrest[1, rows, :] = (im * cosine - re * sine).astype(BF16)
    last_part += lax.dot_general(
        prest[0], shrest[0], NT, preferred_element_type=F32
    ) + lax.dot_general(prest[1], shrest[1], NT, preferred_element_type=F32)
    tiles = []
    for t in range(5):
        if t < 4:
            tiles.append(tile_sum[t] + last_part[:, t * 128 : t * 128 + 128])
        else:
            end = jnp.concatenate([last_part[:, 512:576]] * 2, axis=1)
            tiles.append(jnp.where(lane < 64, tile_sum[t] + end, -3e38))
    high = tiles[0]
    for t in range(1, 5):
        high = jnp.maximum(high, tiles[t])
    high = jnp.max(high, axis=0, keepdims=True)
    high = jnp.maximum(high, pltpu.roll(jnp.broadcast_to(high, (8, 128)), 64, 1)[:1])
    total = jnp.exp(tiles[0] - high)
    for t in range(1, 5):
        total += jnp.exp(tiles[t] - high)
    total = jnp.sum(total, axis=0, keepdims=True)
    total = total + pltpu.roll(jnp.broadcast_to(total, (8, 128)), 64, 1)[:1]
    row8 = lax.broadcasted_iota(jnp.int32, (8, 128), 0)

    def merged(blocks):
        top = blocks[0][0:1, :]
        for block in blocks[1:]:
            top = jnp.maximum(top, block[0:1, :])
        whole = jnp.zeros((1, 128), F32)
        for block in blocks:
            whole += block[1:2, :] * jnp.exp(block[0:1, :] - top)
        return top, whole

    st_copies = []
    for stage in range(2):
        mine_at = l if stage == 0 else y
        stat[stage, mine_at] = jnp.where(row8 == 0, high, total)
        for k in range(1, 4):
            to = y * 4 + lax.rem(l + k, 4) if stage == 0 else lax.rem(ref + 4 * k, 16)
            block = stat.at[stage, mine_at]
            c = copy(block, block, st_s.at[3 * stage + k - 1], st_r.at[3 * stage + k - 1], dev(ref_at=to))
            c.start()
            st_copies.append(c)
        for k in range(1, 4):
            src = lax.rem(mine_at + 4 - k, 4)
            block = stat.at[stage, src]
            come_from = y * 4 + src if stage == 0 else src * 4 + l
            copy(
                block, block, st_s.at[3 * stage + k - 1], st_r.at[3 * stage + k - 1], dev(ref_at=come_from)
            ).wait_recv()
        high, total = merged([stat[stage, b] for b in range(4)])
    evidence = high + jnp.log(total)
    ev_ref[...] = evidence
    for t in range(5):
        w = jnp.exp(tiles[t] - evidence).astype(BF16)
        if t < 4:
            wts[:, t * 128 : t * 128 + 128] = w
        else:
            wts[:, 512:576] = w[:, :64]
    members_all = jnp.concatenate([members.astype(BF16)] * 4 + [members[:, :64].astype(BF16)], axis=1)
    group_sum = lax.dot_general(members_all, wts[...], NT, preferred_element_type=F32)
    group_sum = jnp.concatenate([group_sum, jnp.zeros((GROUPS, 80), F32)], axis=1)

    other = at_img(x, h, o)
    rest_mine = jnp.dot(wts[...], shrest[d], preferred_element_type=F32)
    rest_theirs = jnp.dot(wts[...], shrest[o], preferred_element_type=F32)

    order = [ring(x + 2), ring(x + 1), ring(x + 3), x]
    runs = [ring(h + 2), ring(h + 1), ring(h + 3), h]

    def core_copy(i):
        return copy(core_out.at[i], core_in.at[i], co_s.at[i], co_r.at[i], other)

    def other_chunk(i):
        for u in range(4):
            got = jnp.dot(wts[...], smain[4 * order[i] + runs[u], o], preferred_element_type=F32)
            for v in range(2):
                r = PIECE * (2 * u + v)
                core_out[i, r : r + PIECE, :] = got[:, v * 128 : v * 128 + 128].astype(BF16)
        core_copy(i).start()

    def left(value, by):
        return pltpu.roll(value, lax.rem(256 - by, 128), 1)

    def packed(q, rest_tile, group_tile, c):
        out = left(rest_tile[0:16], 32 * q)
        out = jnp.where(lane < 32, out, left(rest_tile[16:32], 32 * q - 32))
        out = jnp.where(lane < 64, out, left(rest_tile[32:48], 32 * q - 64))
        return jnp.where(lane < 96, out, left(group_tile, 32 + 24 * c))

    def piece_row(k):
        return 16 + PIECE * k

    def rows_of(k):
        return slice(0, 16) if k < 0 else slice(piece_row(k), piece_row(k) + PIECE)

    far_spans = (slice(0, FIRST), slice(FIRST, HALF), slice(HALF, MSG))

    def far_copy(k, part):
        span = far_spans[part]
        rows = pl.ds(span.start, span.stop - span.start)
        c = d if k == 0 else o
        to = at_img(ring(x + 1) if part < 2 else ring(x - 1), h, c)
        at = 2 * part + k
        return copy(far_out.at[k, rows], x_near.at[k, rows], xs_s.at[at], xs_r.at[at], to)

    def far_sums(k, runs_of):
        for u in runs_of:
            got = jnp.dot(
                wts[...], smain[4 * order[0] + runs[u], d if k == 0 else o], preferred_element_type=F32
            ).astype(BF16)
            for v in range(2):
                far_out[k, rows_of(2 * u + v), :] = got[:, v * 128 : v * 128 + 128]

    for k in range(2):
        far_sums(k, (0,))
        rest_tile = rest_mine if k == 0 else rest_theirs
        far_out[k, 0:16, :] = packed(order[0], rest_tile, group_sum, d if k == 0 else o).astype(BF16)
        far_copy(k, 0).start()
    for k in range(2):
        far_sums(k, (1, 2, 3))
        far_copy(k, 2).start()
        far_copy(k, 1).start()

    rest_out[0:48, :] = rest_theirs.astype(BF16)
    rest_out[48:64, :] = group_sum.astype(BF16)
    rest_copy = copy(rest_out, rest_in, co_s.at[4], co_r.at[4], other)
    rest_copy.start()
    for i in range(1, 4):
        other_chunk(i)

    rest_copy.wait_recv()
    rest_sum = rest_mine + rest_in[0:48, :].astype(F32)
    group_sum = group_sum + rest_in[48:64, :].astype(F32)

    def own_chunk(i):
        q = order[i]
        sums = [
            jnp.dot(wts[...], smain[4 * q + runs[u], d], preferred_element_type=F32) for u in range(4)
        ]
        core_copy(i).wait_recv()
        for u in range(4):
            for v in range(2):
                k = 2 * u + v
                r = PIECE * k
                held[rows_of(k), :] = (
                    sums[u][:, v * 128 : v * 128 + 128] + core_in[i, r : r + PIECE, :].astype(F32)
                )
        held[0:16, :] = packed(q, rest_sum, group_sum, d)

    x_up, x_down = at_img(ring(x + 1), h, d), at_img(ring(x - 1), h, d)

    def near_sum(part):
        span = far_spans[part]
        for k in range(2):
            far_copy(k, part).wait_recv()
        both = x_near[0, span, :].astype(F32) + x_near[1, span, :].astype(F32)
        return (held[span, :] + both).astype(BF16)

    def x_copy(way, part):
        rows = pl.ds(0, FIRST) if part == 0 else pl.ds(FIRST, MSG - FIRST)
        k = 6 + 2 * way + part
        to = x_up if way == 0 else x_down
        return copy(x_out.at[way, rows], x_in.at[way, rows], xs_s.at[k], xs_r.at[k], to)

    own_chunk(1)
    x_out[0, 0:FIRST, :] = near_sum(0)
    x_copy(0, 0).start()
    x_out[0, HALF:MSG, :] = held[HALF:MSG, :].astype(BF16)
    x_out[0, FIRST:HALF, :] = near_sum(1)
    x_copy(0, 1).start()

    own_chunk(2)
    x_out[1, 0:HALF, :] = held[0:HALF, :].astype(BF16)
    x_copy(1, 0).start()
    x_out[1, HALF:MSG, :] = near_sum(2)
    x_copy(1, 1).start()

    own_chunk(3)

    def add_x(part):
        rows = slice(0, FIRST) if part == 0 else slice(FIRST, MSG)
        x_copy(0, part).wait_recv()
        x_copy(1, part).wait_recv()
        held[rows, :] += x_in[0, rows, :].astype(F32) + x_in[1, rows, :].astype(F32)

    add_x(0)

    def piece_of(u, dd):
        return held[pl.ds(pl.multiple_of(16 + PIECE * (2 * u + dd), 16), PIECE), :]

    rest_pack = held[0:16, :]
    h_up, h_down = ring(h + 1), ring(h - 1)

    def fill(slot, value, extra):
        z_out[slot, 0:48, :] = value.astype(BF16)
        z_out[slot, 48:64, :] = extra.astype(BF16)

    fill(0, piece_of(0, 0), rest_pack)
    fill(1, piece_of(0, 1), rest_pack)
    relay_up = copy(z_out.at[0], z_relay.at[0], zs_s.at[0], zs_r.at[0], at_img(x, h_up, d))
    relay_down = copy(z_out.at[1], z_relay.at[1], zs_s.at[1], zs_r.at[1], at_img(x, h_down, d))
    relay_up.start()
    relay_down.start()
    add_x(1)

    def z_copy(slot):
        way, dd = (slot - 2) // 2, (slot - 2) % 2
        to = at_img(x, h_up if way == 0 else h_down, dd)
        return copy(z_out.at[slot], z_in.at[way, d], zs_s.at[slot], zs_r.at[2 + 2 * way + d], to)

    fill(3, piece_of(1, 1), rest_pack)
    z_copy(3).start()
    fill(4, piece_of(2, 0), rest_pack)
    z_copy(4).start()
    fill(6, piece_of(3, o), rest_pack)
    core_last = copy(z_out.at[6], z_core, zs_s.at[6], zs_r.at[6], other)
    core_last.start()
    relay_up.wait_recv()
    fill(
        2,
        piece_of(1, 0) + z_relay[0, 0:48, :].astype(F32),
        rest_pack + z_relay[0, 48:64, :].astype(F32),
    )
    z_copy(2).start()
    relay_down.wait_recv()
    fill(
        5,
        piece_of(2, 1) + z_relay[1, 0:48, :].astype(F32),
        rest_pack + z_relay[1, 48:64, :].astype(F32),
    )
    z_copy(5).start()

    mine = jnp.concatenate([piece_of(3, d), rest_pack], axis=0)
    core_last.wait_recv()
    theirs = z_core[...].astype(F32)
    for way in range(2):
        for c in range(2):
            slot = z_in.at[way, c]
            copy(slot, slot, zs_s.at[2], zs_r.at[2 + 2 * way + c], other).wait_recv()
    local = 2 * h + d
    packs = []
    for c in range(2):
        both = jnp.where(d == c, mine, theirs)
        both = both + z_in[0, c].astype(F32) + z_in[1, c].astype(F32)
        cls_ref[c, :, 0:128] = both[0:48]
        pack = both[48:64]
        packs.append(pack)
        for a in range(3):
            cls_ref[c, 16 * a : 16 * a + 16, 128:256] = left(pack, 32 * a + 4 * local)
    group_all = jnp.where(lane < 24, left(packs[0], 96), left(packs[1], 72))
    group_out[...] = jnp.where(lane < 48, group_all, 0.0)

    for e in range(4):
        for part in range(2):
            if e:
                z_send(e, part).wait_send()
            for way in range(2):
                y_copy(way, e, y, part).wait_send()
        for way in range(2):
            f_copy(way, e, y).wait_send()
    for c in st_copies:
        c.wait_send()
    for i in range(1, 4):
        core_copy(i).wait_send()
    for k in range(2):
        for part in range(3):
            far_copy(k, part).wait_send()
    for c in (rest_copy, relay_up, relay_down, core_last):
        c.wait_send()
    for way in range(2):
        for part in range(2):
            x_copy(way, part).wait_send()
    for slot in range(2, 6):
        z_copy(slot).wait_send()


def finish(
    cls_hbm, group_hbm, gain_hbm, ev_hbm, cls_out, con_out, ev_out, cls_ref, group_ref, gain_ref, ev_ref, in_s
):
    loads = [
        pltpu.make_async_copy(src, dst, in_s.at[k])
        for k, (src, dst) in enumerate(
            ((cls_hbm, cls_ref), (group_hbm, group_ref), (gain_hbm, gain_ref), (ev_hbm, ev_ref))
        )
    ]
    for load in loads:
        load.start()
    for load in loads:
        load.wait()
    for c in range(2):
        cls_out[:, c, :] = cls_ref[c, :, 0:132]
    column = jnp.transpose(jnp.concatenate([group_ref[...], jnp.zeros((112, 128), F32)], axis=0))
    con_out[...] = jnp.dot(
        column[:NPROJ, :GROUPS], gain_ref[...], precision=HIGHEST, preferred_element_type=F32
    )[:, :132]
    ev_out[...] = ev_ref[:, :NIMG]


def on_device(
    images, projections, contrast_curve, noise_weight, defocus_group, shifts, orient_index, orient_prior
):
    vmem = pl.BlockSpec(memory_space=pltpu.VMEM)
    sem = pltpu.SemaphoreType.DMA
    hbm = pl.BlockSpec(memory_space=pl.ANY)
    held = pl.pallas_call(
        body,
        out_shape=(
            jax.ShapeDtypeStruct((2, NPROJ, 256), F32),
            jax.ShapeDtypeStruct((GROUPS, 128), F32),
            jax.ShapeDtypeStruct((GROUPS, 256), F32),
            jax.ShapeDtypeStruct((1, 128), F32),
        ),
        in_specs=[hbm] * 8,
        out_specs=(vmem,) * 4,
        scratch_shapes=[
            pltpu.VMEM((NIMG, 2, 264), BF16),
            pltpu.VMEM((GROUPS, NPIX), F32),
            pltpu.VMEM((NPIX // 128, 128), F32),
            pltpu.VMEM((1, NIMG), jnp.int32),
            pltpu.SMEM((2, NSHIFT), jnp.int32),
            pltpu.VMEM((NPROJ, 2, NPIX), BF16),
            pltpu.VMEM((2, NPROJ, NPIX), BF16),
            pltpu.VMEM((1, NPROJ), jnp.int32),
            pltpu.VMEM((2, 128), F32),
            pltpu.VMEM((16, SHARD, 128), BF16),
            pltpu.VMEM((16, 2, NPROJ, 256), BF16),
            pltpu.VMEM((2, NPROJ, 128), BF16),
            pltpu.VMEM((16, 8, 256), F32),
            pltpu.VMEM((16, 8, 256), F32),
            pltpu.VMEM((8, 128), F32),
            pltpu.VMEM((8, 128), F32),
            pltpu.VMEM((16, 2, ROWS, 256), BF16),
            pltpu.VMEM((2, ROWS, 128), BF16),
            pltpu.VMEM((ROWS, NPROJ), F32),
            pltpu.VMEM((5, NPROJ, 128), F32),
            pltpu.VMEM((NPROJ, ROWS), BF16),
            pltpu.VMEM((2, 4, 8, 128), F32),
            pltpu.VMEM((4, 8 * PIECE, 128), BF16),
            pltpu.VMEM((4, 8 * PIECE, 128), BF16),
            pltpu.VMEM((64, 128), BF16),
            pltpu.VMEM((64, 128), BF16),
            pltpu.VMEM((2, MSG, 128), BF16),
            pltpu.VMEM((2, MSG, 128), BF16),
            pltpu.VMEM((2, MSG, 128), BF16),
            pltpu.VMEM((2, MSG, 128), BF16),
            pltpu.VMEM((MSG, 128), F32),
            pltpu.VMEM((7, 64, 128), BF16),
            pltpu.VMEM((2, 64, 128), BF16),
            pltpu.VMEM((2, 2, 64, 128), BF16),
            pltpu.VMEM((64, 128), BF16),
            sem((4, 2)),
            sem((4, 2)),
            sem((2, 4, 2)),
            sem((2, 4, 2)),
            sem((2, 4)),
            sem((2, 4)),
            sem((6,)),
            sem((6,)),
            sem((5,)),
            sem((5,)),
            sem((10,)),
            sem((10,)),
            sem((7,)),
            sem((7,)),
            sem((8,)),
        ],
        compiler_params=pltpu.CompilerParams(
            collective_id=0, has_side_effects=True, vmem_limit_bytes=60 * 1024 * 1024
        ),
        name="expectation",
    )(
        images,
        projections,
        contrast_curve,
        noise_weight.reshape(NPIX // 128, 128),
        defocus_group.reshape(1, NIMG),
        shifts.T,
        orient_index.reshape(1, NPROJ),
        orient_prior.reshape(2, 128),
    )
    cls, con, ev = pl.pallas_call(
        finish,
        out_shape=(
            jax.ShapeDtypeStruct((NPROJ, 2, 132), F32),
            jax.ShapeDtypeStruct((NPROJ, 132), F32),
            jax.ShapeDtypeStruct((1, NIMG), F32),
        ),
        in_specs=[hbm] * 4,
        out_specs=(vmem,) * 3,
        scratch_shapes=[
            pltpu.VMEM((2, NPROJ, 256), F32),
            pltpu.VMEM((GROUPS, 128), F32),
            pltpu.VMEM((GROUPS, 256), F32),
            pltpu.VMEM((1, 128), F32),
            sem((4,)),
        ],
        compiler_params=pltpu.CompilerParams(vmem_limit_bytes=60 * 1024 * 1024),
        name="finish",
    )(*held)
    return cls, con, ev.reshape(NIMG)


def solution(mesh):
    in_specs = (P("img", None, "ref"), P("ref", None, None), P(), P(), P("img"), P(), P("ref"), P())
    out_specs = (P("ref", None, "img"), P("ref", "img"), P("img"))
    return jax.shard_map(
        on_device, mesh=mesh, in_specs=in_specs, out_specs=out_specs, check_vma=False
    )
```

```python
import math

import jax
import jax.numpy as jnp
from jax import lax
from jax.experimental import pallas as pl
from jax.experimental.pallas import tpu as pltpu
from jax.sharding import PartitionSpec as P

MESH = pl.DeviceIdType.MESH
F32 = jnp.float32
BF16 = jnp.bfloat16
HIGHEST = lax.Precision.HIGHEST
NT = (((1,), (1,)), ((), ()))
TN = (((0,), (0,)), ((), ()))

NPIX = 4224
BOX = 128
NSHIFT = 9
NIMG = 64
NPROJ = 48
GROUPS = 16
ROWS = NSHIFT * NIMG
SHARD = 272
PIECE = 48
MSG = 400
HALF = 208
FIRST = 112


def sincos(steps):
    quadrant = lax.shift_right_arithmetic(steps + 16, 5)
    rest = (steps - quadrant * 32).astype(F32) * (2.0 * math.pi / BOX)
    sq = rest * rest
    sin_part = rest * (
        1.0 + sq * (-1.0 / 6 + sq * (1.0 / 120 + sq * (-1.0 / 5040 + sq * (1.0 / 362880))))
    )
    cos_part = 1.0 + sq * (
        -0.5 + sq * (1.0 / 24 + sq * (-1.0 / 720 + sq * (1.0 / 40320 - sq * (1.0 / 3628800))))
    )
    odd = (quadrant & 1) == 1
    flip_sin = (quadrant & 2) == 2
    flip_cos = ((quadrant + 1) & 2) == 2
    sine = jnp.where(odd, cos_part, sin_part)
    cosine = jnp.where(odd, sin_part, cos_part)
    return jnp.where(flip_cos, -cosine, cosine), jnp.where(flip_sin, -sine, sine)


def body(
    img_hbm,
    proj_hbm,
    curve_hbm,
    noise_hbm,
    group_hbm,
    shift_hbm,
    orient_hbm,
    prior_hbm,
    cls_ref,
    group_out,
    gain_out,
    ev_ref,
    img_ref,
    curve_ref,
    noise_ref,
    group_ref,
    shift_ref,
    proj_ref,
    planes,
    orient_ref,
    prior_ref,
    xbuf,
    pmain,
    prest,
    ctab,
    stab,
    crest,
    srest,
    smain,
    shrest,
    score,
    tile_sum,
    wts,
    stat,
    core_out,
    core_in,
    rest_out,
    rest_in,
    far_out,
    x_out,
    x_near,
    x_in,
    held,
    z_out,
    z_relay,
    z_in,
    z_core,
    ag_z_s,
    ag_z_r,
    ag_y_s,
    ag_y_r,
    ag_f_s,
    ag_f_r,
    st_s,
    st_r,
    co_s,
    co_r,
    xs_s,
    xs_r,
    zs_s,
    zs_r,
    in_s,
):
    img = lax.axis_index("img")
    ref = lax.axis_index("ref")
    x = lax.div(img, 8)
    h = lax.rem(lax.div(img, 2), 4)
    d = lax.rem(img, 2)
    o = 1 - d
    y = lax.div(ref, 4)
    l = lax.rem(ref, 4)

    def ring(v):
        return lax.rem(v + 4, 4)

    def dev(img_at=img, ref_at=ref):
        return {"img": img_at, "ref": ref_at}

    def at_img(xx, hh, dd):
        return dev(img_at=(xx * 4 + hh) * 2 + dd)

    def copy(src, dst, send, recv, to):
        return pltpu.make_async_remote_copy(
            src_ref=src, dst_ref=dst, send_sem=send, recv_sem=recv, device_id=to, device_id_type=MESH
        )

    barrier = pltpu.get_barrier_semaphore()
    peers = [dev(ref_at=y * 4 + lax.rem(l + k, 4)) for k in range(1, 4)]
    peers += [dev(ref_at=lax.rem(ref + 4 * k, 16)) for k in range(1, 4)]
    peers += [at_img(x, h, o), at_img(ring(x + 1), h, d), at_img(ring(x - 1), h, d)]
    peers += [at_img(ring(x + 1), h, o), at_img(ring(x - 1), h, o)]
    for hh in (ring(h + 1), ring(h - 1)):
        peers += [at_img(x, hh, d), at_img(x, hh, o)]
    for peer in peers:
        pl.semaphore_signal(barrier, inc=1, device_id=peer, device_id_type=MESH)

    loads = [
        pltpu.make_async_copy(src, dst, in_s.at[k])
        for k, (src, dst) in enumerate(
            (
                (group_hbm, group_ref),
                (curve_hbm, curve_ref),
                (noise_hbm, noise_ref),
                (img_hbm, img_ref),
                (shift_hbm, shift_ref),
                (proj_hbm, proj_ref),
                (orient_hbm, orient_ref),
                (prior_hbm, prior_ref),
            )
        )
    ]
    for load in loads:
        load.start()
    for load in loads[:4]:
        load.wait()

    lane = lax.broadcasted_iota(jnp.int32, (1, 128), 1)

    def noise_row(tile, count):
        return jnp.concatenate([noise_ref[pl.ds(tile + t, 1), :] for t in range(count)], axis=1)


    group_row = group_ref[...].astype(F32)
    group_row = jnp.concatenate([group_row, group_row], axis=1)
    group_col = jnp.transpose(jnp.broadcast_to(group_row, (128, 128)))[:NIMG, :]
    start = pl.multiple_of(ref * 256, 128)
    turn = lax.rem(384 - 8 * ref, 384)
    curve_here = pltpu.roll(curve_ref[:, pl.ds(start, 384)], turn, 1)
    noise_here = pltpu.roll(jnp.broadcast_to(noise_row(2 * ref, 3), (8, 384)), turn, 1)[:1, :]
    parts = []
    for tile in range(3):
        span = slice(tile * 128, tile * 128 + 128)
        gain = jnp.zeros((NIMG, 128), F32)
        for g in range(GROUPS):
            gain = jnp.where(group_col == float(g), curve_here[g : g + 1, span], gain)
        gain = gain * noise_here[:, span]
        both = []
        for c in range(2):
            if tile < 2:
                pixels = img_ref[:, c, span].astype(F32)
            else:
                pixels = img_ref[:, c, 256:264].astype(F32)
                pixels = jnp.concatenate([pixels, jnp.zeros((NIMG, 120), F32)], axis=1)
            both.append(pixels * gain)
        parts.append(jnp.concatenate(both, axis=0))
    second = pltpu.roll(jnp.concatenate(parts[1:], axis=1), 252, 1)[:, :128]
    rest = jnp.transpose(jnp.where(lane < 4, parts[1], parts[2]))[:16, :]
    row16 = lax.broadcasted_iota(jnp.int32, (16, 128), 0)
    rest = jnp.where(row16 < 8, rest, 0.0)
    xbuf[ref, 0:128, :] = parts[0].astype(BF16)
    xbuf[ref, 128:256, :] = second.astype(BF16)
    xbuf[ref, 256:272, :] = rest.astype(BF16)

    pl.semaphore_wait(barrier, len(peers))

    columns = [lax.rem(l + 4 - e, 4) for e in range(4)]
    halves = (pl.ds(0, 144), pl.ds(144, 128))

    def shard(yy, e):
        return yy * 4 + columns[e]

    def z_send(e, part):
        block = xbuf.at[ref, halves[part]]
        to = dev(ref_at=y * 4 + lax.rem(l + e, 4))
        return copy(block, block, ag_z_s.at[e, part], ag_z_r.at[e, part], to)

    y_up, y_down, y_far = ring(y + 1), ring(y - 1), ring(y + 2)

    def y_copy(way, e, src_y, part):
        to = dev(ref_at=(y_up if way == 0 else y_down) * 4 + l)
        block = xbuf.at[shard(src_y, e), halves[part]]
        return copy(block, block, ag_y_s.at[way, e, part], ag_y_r.at[way, e, part], to)

    def f_copy(way, e, src_y):
        to = dev(ref_at=(y_up if way == 0 else y_down) * 4 + l)
        block = xbuf.at[shard(src_y, e), halves[way]]
        return copy(block, block, ag_f_s.at[way, e], ag_f_r.at[way, e], to)

    def send_y(e, part):
        for way in (part, 1 - part):
            y_copy(way, e, y, part).start()

    def near_z():
        for part in range(2):
            z_send(1, part).start()
            z_send(3, part).start()

    @pl.when(d == 0)
    def _():
        near_z()

    send_y(0, 0)
    send_y(0, 1)

    def take_z(e, part):
        block = xbuf.at[shard(y, e), halves[part]]
        copy(block, block, ag_z_s.at[e, part], ag_z_r.at[e, part], dev(ref_at=shard(y, e))).wait_recv()
        send_y(e, part)

    def take_y(e):
        y_copy(0, e, y_down, 0).wait_recv()
        f_copy(0, e, y_down).start()
        y_copy(1, e, y_up, 1).wait_recv()
        f_copy(1, e, y_up).start()
        y_copy(0, e, y_down, 1).wait_recv()
        y_copy(1, e, y_up, 0).wait_recv()

    def take_far(e):
        f_copy(0, e, y_far).wait_recv()
        f_copy(1, e, y_far).wait_recv()

    loads[4].wait()

    def table(pixel, width):
        srow = lax.broadcasted_iota(jnp.int32, (8, width), 0) + 1
        move_x = jnp.zeros((8, width), jnp.int32)
        move_y = jnp.zeros((8, width), jnp.int32)
        for s in range(1, NSHIFT):
            move_x = jnp.where(srow == s, shift_ref[0, s], move_x)
            move_y = jnp.where(srow == s, shift_ref[1, s], move_y)
        freq_x = pixel & (BOX // 2 - 1)
        freq_y = lax.shift_right_logical(pixel, 6) - NPIX // BOX
        return sincos((move_x * freq_x + move_y * freq_y) & (BOX - 1))

    def table_step(b, carry):
        at = lax.broadcasted_iota(jnp.int32, (8, 256), 1)
        pixel = 264 * b + at + jnp.where(at >= 128, 4, 0)
        cosine, sine = table(pixel, 256)
        ctab[b] = cosine
        stab[b] = sine
        return carry

    lax.fori_loop(0, 16, table_step, 0)
    at = lax.broadcasted_iota(jnp.int32, (8, 128), 1)
    cosine, sine = table(132 * lax.shift_right_logical(at, 2) + 128 + (at & 3), 128)
    crest[...] = cosine
    srest[...] = sine

    @pl.when(d == 1)
    def _():
        near_z()

    @pl.when(d == 0)
    def _():
        for part in range(2):
            z_send(2, part).start()

    for load in loads[5:]:
        load.wait()

    def plane_step(t, carry):
        span = pl.ds(pl.multiple_of(t * 384, 128), 384)
        for c in range(2):
            planes[c, :, span] = proj_ref[:, c, span]
        return carry

    lax.fori_loop(0, 11, plane_step, 0)

    @pl.when(d == 1)
    def _():
        for part in range(2):
            z_send(2, part).start()

    take_y(0)


    def proj_step(b, carry):
        out = []
        for c in range(2):
            kept = carry[c]
            for u in range(2):
                n = 2 * b + u
                window = planes[c, :, pl.ds(pl.multiple_of(n * 128, 128), 256)].astype(F32)
                turned = pltpu.roll(window, lax.rem(256 - 4 * n, 256), 1)
                pmain[b, c, :, u * 128 : u * 128 + 128] = turned[:, :128].astype(BF16)
                kept = jnp.where(lax.shift_right_logical(lane, 2) == n, window[:, 128:], kept)
            out.append(kept)
        return tuple(out)

    zero_rest = jnp.zeros((NPROJ, 128), F32)
    rests = lax.fori_loop(0, 8, proj_step, (zero_rest, zero_rest))
    for part in range(2):
        take_z(1, part)
        take_z(3, part)
    rests = lax.fori_loop(8, 16, proj_step, rests)
    for c in range(2):
        prest[c] = rests[c].astype(BF16)


    score[...] = jnp.zeros_like(score)

    def process(b, last=False):
        for t in range(2):
            span = slice(t * 128, t * 128 + 128)
            re = xbuf[b, t * 128 : t * 128 + 64, :]
            im = xbuf[b, t * 128 + 64 : t * 128 + 128, :]
            smain[b, 0, 0:NIMG, span] = re
            smain[b, 1, 0:NIMG, span] = im
            re = re.astype(F32)
            im = im.astype(F32)
            for s in range(1, NSHIFT):
                rows = slice(s * NIMG, s * NIMG + NIMG)
                cosine = ctab[b, s - 1 : s, span]
                sine = stab[b, s - 1 : s, span]
                smain[b, 0, rows, span] = (re * cosine + im * sine).astype(BF16)
                smain[b, 1, rows, span] = (im * cosine - re * sine).astype(BF16)
        if last:
            return lax.dot_general(
                pmain[b, 0], smain[b, 0], NT, preferred_element_type=F32
            ) + lax.dot_general(pmain[b, 1], smain[b, 1], NT, preferred_element_type=F32)
        score[...] += lax.dot_general(
            smain[b, 0], pmain[b, 0], NT, preferred_element_type=F32
        ) + lax.dot_general(smain[b, 1], pmain[b, 1], NT, preferred_element_type=F32)

    def process_all(blocks):
        def step(t, carry):
            b = blocks[0]
            for k in range(1, len(blocks)):
                b = jnp.where(t == k, blocks[k], b)
            process(b)
            return carry

        lax.fori_loop(0, len(blocks), step, 0)

    take_z(2, 0)
    take_z(2, 1)
    process_all([shard(y, 0), shard(y, 1)])
    take_y(1)
    process_all([shard(y_down, 0), shard(y_up, 0)])
    take_far(0)
    take_y(3)
    process_all([shard(y_far, 0), shard(y, 3), shard(y_down, 1)])
    take_y(2)
    process_all([shard(y_up, 1), shard(y, 2), shard(y_down, 3), shard(y_up, 3)])
    take_far(1)
    process_all([shard(y_far, 1), shard(y_down, 2), shard(y_up, 2)])
    def norm_step(t, total):
        span = pl.ds(pl.multiple_of(t * 384, 128), 384)
        re = planes[0, :, span].astype(F32)
        im = planes[1, :, span].astype(F32)
        curve = curve_ref[:, span]
        gain = 0.5 * (curve * curve * noise_row(3 * t, 3))
        power = re * re + im * im
        return total + lax.dot_general(
            two_parts(power), two_parts(gain), NT, preferred_element_type=F32
        )

    def two_parts(value):
        high = value.astype(BF16)
        return jnp.concatenate([high, (value - high.astype(F32)).astype(BF16)], axis=0)

    norm = lax.fori_loop(0, 11, norm_step, jnp.zeros((2 * NPROJ, 2 * GROUPS), F32))
    norm = norm[:NPROJ] + norm[NPROJ:]
    norm = norm[:, :GROUPS] + norm[:, GROUPS:]
    grow = lax.broadcasted_iota(jnp.int32, (GROUPS, 128), 0)
    members = (group_row == grow.astype(F32)).astype(F32)
    penalty = jnp.dot(norm, members, precision=HIGHEST, preferred_element_type=F32)
    orient_row = jnp.concatenate([orient_ref[...].astype(F32), jnp.zeros((1, 80), F32)], axis=1)
    orient_col = jnp.transpose(jnp.broadcast_to(orient_row, (128, 128)))[:NPROJ, :]
    prior = jnp.zeros((NPROJ, 1), F32)
    for half in range(2):
        hit = orient_col == (lane + half * 128).astype(F32)
        prior += jnp.sum(
            jnp.where(hit, prior_ref[half : half + 1, :], 0.0), axis=1, keepdims=True
        )
    base = prior - penalty
    span = pl.ds(pl.multiple_of(img * 128, 128), 256)
    curve = curve_ref[:, span]
    gain_out[...] = pltpu.roll(curve * curve * noise_row(img, 2), lax.rem(256 - 4 * img, 256), 1)

    take_far(3)
    process(shard(y_far, 3))
    full = jnp.concatenate([score[...], jnp.zeros((ROWS, 128 - NPROJ), F32)], axis=1)
    for t in range(5):
        if t < 4:
            turned = full[t * 128 : t * 128 + 128]
        else:
            turned = jnp.concatenate([full[512:576], jnp.zeros((64, 128), F32)], axis=0)
        tile_sum[t] = jnp.transpose(turned)[:NPROJ] + base
    take_far(2)
    last_part = process(shard(y_far, 2), last=True)

    rest_t = jnp.concatenate([xbuf[b, 256:272, :].astype(F32)[:8] for b in range(16)], axis=0)
    rest_x = jnp.transpose(rest_t)
    re, im = rest_x[:NIMG], rest_x[NIMG:]
    shrest[0, 0:NIMG, :] = re.astype(BF16)
    shrest[1, 0:NIMG, :] = im.astype(BF16)
    for s in range(1, NSHIFT):
        rows = slice(s * NIMG, s * NIMG + NIMG)
        cosine = crest[s - 1 : s, :]
        sine = srest[s - 1 : s, :]
        shrest[0, rows, :] = (re * cosine + im * sine).astype(BF16)
        shrest[1, rows, :] = (im * cosine - re * sine).astype(BF16)
    last_part += lax.dot_general(
        prest[0], shrest[0], NT, preferred_element_type=F32
    ) + lax.dot_general(prest[1], shrest[1], NT, preferred_element_type=F32)
    tiles = []
    for t in range(5):
        if t < 4:
            tiles.append(tile_sum[t] + last_part[:, t * 128 : t * 128 + 128])
        else:
            end = jnp.concatenate([last_part[:, 512:576]] * 2, axis=1)
            tiles.append(jnp.where(lane < 64, tile_sum[t] + end, -3e38))
    high = tiles[0]
    for t in range(1, 5):
        high = jnp.maximum(high, tiles[t])
    high = jnp.max(high, axis=0, keepdims=True)
    high = jnp.maximum(high, pltpu.roll(jnp.broadcast_to(high, (8, 128)), 64, 1)[:1])
    total = jnp.exp(tiles[0] - high)
    for t in range(1, 5):
        total += jnp.exp(tiles[t] - high)
    total = jnp.sum(total, axis=0, keepdims=True)
    total = total + pltpu.roll(jnp.broadcast_to(total, (8, 128)), 64, 1)[:1]
    row8 = lax.broadcasted_iota(jnp.int32, (8, 128), 0)

    def merged(blocks):
        top = blocks[0][0:1, :]
        for block in blocks[1:]:
            top = jnp.maximum(top, block[0:1, :])
        whole = jnp.zeros((1, 128), F32)
        for block in blocks:
            whole += block[1:2, :] * jnp.exp(block[0:1, :] - top)
        return top, whole

    st_copies = []
    for stage in range(2):
        mine_at = l if stage == 0 else y
        stat[stage, mine_at] = jnp.where(row8 == 0, high, total)
        for k in range(1, 4):
            to = y * 4 + lax.rem(l + k, 4) if stage == 0 else lax.rem(ref + 4 * k, 16)
            block = stat.at[stage, mine_at]
            c = copy(block, block, st_s.at[3 * stage + k - 1], st_r.at[3 * stage + k - 1], dev(ref_at=to))
            c.start()
            st_copies.append(c)
        for k in range(1, 4):
            src = lax.rem(mine_at + 4 - k, 4)
            block = stat.at[stage, src]
            come_from = y * 4 + src if stage == 0 else src * 4 + l
            copy(
                block, block, st_s.at[3 * stage + k - 1], st_r.at[3 * stage + k - 1], dev(ref_at=come_from)
            ).wait_recv()
        high, total = merged([stat[stage, b] for b in range(4)])
    evidence = high + jnp.log(total)
    ev_ref[...] = evidence
    for t in range(5):
        w = jnp.exp(tiles[t] - evidence).astype(BF16)
        if t < 4:
            wts[:, t * 128 : t * 128 + 128] = w
        else:
            wts[:, 512:576] = w[:, :64]
    members_all = jnp.concatenate([members.astype(BF16)] * 4 + [members[:, :64].astype(BF16)], axis=1)
    group_sum = lax.dot_general(members_all, wts[...], NT, preferred_element_type=F32)
    group_sum = jnp.concatenate([group_sum, jnp.zeros((GROUPS, 80), F32)], axis=1)

    other = at_img(x, h, o)
    rest_mine = jnp.dot(wts[...], shrest[d], preferred_element_type=F32)
    rest_theirs = jnp.dot(wts[...], shrest[o], preferred_element_type=F32)

    order = [ring(x + 2), ring(x + 1), ring(x + 3), x]
    runs = [ring(h + 2), ring(h + 1), ring(h + 3), h]

    def core_copy(i):
        return copy(core_out.at[i], core_in.at[i], co_s.at[i], co_r.at[i], other)

    def other_chunk(i):
        for u in range(4):
            got = jnp.dot(wts[...], smain[4 * order[i] + runs[u], o], preferred_element_type=F32)
            for v in range(2):
                r = PIECE * (2 * u + v)
                core_out[i, r : r + PIECE, :] = got[:, v * 128 : v * 128 + 128].astype(BF16)
        core_copy(i).start()

    def left(value, by):
        return pltpu.roll(value, lax.rem(256 - by, 128), 1)

    def packed(q, rest_tile, group_tile, c):
        out = left(rest_tile[0:16], 32 * q)
        out = jnp.where(lane < 32, out, left(rest_tile[16:32], 32 * q - 32))
        out = jnp.where(lane < 64, out, left(rest_tile[32:48], 32 * q - 64))
        return jnp.where(lane < 96, out, left(group_tile, 32 + 24 * c))

    def piece_row(k):
        return 16 + PIECE * k

    def rows_of(k):
        return slice(0, 16) if k < 0 else slice(piece_row(k), piece_row(k) + PIECE)

    far_spans = (slice(0, FIRST), slice(FIRST, HALF), slice(HALF, MSG))

    def far_copy(k, part):
        span = far_spans[part]
        rows = pl.ds(span.start, span.stop - span.start)
        c = d if k == 0 else o
        to = at_img(ring(x + 1) if part < 2 else ring(x - 1), h, c)
        at = 2 * part + k
        return copy(far_out.at[k, rows], x_near.at[k, rows], xs_s.at[at], xs_r.at[at], to)

    def far_sums(k, runs_of):
        for u in runs_of:
            got = jnp.dot(
                wts[...], smain[4 * order[0] + runs[u], d if k == 0 else o], preferred_element_type=F32
            ).astype(BF16)
            for v in range(2):
                far_out[k, rows_of(2 * u + v), :] = got[:, v * 128 : v * 128 + 128]

    for k in range(2):
        far_sums(k, (0,))
        rest_tile = rest_mine if k == 0 else rest_theirs
        far_out[k, 0:16, :] = packed(order[0], rest_tile, group_sum, d if k == 0 else o).astype(BF16)
        far_copy(k, 0).start()
    for k in range(2):
        far_sums(k, (1, 2, 3))
        far_copy(k, 2).start()
        far_copy(k, 1).start()

    rest_out[0:48, :] = rest_theirs.astype(BF16)
    rest_out[48:64, :] = group_sum.astype(BF16)
    rest_copy = copy(rest_out, rest_in, co_s.at[4], co_r.at[4], other)
    rest_copy.start()
    for i in range(1, 4):
        other_chunk(i)

    rest_copy.wait_recv()
    rest_sum = rest_mine + rest_in[0:48, :].astype(F32)
    group_sum = group_sum + rest_in[48:64, :].astype(F32)

    def own_chunk(i):
        q = order[i]
        sums = [
            jnp.dot(wts[...], smain[4 * q + runs[u], d], preferred_element_type=F32) for u in range(4)
        ]
        core_copy(i).wait_recv()
        for u in range(4):
            for v in range(2):
                k = 2 * u + v
                r = PIECE * k
                held[rows_of(k), :] = (
                    sums[u][:, v * 128 : v * 128 + 128] + core_in[i, r : r + PIECE, :].astype(F32)
                )
        held[0:16, :] = packed(q, rest_sum, group_sum, d)

    x_up, x_down = at_img(ring(x + 1), h, d), at_img(ring(x - 1), h, d)

    def near_sum(part):
        span = far_spans[part]
        for k in range(2):
            far_copy(k, part).wait_recv()
        both = x_near[0, span, :].astype(F32) + x_near[1, span, :].astype(F32)
        return (held[span, :] + both).astype(BF16)

    def x_copy(way, part):
        rows = pl.ds(0, FIRST) if part == 0 else pl.ds(FIRST, MSG - FIRST)
        k = 6 + 2 * way + part
        to = x_up if way == 0 else x_down
        return copy(x_out.at[way, rows], x_in.at[way, rows], xs_s.at[k], xs_r.at[k], to)

    own_chunk(1)
    x_out[0, 0:FIRST, :] = near_sum(0)
    x_copy(0, 0).start()
    x_out[0, HALF:MSG, :] = held[HALF:MSG, :].astype(BF16)
    x_out[0, FIRST:HALF, :] = near_sum(1)
    x_copy(0, 1).start()

    own_chunk(2)
    x_out[1, 0:HALF, :] = held[0:HALF, :].astype(BF16)
    x_copy(1, 0).start()
    x_out[1, HALF:MSG, :] = near_sum(2)
    x_copy(1, 1).start()

    own_chunk(3)

    def add_x(part):
        rows = slice(0, FIRST) if part == 0 else slice(FIRST, MSG)
        x_copy(0, part).wait_recv()
        x_copy(1, part).wait_recv()
        held[rows, :] += x_in[0, rows, :].astype(F32) + x_in[1, rows, :].astype(F32)

    add_x(0)

    def piece_of(u, dd):
        return held[pl.ds(pl.multiple_of(16 + PIECE * (2 * u + dd), 16), PIECE), :]

    rest_pack = held[0:16, :]
    h_up, h_down = ring(h + 1), ring(h - 1)

    def fill(slot, value, extra):
        z_out[slot, 0:48, :] = value.astype(BF16)
        z_out[slot, 48:64, :] = extra.astype(BF16)

    fill(0, piece_of(0, 0), rest_pack)
    fill(1, piece_of(0, 1), rest_pack)
    relay_up = copy(z_out.at[0], z_relay.at[0], zs_s.at[0], zs_r.at[0], at_img(x, h_up, d))
    relay_down = copy(z_out.at[1], z_relay.at[1], zs_s.at[1], zs_r.at[1], at_img(x, h_down, d))
    relay_up.start()
    relay_down.start()
    add_x(1)

    def z_copy(slot):
        way, dd = (slot - 2) // 2, (slot - 2) % 2
        to = at_img(x, h_up if way == 0 else h_down, dd)
        return copy(z_out.at[slot], z_in.at[way, d], zs_s.at[slot], zs_r.at[2 + 2 * way + d], to)

    fill(3, piece_of(1, 1), rest_pack)
    z_copy(3).start()
    fill(4, piece_of(2, 0), rest_pack)
    z_copy(4).start()
    fill(6, piece_of(3, o), rest_pack)
    core_last = copy(z_out.at[6], z_core, zs_s.at[6], zs_r.at[6], other)
    core_last.start()
    relay_up.wait_recv()
    fill(
        2,
        piece_of(1, 0) + z_relay[0, 0:48, :].astype(F32),
        rest_pack + z_relay[0, 48:64, :].astype(F32),
    )
    z_copy(2).start()
    relay_down.wait_recv()
    fill(
        5,
        piece_of(2, 1) + z_relay[1, 0:48, :].astype(F32),
        rest_pack + z_relay[1, 48:64, :].astype(F32),
    )
    z_copy(5).start()

    mine = jnp.concatenate([piece_of(3, d), rest_pack], axis=0)
    core_last.wait_recv()
    theirs = z_core[...].astype(F32)
    for way in range(2):
        for c in range(2):
            slot = z_in.at[way, c]
            copy(slot, slot, zs_s.at[2], zs_r.at[2 + 2 * way + c], other).wait_recv()
    local = 2 * h + d
    packs = []
    for c in range(2):
        both = jnp.where(d == c, mine, theirs)
        both = both + z_in[0, c].astype(F32) + z_in[1, c].astype(F32)
        cls_ref[c, :, 0:128] = both[0:48]
        pack = both[48:64]
        packs.append(pack)
        for a in range(3):
            cls_ref[c, 16 * a : 16 * a + 16, 128:256] = left(pack, 32 * a + 4 * local)
    group_all = jnp.where(lane < 24, left(packs[0], 96), left(packs[1], 72))
    group_out[...] = jnp.where(lane < 48, group_all, 0.0)

    for e in range(4):
        for part in range(2):
            if e:
                z_send(e, part).wait_send()
            for way in range(2):
                y_copy(way, e, y, part).wait_send()
        for way in range(2):
            f_copy(way, e, y).wait_send()
    for c in st_copies:
        c.wait_send()
    for i in range(1, 4):
        core_copy(i).wait_send()
    for k in range(2):
        for part in range(3):
            far_copy(k, part).wait_send()
    for c in (rest_copy, relay_up, relay_down, core_last):
        c.wait_send()
    for way in range(2):
        for part in range(2):
            x_copy(way, part).wait_send()
    for slot in range(2, 6):
        z_copy(slot).wait_send()


def finish(
    cls_hbm, group_hbm, gain_hbm, ev_hbm, cls_out, con_out, ev_out, cls_ref, group_ref, gain_ref, ev_ref, in_s
):
    loads = [
        pltpu.make_async_copy(src, dst, in_s.at[k])
        for k, (src, dst) in enumerate(
            ((cls_hbm, cls_ref), (group_hbm, group_ref), (gain_hbm, gain_ref), (ev_hbm, ev_ref))
        )
    ]
    for load in loads:
        load.start()
    for load in loads:
        load.wait()
    for c in range(2):
        cls_out[:, c, :] = cls_ref[c, :, 0:132]
    column = jnp.transpose(jnp.concatenate([group_ref[...], jnp.zeros((112, 128), F32)], axis=0))
    con_out[...] = jnp.dot(
        column[:NPROJ, :GROUPS], gain_ref[...], precision=HIGHEST, preferred_element_type=F32
    )[:, :132]
    ev_out[...] = ev_ref[:, :NIMG]


def on_device(
    images, projections, contrast_curve, noise_weight, defocus_group, shifts, orient_index, orient_prior
):
    vmem = pl.BlockSpec(memory_space=pltpu.VMEM)
    sem = pltpu.SemaphoreType.DMA
    hbm = pl.BlockSpec(memory_space=pl.ANY)
    held = pl.pallas_call(
        body,
        out_shape=(
            jax.ShapeDtypeStruct((2, NPROJ, 256), F32),
            jax.ShapeDtypeStruct((GROUPS, 128), F32),
            jax.ShapeDtypeStruct((GROUPS, 256), F32),
            jax.ShapeDtypeStruct((1, 128), F32),
        ),
        in_specs=[hbm] * 8,
        out_specs=(vmem,) * 4,
        scratch_shapes=[
            pltpu.VMEM((NIMG, 2, 264), BF16),
            pltpu.VMEM((GROUPS, NPIX), F32),
            pltpu.VMEM((NPIX // 128, 128), F32),
            pltpu.VMEM((1, NIMG), jnp.int32),
            pltpu.SMEM((2, NSHIFT), jnp.int32),
            pltpu.VMEM((NPROJ, 2, NPIX), BF16),
            pltpu.VMEM((2, NPROJ, NPIX), BF16),
            pltpu.VMEM((1, NPROJ), jnp.int32),
            pltpu.VMEM((2, 128), F32),
            pltpu.VMEM((16, SHARD, 128), BF16),
            pltpu.VMEM((16, 2, NPROJ, 256), BF16),
            pltpu.VMEM((2, NPROJ, 128), BF16),
            pltpu.VMEM((16, 8, 256), F32),
            pltpu.VMEM((16, 8, 256), F32),
            pltpu.VMEM((8, 128), F32),
            pltpu.VMEM((8, 128), F32),
            pltpu.VMEM((16, 2, ROWS, 256), BF16),
            pltpu.VMEM((2, ROWS, 128), BF16),
            pltpu.VMEM((ROWS, NPROJ), F32),
            pltpu.VMEM((5, NPROJ, 128), F32),
            pltpu.VMEM((NPROJ, ROWS), BF16),
            pltpu.VMEM((2, 4, 8, 128), F32),
            pltpu.VMEM((4, 8 * PIECE, 128), BF16),
            pltpu.VMEM((4, 8 * PIECE, 128), BF16),
            pltpu.VMEM((64, 128), BF16),
            pltpu.VMEM((64, 128), BF16),
            pltpu.VMEM((2, MSG, 128), BF16),
            pltpu.VMEM((2, MSG, 128), BF16),
            pltpu.VMEM((2, MSG, 128), BF16),
            pltpu.VMEM((2, MSG, 128), BF16),
            pltpu.VMEM((MSG, 128), F32),
            pltpu.VMEM((7, 64, 128), BF16),
            pltpu.VMEM((2, 64, 128), BF16),
            pltpu.VMEM((2, 2, 64, 128), BF16),
            pltpu.VMEM((64, 128), BF16),
            sem((4, 2)),
            sem((4, 2)),
            sem((2, 4, 2)),
            sem((2, 4, 2)),
            sem((2, 4)),
            sem((2, 4)),
            sem((6,)),
            sem((6,)),
            sem((5,)),
            sem((5,)),
            sem((10,)),
            sem((10,)),
            sem((7,)),
            sem((7,)),
            sem((8,)),
        ],
        compiler_params=pltpu.CompilerParams(
            collective_id=0, has_side_effects=True, vmem_limit_bytes=60 * 1024 * 1024
        ),
        name="expectation",
    )(
        images,
        projections,
        contrast_curve,
        noise_weight.reshape(NPIX // 128, 128),
        defocus_group.reshape(1, NIMG),
        shifts.T,
        orient_index.reshape(1, NPROJ),
        orient_prior.reshape(2, 128),
    )
    cls, con, ev = pl.pallas_call(
        finish,
        out_shape=(
            jax.ShapeDtypeStruct((NPROJ, 2, 132), F32),
            jax.ShapeDtypeStruct((NPROJ, 132), F32),
            jax.ShapeDtypeStruct((1, NIMG), F32),
        ),
        in_specs=[hbm] * 4,
        out_specs=(vmem,) * 3,
        scratch_shapes=[
            pltpu.VMEM((2, NPROJ, 256), F32),
            pltpu.VMEM((GROUPS, 128), F32),
            pltpu.VMEM((GROUPS, 256), F32),
            pltpu.VMEM((1, 128), F32),
            sem((4,)),
        ],
        compiler_params=pltpu.CompilerParams(vmem_limit_bytes=60 * 1024 * 1024),
        name="finish",
    )(*held)
    return cls, con, ev.reshape(NIMG)


def solution(mesh):
    in_specs = (P("img", None, "ref"), P("ref", None, None), P(), P(), P("img"), P(), P("ref"), P())
    out_specs = (P("ref", None, "img"), P("ref", "img"), P("img"))
    return jax.shard_map(
        on_device, mesh=mesh, in_specs=in_specs, out_specs=out_specs, check_vma=False
    )
```
